32 devices in a mesh: facet: 8 (over y, x, core), sub: 4 (over z).
Axes of the slice: x: 2, y: 2, z: 4, core: 2. Of those that a mesh axis runs over, the one named last changes fastest.
Arguments:
- strips: bfloat16 [8, 32, 8192], P('facet', 'sub'), may hold values from -6 to 6
- facet_offset: int32 [8], replicated, may hold values from 0 to 448
- subgrid_offset: int32 [32], replicated, may hold values from 0 to 4095
- owner: int32 [32], replicated, may hold values from 0 to 31, as said below
- screen_index: int32 [32], replicated, may hold values from 0 to 15
- screens: bfloat16 [16, 32, 1024], replicated, may hold values from -1 to 1, as said below
- grid_weight: float32 [128, 512], P(('facet', 'sub')), may hold values from 0.3 to 3
Outputs:
- facet_out: float32 [8, 32, 8192], P('facet', 'sub')
The draws below stay inside these ranges and needn't reach their ends.
Inputs may be any that keep to these rules, and one draw needn't show every extreme that they name: `owner`: device number i * 4 + k is the device at index i of facet and k of sub. No device owns more than 4 subgrids, and some device owns exactly 4. `screens`: element g and element 512 + g of a row are the cosine and sine of one phase.
All inputs are finite; a program needn't handle non-finite values.
Results may differ from the reference program's by a relative error of at most 0.0059.
Values may be sent and summed in bfloat16 or wider, within the bound.
No kernel may reach another device: no remote copies, remote signals or barrier semaphores. Data moves between devices by JAX's collectives and lax.ppermute only.
A program may use at most 64 MiB of HBM per device.

```python
import math
import jax
import jax.numpy as jnp
from jax import lax

FL = 4096
M = 64
SG = 512
WS = 16
CAP = 4
FACETS = 8
COLS = 32
OWNERS = 32
SUBGRIDS = 32


def draw_owner(key, part):
    first_key = jax.random.fold_in(key, 11)
    second_key = jax.random.fold_in(key, 12)
    third_key = jax.random.fold_in(key, 13)
    slot_total = OWNERS * CAP
    slot_ids = jnp.arange(slot_total, dtype=jnp.int32)
    scores = jax.random.permutation(first_key, slot_total).astype(jnp.int32)
    busiest = jax.random.randint(second_key, (), 0, OWNERS, dtype=jnp.int32)
    scores = jnp.where(slot_ids // CAP == busiest, -CAP + slot_ids % CAP, scores)
    chosen = jnp.argsort(scores, stable=True)[:SUBGRIDS].astype(jnp.int32)
    owners_list = chosen // CAP
    return jax.random.permutation(third_key, owners_list).astype(jnp.int32)


def draw_screens(key, part):
    phase_key = jax.random.fold_in(key, 21)
    angles = jax.random.uniform(phase_key, (WS, COLS, SG), jnp.float32, -math.pi, math.pi)
    return jnp.concatenate([jnp.cos(angles), jnp.sin(angles)], axis=-1).astype(jnp.bfloat16)


def plant(drawn, rng, least, top_value):
    longest = drawn.shape.index(max(drawn.shape))
    spots = []
    for shift in (0, 1):
        where = [jax.random.randint(jax.random.fold_in(rng, axis), (), 0, length) for axis, length in enumerate(drawn.shape)]
        where[longest] = (where[longest] + shift) % drawn.shape[longest]
        spots.append(tuple(where))
    return drawn.at[spots[0]].set(least).at[spots[1]].set(top_value)


def steps_of(stream_key, shape, cuts, low, largest):
    def one(dim, shards_of):
        heights = jax.random.uniform(jax.random.fold_in(jax.random.fold_in(stream_key, 6), dim), (shards_of,), jnp.float32, low / len(cuts), largest / len(cuts))
        return jnp.repeat(jnp.exp(heights), shape[dim] // shards_of).reshape((-1,) + (1,) * (len(shape) - dim - 1))

    gain = one(*cuts[0])
    for cut in cuts[1:]:
        gain = gain * one(*cut)
    return gain


def centred(rng, shape, deviation, limit, cuts=(), kind=jnp.bfloat16):
    entries = deviation * jax.random.normal(rng, shape, jnp.float32)
    if cuts:
        entries = entries * steps_of(rng, shape, cuts, -0.22, 0.18)
    return jnp.clip(entries, -limit, limit).astype(kind)


def setup_inputs(seed: int = 0) -> dict:
    splits = jax.random.split(jax.random.key(seed), 8)
    return {
        "strips": centred(splits[0], (FACETS, COLS, 2 * FL), 1.0, 6.0, ((0, 8), (1, 4))),
        "facet_offset": plant(jax.random.randint(splits[1], (FACETS,), 0, SG - M + 1), jax.random.fold_in(splits[1], 1), 0, SG - M).astype(jnp.int32),
        "subgrid_offset": plant(jax.random.randint(splits[2], (SUBGRIDS,), 0, FL), jax.random.fold_in(splits[2], 1), 0, FL - 1).astype(jnp.int32),
        "owner": draw_owner(jax.random.fold_in(splits[7], 71), 0),
        "screen_index": plant(jax.random.randint(splits[4], (SUBGRIDS,), 0, WS), jax.random.fold_in(splits[4], 1), 0, WS - 1).astype(jnp.int32),
        "screens": draw_screens(jax.random.fold_in(splits[7], 71), 0),
        "grid_weight": jnp.clip(jnp.exp(math.log(3.0) - 2.3025851 * jax.random.uniform(splits[6], (OWNERS * CAP, SG), jnp.float32) ** steps_of(splits[6], (OWNERS * CAP, SG), ((0, 32),), -0.2, 0.2)), 0.3, 3.0),
    }


def table_block(start, length, count):
    points = jnp.arange(length, dtype=jnp.int32)
    orders = start + jnp.arange(count, dtype=jnp.int32)
    turn_counts = points[:, None] * orders[None, :] % length
    angles = turn_counts.astype(jnp.float32) * (2.0 * math.pi / length)
    factor = 1.0 / math.sqrt(length)
    cosine = jnp.cos(angles) * factor
    sine_part = jnp.sin(angles) * factor
    upper = jnp.concatenate([cosine, -sine_part], axis=1)
    lower = jnp.concatenate([sine_part, cosine], axis=1)
    return jnp.concatenate([upper, lower], axis=0).astype(jnp.bfloat16)

def full_spectrum(rows):
    width = min(FL, 512)
    blocks = FL // width
    row_count = rows.shape[0]

    def one_block(index):
        block = table_block(index * width, FL, width)
        product = jnp.dot(rows, block, preferred_element_type=jnp.float32)
        return product.astype(jnp.bfloat16).reshape(row_count, 2, width)
    pieces = lax.map(one_block, jnp.arange(blocks, dtype=jnp.int32))
    return jnp.transpose(pieces, (1, 2, 0, 3)).reshape(row_count, 2 * FL)

def synthesize(spectrum):
    width = min(FL, 512)
    blocks = FL // width
    row_count = spectrum.shape[0]
    shaped = spectrum.reshape(row_count, 2, blocks, width)

    def add_block(index, accumulated):
        block = table_block(index * width, FL, width)
        piece = lax.dynamic_index_in_dim(shaped, index, 2, keepdims=False).reshape(row_count, 2 * width)
        return accumulated + lax.dot_general(piece, block, (((1,), (1,)), ((), ())), preferred_element_type=jnp.float32)
    return lax.fori_loop(jnp.int32(0), jnp.int32(blocks), add_block, jnp.zeros((row_count, 2 * FL), jnp.float32))

def reference(strips, facet_offset, subgrid_offset, owner, screen_index, screens, grid_weight):
    subgrid_ids = jnp.arange(SUBGRIDS, dtype=jnp.int32)
    orders = jnp.arange(M, dtype=jnp.int32)
    spectrum = full_spectrum(strips.reshape(FACETS * COLS, 2 * FL)).reshape(FACETS, COLS, 2 * FL)
    frequencies = (subgrid_offset[None, :, None] + facet_offset[:, None, None] + orders[None, None, :]) % FL

    def facet_forward(facet_number):
        spec_f = spectrum[facet_number]
        chosen = frequencies[facet_number]
        real_part = jnp.transpose(spec_f[:, chosen], (1, 0, 2))
        imag_part = jnp.transpose(spec_f[:, FL + chosen], (1, 0, 2))
        return jnp.concatenate([real_part, imag_part], axis=2)
    contributions = lax.map(facet_forward, jnp.arange(FACETS, dtype=jnp.int32))
    onehot = (owner[:, None] == jnp.arange(OWNERS, dtype=jnp.int32)[None, :]).astype(jnp.int32)
    before = jnp.cumsum(onehot, axis=0) - onehot
    slot = lax.optimization_barrier(jnp.sum(before * onehot, axis=1))
    weight_row = owner * CAP + slot

    def process(subgrid):
        subgrid_sum = jnp.zeros((COLS, 2, SG), jnp.float32)
        starts = []
        for facet_number in range(FACETS):
            start = (jnp.int32(0), jnp.int32(0), facet_offset[facet_number].astype(jnp.int32))
            starts.append(start)
            piece = contributions[facet_number, subgrid].reshape(COLS, 2, M).astype(jnp.float32)
            current = lax.dynamic_slice(subgrid_sum, start, (COLS, 2, M))
            subgrid_sum = lax.dynamic_update_slice(subgrid_sum, current + piece, start)
        screen_f = screens[screen_index[subgrid]].reshape(COLS, 2, SG).astype(jnp.float32)
        weighting = grid_weight[weight_row[subgrid]][None, :]
        real_part = (subgrid_sum[:, 0] * screen_f[:, 0] - subgrid_sum[:, 1] * screen_f[:, 1]) * weighting
        imag_part = (subgrid_sum[:, 0] * screen_f[:, 1] + subgrid_sum[:, 1] * screen_f[:, 0]) * weighting
        processed = jnp.stack([real_part, imag_part], axis=1).astype(jnp.bfloat16)
        extracted = [lax.dynamic_slice(processed, start, (COLS, 2, M)).reshape(COLS, 2 * M) for start in starts]
        return jnp.stack(extracted, axis=0)
    returned = lax.map(process, subgrid_ids)

    def facet_backward(facet_number):
        chosen = frequencies[facet_number]
        rows_f = jnp.transpose(returned[:, facet_number].astype(jnp.float32), (1, 0, 2))
        back = jnp.zeros((COLS, 2, FL), jnp.float32)
        back = back.at[:, 0, chosen].add(rows_f[:, :, :M])
        back = back.at[:, 1, chosen].add(rows_f[:, :, M:])
        return synthesize(back.reshape(COLS, 2 * FL).astype(jnp.bfloat16))
    return lax.map(facet_backward, jnp.arange(FACETS, dtype=jnp.int32))
```

```python
import functools
import math

import jax
import jax.numpy as jnp
import numpy as np
from jax import lax
from jax.experimental import pallas as pl
from jax.experimental.pallas import tpu as pltpu
from jax.sharding import PartitionSpec as P

M = 64
CAP = 4
LANES = 128

BF = jnp.bfloat16
F32 = jnp.float32


def split(table):
    high = table.astype(BF).astype(np.float64)
    return high, table - high


def tables(length):
    chunks = length // LANES
    blocks = length // M
    g = np.arange(LANES)
    v = np.arange(LANES)
    u = np.arange(chunks)
    a = np.arange(blocks)
    outer = 2 * math.pi * ((u[:, None] * u[None, :]) % chunks) / chunks
    co, so = np.cos(outer), np.sin(outer)
    fwd = np.block([[co, so], [-so, co]])
    high, low = split(fwd)
    fwd2 = np.concatenate([high, low], axis=1)
    wide = 2 * math.pi * ((u[:, None] * g[None, :]) % chunks) / chunks
    cw, sw = np.cos(wide), np.sin(wide)
    inv = np.block([[cw, -sw], [sw, cw]])
    high, low = split(inv)
    inv2 = np.concatenate([high, low], axis=0)
    twist = 2 * math.pi * ((g[:, None] * v[None, :]) % length) / length
    turn = np.concatenate([np.cos(twist), np.sin(twist)], axis=0)
    coarse = 2 * math.pi * ((a[:, None] * v[None, :]) % blocks) / blocks
    ca, sa = np.cos(coarse) / math.sqrt(length), np.sin(coarse) / math.sqrt(length)
    chigh, clow = split(ca)
    shigh, slow = split(sa)
    pick = np.concatenate(
        [
            np.concatenate([chigh, shigh], axis=1),
            np.concatenate([-shigh, chigh], axis=1),
            np.concatenate([clow, slow], axis=1),
            np.concatenate([-slow, clow], axis=1),
        ],
        axis=0,
    )
    half = [t[:, :M].T for t in (chigh, shigh, clow, slow)]
    back = np.concatenate(
        [
            np.concatenate([half[0], -half[1], half[2], -half[3]], axis=1),
            np.concatenate([half[1], half[0], half[3], half[2]], axis=1),
        ],
        axis=0,
    )
    as_bf = lambda t: np.asarray(t, dtype=BF)
    return as_bf(fwd2), as_bf(inv2), np.asarray(turn, np.float32), as_bf(pick), as_bf(back)


def dot(x, y):
    return jnp.dot(x, y, preferred_element_type=F32)


def dot_t(x, y):
    return lax.dot_general(x, y, (((1,), (1,)), ((), ())), preferred_element_type=F32)


def start_of(where_ref, sub_ref, off_ref, j, length):
    return (sub_ref[j] + off_ref[where_ref[0]]) & (length - 1)


def choose(where_ref, sub_ref, off_ref, length):
    count = sub_ref.shape[0]
    blocks = length // M
    groups = []
    row = lax.broadcasted_iota(jnp.int32, (8, 4 * blocks), 0)
    for group in range(count // 8):
        value = jnp.zeros((8, 4 * blocks), jnp.int32)
        for r in range(8):
            block = start_of(where_ref, sub_ref, off_ref, group * 8 + r, length) // M
            value = jnp.where(row == r, block, value)
        groups.append(value)
    value = jnp.concatenate(groups, axis=0)
    lane = lax.broadcasted_iota(jnp.int32, value.shape, 1)
    return jnp.concatenate(
        [jnp.where(lane == value + q * blocks, 1.0, 0.0) for q in range(4)], axis=0
    ).astype(BF)


def forward_kernel(
    where_ref, sub_ref, off_ref, strips_ref, fwd_ref, turn_ref, pick_ref, out_ref, in_scr, out_scr
):
    rows = strips_ref.shape[1]
    length = strips_ref.shape[2] // 2
    chunks = length // LANES
    count = sub_ref.shape[0]
    for c in range(2 * chunks):
        piece = strips_ref[0, :, c * LANES : (c + 1) * LANES].astype(F32)
        in_scr[pl.ds(c, rows, stride=2 * chunks), :] = piece
    points = jnp.concatenate(
        [in_scr[r * 2 * chunks : (r + 1) * 2 * chunks, :].astype(BF) for r in range(rows)], axis=1
    )
    inner = dot(fwd_ref[...], jnp.concatenate([points, points], axis=0))
    twisted = []
    for r in range(rows):
        re = inner[:chunks, r * LANES : (r + 1) * LANES]
        im = inner[chunks:, r * LANES : (r + 1) * LANES]
        for q in range(LANES // chunks):
            cos = turn_ref[q * chunks : (q + 1) * chunks, :]
            sin = turn_ref[LANES + q * chunks : LANES + (q + 1) * chunks, :]
            both = jnp.concatenate([re * cos + im * sin, im * cos - re * sin], axis=1)
            twisted.append(both.astype(BF))
    twisted = jnp.concatenate(twisted, axis=0)
    chosen = choose(where_ref, sub_ref, off_ref, length)
    coarse = dot(chosen, pick_ref[...]).astype(BF)
    window = dot_t(coarse, twisted)
    window = window[: 2 * count] + window[2 * count :]
    for r in range(rows):
        out_scr[pl.ds(r, 2 * count, stride=rows), :] = window[:, r * LANES : (r + 1) * LANES]
    lane = lax.broadcasted_iota(jnp.int32, (rows, LANES), 1)

    def emit(j):
        shift = start_of(where_ref, sub_ref, off_ref, j, length) % M
        re = out_scr[j * rows : (j + 1) * rows, :]
        im = out_scr[(count + j) * rows : (count + j + 1) * rows, :]
        re = pltpu.roll(re, (LANES - shift) % LANES, 1)
        im = pltpu.roll(im, M - shift, 1)
        return jnp.where(lane < M, re, im)

    for j in range(0, count, 2):
        out_ref[j * rows : (j + 2) * rows, :] = jnp.concatenate([emit(j), emit(j + 1)], axis=0).astype(BF)


def backward_kernel(
    facets,
    subs,
    where_ref,
    sub_ref,
    off_ref,
    owner_ref,
    index_ref,
    *refs,
):
    arrived = refs[:facets]
    screens_ref, inv_ref, turn_ref, back_ref, out_ref = refs[facets : facets + 5]
    place_scr, cos_scr, sin_scr, weight_scr, re_scr, im_scr, out_scr, seen = refs[facets + 5 :]
    rows = out_ref.shape[1]
    length = out_ref.shape[2] // 2
    chunks = length // LANES
    count = sub_ref.shape[0]
    span = screens_ref.shape[2] // 2
    held = subs * CAP
    windows = count * rows
    mine = where_ref[0]
    my_sub = where_ref[1]
    my_off = off_ref[mine]

    shape = (LANES, 2 * LANES)
    row = lax.broadcasted_iota(jnp.int32, shape, 0)
    lane = lax.broadcasted_iota(jnp.int32, shape, 1)
    lane_part = jnp.where((lane // M == 1) | (lane // M == 2), 1, 0)
    apart = (lane_part - row // M) * 8192 + (lane % M - row % M)
    for s in range(facets):
        delta = off_ref[mine ^ s] - my_off
        place_scr[s * LANES : (s + 1) * LANES, :] = jnp.where(apart == delta, 1.0, 0.0).astype(BF)
    total = dot(arrived[0][:windows, :], place_scr[:LANES, :])
    for s in range(1, facets):
        total = total + dot(arrived[s][:windows, :], place_scr[s * LANES : (s + 1) * LANES, :])

    shape = (span, LANES)
    row = lax.broadcasted_iota(jnp.int32, shape, 0)
    lane = lax.broadcasted_iota(jnp.int32, shape, 1)
    hit = row == my_off + lane % M
    both = jnp.where(hit, 1.0, 0.0).astype(BF)
    signed = jnp.where(hit, jnp.where(lane < M, -1.0, 1.0), 0.0).astype(BF)
    kinds = screens_ref.shape[0]
    cosines = screens_ref[:, :, :span].reshape(kinds * rows, span)
    sines = screens_ref[:, :, span:].reshape(kinds * rows, span)
    cos_scr[...] = dot(cosines, both)
    sin_scr[...] = dot(sines, signed)
    pieces = []
    for s in range(facets):
        block = arrived[s][windows:, :].astype(F32)
        pieces.append(
            jnp.concatenate([block[c * held : (c + 1) * held] for c in range(span // LANES)], axis=1)
        )
    weight_scr[...] = dot(jnp.concatenate(pieces, axis=0).astype(BF), both)

    for o in range(facets * subs):
        seen[o] = 0
    lane = lax.broadcasted_iota(jnp.int32, (rows, LANES), 1)
    for j in range(count):
        who = owner_ref[j]
        slot = seen[who]
        seen[who] = slot + 1
        at = ((who // subs) ^ mine) * held + ((who % subs) ^ my_sub) * CAP + slot
        weight = weight_scr[pl.ds(at, 1), :]
        kind = pl.multiple_of(index_ref[j] * rows, rows)
        cos = cos_scr[pl.ds(kind, rows), :] * weight
        sin = sin_scr[pl.ds(kind, rows), :] * weight
        here = total[j * rows : (j + 1) * rows, :LANES]
        swapped = total[j * rows : (j + 1) * rows, LANES:]
        value = (here * cos + swapped * sin).astype(BF).astype(F32)
        shift = start_of(where_ref, sub_ref, off_ref, j, length) % M
        mask = (lane >= shift) & (lane < shift + M)
        re_scr[pl.ds(j, rows, stride=count), :] = jnp.where(mask, pltpu.roll(value, shift, 1), 0.0)
        im_scr[pl.ds(j, rows, stride=count), :] = jnp.where(mask, pltpu.roll(value, shift + M, 1), 0.0)

    chosen = choose(where_ref, sub_ref, off_ref, length)
    coarse = dot_t(back_ref[...], chosen).astype(BF)
    halves = []
    for scr in (re_scr, im_scr):
        halves.append(
            jnp.concatenate([scr[r * count : (r + 1) * count, :].astype(BF) for r in range(rows)], axis=1)
        )
    spread = jnp.concatenate(halves + halves, axis=0)
    inner = dot(coarse, spread)
    twisted = []
    for r in range(rows):
        re = inner[:M, r * LANES : (r + 1) * LANES]
        im = inner[M:, r * LANES : (r + 1) * LANES]
        for q in range(LANES // M):
            cos = turn_ref[q * M : (q + 1) * M, :]
            sin = turn_ref[LANES + q * M : LANES + (q + 1) * M, :]
            both = jnp.concatenate([re * cos - im * sin, re * sin + im * cos], axis=1)
            twisted.append(both.astype(BF))
    twisted = jnp.concatenate(twisted, axis=0)
    points = dot_t(inv_ref[...], twisted)
    points = points[: 2 * chunks] + points[2 * chunks :]
    for r in range(rows):
        out_scr[pl.ds(r, 2 * chunks, stride=rows), :] = points[:, r * LANES : (r + 1) * LANES]
    for c in range(2 * chunks):
        out_ref[0, :, c * LANES : (c + 1) * LANES] = out_scr[c * rows : (c + 1) * rows, :]


def local(strips, facet_offset, subgrid_offset, owner, screen_index, screens, grid_weight):
    facets = lax.axis_size("facet")
    subs = lax.axis_size("sub")
    rows = strips.shape[1]
    length = strips.shape[2] // 2
    chunks = length // LANES
    count = subgrid_offset.shape[0]
    span = grid_weight.shape[1]
    kinds = screens.shape[0]
    fwd, inv, turn, pick, back = [jnp.asarray(t) for t in tables(length)]
    mine = lax.axis_index("facet")
    my_sub = lax.axis_index("sub")
    where = jnp.stack([mine, my_sub]).astype(jnp.int32)
    smem = pl.BlockSpec(memory_space=pltpu.SMEM)
    vmem = pl.BlockSpec(memory_space=pltpu.VMEM)
    limit = pltpu.CompilerParams(vmem_limit_bytes=32 * 1024 * 1024)

    rows_here = grid_weight.astype(BF)
    gathered = [rows_here]
    for s in range(1, subs):
        gathered.append(lax.ppermute(rows_here, "sub", [(i, i ^ s) for i in range(subs)]))
    held = jnp.concatenate(gathered, axis=0)
    held = jnp.transpose(held.reshape(subs * CAP, span // LANES, LANES), (1, 0, 2)).reshape(-1, LANES)

    windows = pl.pallas_call(
        forward_kernel,
        out_shape=jax.ShapeDtypeStruct((count * rows, LANES), BF),
        in_specs=[smem] * 3 + [vmem] * 4,
        out_specs=vmem,
        scratch_shapes=[
            pltpu.VMEM((rows * 2 * chunks, LANES), F32),
            pltpu.VMEM((2 * count * rows, LANES), F32),
        ],
        compiler_params=limit,
    )(where, subgrid_offset, facet_offset, strips, fwd, turn, pick)
    payload = jnp.concatenate([windows, held], axis=0)

    arrived = [payload] + [None] * (facets - 1)
    for s in range(2, facets, 2):
        arrived[s] = lax.ppermute(payload, "facet", [(i, i ^ s) for i in range(facets)])
    for s in range(0, facets, 2):
        arrived[s + 1] = lax.ppermute(arrived[s], "facet", [(i, i ^ 1) for i in range(facets)])

    screens_here = lax.dynamic_slice_in_dim(screens, my_sub * rows, rows, 1)
    out = pl.pallas_call(
        functools.partial(backward_kernel, facets, subs),
        out_shape=jax.ShapeDtypeStruct((1, rows, 2 * length), F32),
        in_specs=[smem] * 5 + [vmem] * (facets + 4),
        out_specs=vmem,
        scratch_shapes=[
            pltpu.VMEM((facets * LANES, 2 * LANES), BF),
            pltpu.VMEM((kinds * rows, LANES), F32),
            pltpu.VMEM((kinds * rows, LANES), F32),
            pltpu.VMEM((facets * subs * CAP, LANES), F32),
            pltpu.VMEM((rows * count, LANES), F32),
            pltpu.VMEM((rows * count, LANES), F32),
            pltpu.VMEM((2 * chunks * rows, LANES), F32),
            pltpu.SMEM((facets * subs,), jnp.int32),
        ],
        compiler_params=limit,
    )(
        where,
        subgrid_offset,
        facet_offset,
        owner,
        screen_index,
        *arrived,
        screens_here,
        inv,
        turn,
        back,
    )
    return out


def solution(mesh):
    in_specs = (P("facet", "sub", None), P(), P(), P(), P(), P(), P(("facet", "sub"), None))
    out_specs = P("facet", "sub", None)
    return jax.shard_map(local, mesh=mesh, in_specs=in_specs, out_specs=out_specs, check_vma=False)
```

```python
import functools
import math

import jax
import jax.numpy as jnp
from jax import lax
from jax.experimental import pallas as pl
from jax.experimental.pallas import tpu as pltpu
from jax.sharding import PartitionSpec as P

M = 64
CAP = 4
LANES = 128

BF = jnp.bfloat16
F32 = jnp.float32


def dot(x, y):
    return jnp.dot(x, y, preferred_element_type=F32)


def dot_t(x, y):
    return lax.dot_general(x, y, (((1,), (1,)), ((), ())), preferred_element_type=F32)


def iota(shape, dim):
    return lax.broadcasted_iota(jnp.int32, shape, dim)


def sine(r):
    x = r * (2 * math.pi)
    y = x * x
    total = -1 / math.factorial(11)
    for n in (9, 7, 5, 3, 1):
        total = total * y + (-1) ** (n // 2) / math.factorial(n)
    return x * total


def circle(index, period):
    r = (index & (period - 1)).astype(F32) * (1 / period) - 0.5
    near = jnp.maximum(jnp.minimum(-r, 0.5 + r), r - 0.5)
    return sine(jnp.abs(r) - 0.25), sine(near)


def high_low(x, low):
    high = x.astype(BF).astype(F32)
    return jnp.where(low, x - high, high).astype(BF)


def column(values, width):
    groups = []
    row = iota((8, width), 0)
    for group in range(len(values) // 8):
        value = jnp.zeros((8, width), jnp.int32)
        for r in range(8):
            value = jnp.where(row == r, values[group * 8 + r], value)
        groups.append(value)
    return jnp.concatenate(groups, axis=0)


def start_of(mine, sub_ref, off_ref, j, length):
    return (sub_ref[j] + off_ref[mine]) & (length - 1)


def table_kernel(length, turn_ref, fwd_ref):
    cos, sin = circle(iota((LANES, LANES), 0) * iota((LANES, LANES), 1), length)
    turn_ref[:LANES, :] = cos
    turn_ref[LANES:, :] = sin

    chunks = length // LANES
    shape = (2 * chunks, 4 * chunks)
    row, lane = iota(shape, 0), iota(shape, 1)
    cos, sin = circle((row & (chunks - 1)) * (lane & (chunks - 1)), chunks)
    row_im, lane_im = row // chunks, lane // chunks % 2
    table = jnp.where(row_im == lane_im, cos, jnp.where(row_im == 0, sin, -sin))
    fwd_ref[...] = high_low(table, lane >= 2 * chunks)


def join_kernel(*refs):
    out_ref = refs[-1]
    row = 0
    for ref in refs[:-1]:
        out_ref[row : row + ref.shape[0], :] = ref[...]
        row += ref.shape[0]


def pack_kernel(windows_ref, *refs):
    out_ref = refs[-1]
    out_ref[: windows_ref.shape[0], :] = windows_ref[...]
    held = jnp.concatenate([ref[...] for ref in refs[:-1]], axis=0)
    row = windows_ref.shape[0]
    for c in range(0, held.shape[1], LANES):
        out_ref[row : row + held.shape[0], :] = held[:, c : c + LANES].astype(BF)
        row += held.shape[0]


def inner_kernel(strips_ref, turn_ref, fwd_ref, out_ref, in_scr):
    rows = strips_ref.shape[1]
    length = strips_ref.shape[2] // 2
    chunks = length // LANES
    for c in range(2 * chunks):
        piece = strips_ref[0, :, c * LANES : (c + 1) * LANES].astype(F32)
        in_scr[pl.ds(c, rows, stride=2 * chunks), :] = piece
    points = jnp.concatenate(
        [in_scr[r * 2 * chunks : (r + 1) * 2 * chunks, :].astype(BF) for r in range(rows)], axis=1
    )
    inner = dot(fwd_ref[...], jnp.concatenate([points, points], axis=0))
    for r in range(rows):
        re = inner[:chunks, r * LANES : (r + 1) * LANES]
        im = inner[chunks:, r * LANES : (r + 1) * LANES]
        for q in range(LANES // chunks):
            cos = turn_ref[q * chunks : (q + 1) * chunks, :]
            sin = turn_ref[LANES + q * chunks : LANES + (q + 1) * chunks, :]
            at = r * LANES + q * chunks
            out_ref[at : at + chunks, :LANES] = (re * cos + im * sin).astype(BF)
            out_ref[at : at + chunks, LANES:] = (im * cos - re * sin).astype(BF)


def window_kernel(length, sub_ref, off_ref, twisted_ref, out_ref, out_scr):
    mine = lax.axis_index("facet")
    rows = twisted_ref.shape[0] // LANES
    count = out_ref.shape[0] // rows
    starts = [start_of(mine, sub_ref, off_ref, j, length) for j in range(count)]
    block = column([s // M for s in starts], LANES)
    cos, sin = circle(block * iota((count, LANES), 1), length // M)
    scale = 1 / math.sqrt(length)
    cos, sin = cos * scale, sin * scale
    coarse = jnp.concatenate(
        [jnp.concatenate([cos, sin], axis=1), jnp.concatenate([-sin, cos], axis=1)], axis=0
    )
    coarse = jnp.concatenate([high_low(coarse, False), high_low(coarse, True)], axis=0)
    window = dot_t(coarse, twisted_ref[...])
    window = window[: 2 * count] + window[2 * count :]
    for r in range(rows):
        out_scr[pl.ds(r, 2 * count, stride=rows), :] = window[:, r * LANES : (r + 1) * LANES]
    lane = iota((rows, LANES), 1)

    def emit(j):
        shift = starts[j] & (M - 1)
        re = out_scr[j * rows : (j + 1) * rows, :]
        im = out_scr[(count + j) * rows : (count + j + 1) * rows, :]
        re = pltpu.roll(re, (LANES - shift) & (LANES - 1), 1)
        im = pltpu.roll(im, M - shift, 1)
        return jnp.where(lane < M, re, im)

    for j in range(0, count, 2):
        out_ref[j * rows : (j + 2) * rows, :] = jnp.concatenate([emit(j), emit(j + 1)], axis=0).astype(BF)


def prepare_kernel(
    facets,
    subs,
    length,
    sub_ref,
    off_ref,
    owner_ref,
    kind_ref,
    after_ref,
    screens_ref,
    place_ref,
    cos_ref,
    sin_ref,
    both_ref,
    rank_ref,
    coarse_ref,
    inv_ref,
    seen,
    cos_scr,
    sin_scr,
):
    count = sub_ref.shape[0]
    rows = cos_ref.shape[0] // count
    span = screens_ref.shape[2] // 2
    pieces = span // LANES
    chunks = length // LANES
    mine = lax.axis_index("facet")
    my_sub = lax.axis_index("sub")
    my_off = off_ref[mine]

    shape = (LANES, 2 * LANES)
    row = iota(shape, 0)
    lane = iota(shape, 1)
    lane_part = jnp.where((lane // M == 1) | (lane // M == 2), 1, 0)
    apart = (lane_part - row // M) * 8192 + (lane % M - row % M)
    for s in range(facets):
        delta = off_ref[mine ^ s] - my_off
        place_ref[s * LANES : (s + 1) * LANES, :] = jnp.where(apart == delta, 1.0, 0.0).astype(BF)

    shape = (span, LANES)
    row = iota(shape, 0)
    lane = iota(shape, 1)
    hit = row == my_off + lane % M
    both = jnp.where(hit, 1.0, 0.0).astype(BF)
    signed = jnp.where(hit, jnp.where(lane < M, -1.0, 1.0), 0.0).astype(BF)
    kinds = screens_ref.shape[0]
    tall = cos_scr.shape[0] // kinds
    first = my_sub * rows // tall * tall
    block = pl.ds(pl.multiple_of(first, tall), tall)
    cosines = screens_ref[:, block, :span].reshape(kinds * tall, span)
    sines = screens_ref[:, block, span:].reshape(kinds * tall, span)
    cos_scr[...] = dot(cosines, both)
    sin_scr[...] = dot(sines, signed)
    for j in range(count):
        kind = pl.multiple_of(kind_ref[j] * tall + my_sub * rows - first, rows)
        cos_ref[j * rows : (j + 1) * rows, :] = cos_scr[pl.ds(kind, rows), :]
        sin_ref[j * rows : (j + 1) * rows, :] = sin_scr[pl.ds(kind, rows), :]
    both_ref[...] = both

    for o in range(facets * subs):
        seen[o] = 0
    held = subs * CAP
    places = []
    for j in range(count):
        who = owner_ref[j]
        slot = seen[who]
        seen[who] = slot + 1
        facet_step = (who // subs) ^ mine
        sub_step = (who % subs) ^ my_sub
        places.append(facet_step * held * pieces + sub_step * CAP + slot)
    width = rank_ref.shape[1]
    place = column(places, width)
    lane = iota((count, width), 1)
    for c in range(pieces):
        hit = jnp.where(lane == place + c * held, 1.0, 0.0)
        rank_ref[c * count : (c + 1) * count, :] = hit.astype(BF)

    lane = iota((8, 4 * count), 1)
    block = jnp.zeros((8, 4 * count), jnp.int32)
    for j in range(count):
        start = start_of(mine, sub_ref, off_ref, j, length) // M
        block = jnp.where(lane % count == j, start, block)
    block = jnp.concatenate([block] * (M // 8), axis=0)
    shape = (M, 4 * count)
    lane = iota(shape, 1)
    cos, sin = circle(block * iota(shape, 0), length // M)
    scale = 1 / math.sqrt(length)
    cos, sin = cos * scale, sin * scale
    lane_im = lane // count % 2 == 1
    low = lane >= 2 * count
    coarse_ref[:M, :] = high_low(jnp.where(lane_im, -sin, cos), low)
    coarse_ref[M:, :] = high_low(jnp.where(lane_im, cos, sin), low)

    shape = (chunks, LANES)
    cos, sin = circle(iota(shape, 0) * iota(shape, 1), chunks)
    table = jnp.concatenate(
        [jnp.concatenate([cos, -sin], axis=1), jnp.concatenate([sin, cos], axis=1)], axis=0
    )
    inv_ref[: 2 * chunks, :] = high_low(table, False)
    inv_ref[2 * chunks :, :] = high_low(table, True)


def backward_kernel(facets, sub_ref, off_ref, *refs):
    arrived = refs[:facets]
    place_ref, cos_ref, sin_ref, both_ref, rank_ref, coarse_ref = refs[facets : facets + 6]
    inv_ref, turn_ref, out_ref, re_scr, im_scr, out_scr = refs[facets + 6 :]
    mine = lax.axis_index("facet")
    rows = out_ref.shape[1]
    length = out_ref.shape[2] // 2
    chunks = length // LANES
    count = sub_ref.shape[0]
    windows = count * rows

    total = dot(arrived[0][:windows, :], place_ref[:LANES, :])
    for s in range(1, facets):
        total = total + dot(arrived[s][:windows, :], place_ref[s * LANES : (s + 1) * LANES, :])

    held = jnp.concatenate([block[windows:, :] for block in arrived], axis=0)
    ranked = dot(rank_ref[...], held).astype(BF)
    ranked = jnp.concatenate([ranked[c : c + count] for c in range(0, ranked.shape[0], count)], axis=1)
    weights = dot(ranked, both_ref[...])

    lane = iota((rows, LANES), 1)
    for j in range(count):
        weight = weights[j : j + 1, :]
        cos = cos_ref[j * rows : (j + 1) * rows, :] * weight
        sin = sin_ref[j * rows : (j + 1) * rows, :] * weight
        here = total[j * rows : (j + 1) * rows, :LANES]
        swapped = total[j * rows : (j + 1) * rows, LANES:]
        value = (here * cos + swapped * sin).astype(BF).astype(F32)
        shift = start_of(mine, sub_ref, off_ref, j, length) & (M - 1)
        mask = (lane >= shift) & (lane < shift + M)
        re_scr[pl.ds(j, rows, stride=count), :] = jnp.where(mask, pltpu.roll(value, shift, 1), 0.0)
        im_scr[pl.ds(j, rows, stride=count), :] = jnp.where(mask, pltpu.roll(value, shift + M, 1), 0.0)

    halves = []
    for scr in (re_scr, im_scr):
        halves.append(
            jnp.concatenate([scr[r * count : (r + 1) * count, :].astype(BF) for r in range(rows)], axis=1)
        )
    spread = jnp.concatenate(halves + halves, axis=0)
    inner = dot(coarse_ref[...], spread)
    twisted = []
    for r in range(rows):
        re = inner[:M, r * LANES : (r + 1) * LANES]
        im = inner[M:, r * LANES : (r + 1) * LANES]
        for q in range(LANES // M):
            cos = turn_ref[q * M : (q + 1) * M, :]
            sin = turn_ref[LANES + q * M : LANES + (q + 1) * M, :]
            both = jnp.concatenate([re * cos - im * sin, re * sin + im * cos], axis=1)
            twisted.append(both.astype(BF))
    twisted = jnp.concatenate(twisted, axis=0)
    points = dot_t(inv_ref[...], twisted)
    points = points[: 2 * chunks] + points[2 * chunks :]
    for r in range(rows):
        out_scr[pl.ds(r, 2 * chunks, stride=rows), :] = points[:, r * LANES : (r + 1) * LANES]
    for c in range(2 * chunks):
        out_ref[0, :, c * LANES : (c + 1) * LANES] = out_scr[c * rows : (c + 1) * rows, :]


def local(strips, facet_offset, subgrid_offset, owner, screen_index, screens, grid_weight):
    facets = lax.axis_size("facet")
    subs = lax.axis_size("sub")
    rows = strips.shape[1]
    length = strips.shape[2] // 2
    chunks = length // LANES
    count = subgrid_offset.shape[0]
    span = grid_weight.shape[1]
    kinds = screens.shape[0]
    smem = pl.BlockSpec(memory_space=pltpu.SMEM)
    vmem = pl.BlockSpec(memory_space=pltpu.VMEM)
    limit = pltpu.CompilerParams(vmem_limit_bytes=32 * 1024 * 1024)
    shaped = jax.ShapeDtypeStruct

    def swap(x, step):
        return lax.ppermute(x, "facet", [(i, i ^ step) for i in range(facets)])

    def cost(flops):
        return pl.CostEstimate(flops=flops, bytes_accessed=1 << 20, transcendentals=0)

    turn, fwd = pl.pallas_call(
        functools.partial(table_kernel, length),
        out_shape=[shaped((2 * LANES, LANES), F32), shaped((2 * chunks, 4 * chunks), BF)],
        out_specs=[vmem] * 2,
        compiler_params=limit,
        cost_estimate=cost(10**11),
    )()
    held = grid_weight
    step = 1
    others = []
    while step < subs:
        beside = lax.ppermute(held, "sub", [(k, k ^ step) for k in range(subs)])
        if step == 1:
            twisted = pl.pallas_call(
                inner_kernel,
                out_shape=shaped((rows * LANES, 2 * LANES), BF),
                in_specs=[vmem] * 3,
                out_specs=vmem,
                scratch_shapes=[pltpu.VMEM((rows * 2 * chunks, LANES), F32)],
                compiler_params=limit,
            )(strips, turn, fwd)
            windows = pl.pallas_call(
                functools.partial(window_kernel, length),
                out_shape=shaped((count * rows, LANES), BF),
                in_specs=[smem] * 2 + [vmem],
                out_specs=vmem,
                scratch_shapes=[pltpu.VMEM((2 * count * rows, LANES), F32)],
                compiler_params=limit,
            )(subgrid_offset, facet_offset, twisted)
        step *= 2
        if step < subs:
            held = pl.pallas_call(
                join_kernel,
                out_shape=shaped((2 * held.shape[0], span), F32),
                in_specs=[vmem] * 2,
                out_specs=vmem,
                compiler_params=limit,
            )(held, beside)
            held, _ = lax.optimization_barrier((held, windows))
    held = [held, beside]

    tall = max(rows, 16)
    prepared = pl.pallas_call(
        functools.partial(prepare_kernel, facets, subs, length),
        out_shape=[
            shaped((facets * LANES, 2 * LANES), BF),
            shaped((count * rows, LANES), F32),
            shaped((count * rows, LANES), F32),
            shaped((span, LANES), BF),
            shaped((span // LANES * count, facets * subs * grid_weight.size // LANES), BF),
            shaped((2 * M, 4 * count), BF),
            shaped((4 * chunks, 2 * LANES), BF),
        ],
        in_specs=[smem] * 4 + [pl.BlockSpec(memory_space=pl.ANY), vmem],
        out_specs=[vmem] * 7,
        scratch_shapes=[
            pltpu.SMEM((facets * subs,), jnp.int32),
            pltpu.VMEM((kinds * tall, LANES), F32),
            pltpu.VMEM((kinds * tall, LANES), F32),
        ],
        compiler_params=limit,
        cost_estimate=cost(2*10**10),
    )(subgrid_offset, facet_offset, owner, screen_index, held[0], screens)

    windows, _ = lax.optimization_barrier((windows, prepared[3]))
    payload = pl.pallas_call(
        pack_kernel,
        out_shape=shaped((count * rows + subs * grid_weight.size // LANES, LANES), BF),
        in_specs=[vmem] * (1 + len(held)),
        out_specs=vmem,
        compiler_params=limit,
    )(windows, *held)

    arrived = [payload] + [None] * (facets - 1)
    for s in reversed(range(2, facets, 2)):
        arrived[s] = swap(payload, s)

    for s in range(0, facets, 2):
        arrived[s + 1] = swap(arrived[s], 1)

    return pl.pallas_call(
        functools.partial(backward_kernel, facets),
        out_shape=shaped((1, rows, 2 * length), F32),
        in_specs=[smem] * 2 + [vmem] * (facets + 8),
        out_specs=vmem,
        scratch_shapes=[
            pltpu.VMEM((rows * count, LANES), F32),
            pltpu.VMEM((rows * count, LANES), F32),
            pltpu.VMEM((2 * chunks * rows, LANES), F32),
        ],
        compiler_params=limit,
    )(subgrid_offset, facet_offset, *arrived, *prepared, turn)


def solution(mesh):
    in_specs = (P("facet", "sub", None), P(), P(), P(), P(), P(), P(("facet", "sub"), None))
    out_specs = P("facet", "sub", None)
    return jax.shard_map(local, mesh=mesh, in_specs=in_specs, out_specs=out_specs, check_vma=False)
```

```python
import functools
import math

import jax
import jax.numpy as jnp
from jax import lax
from jax.experimental import pallas as pl
from jax.experimental.pallas import tpu as pltpu
from jax.sharding import PartitionSpec as P

M = 64
CAP = 4
LANES = 128

BF = jnp.bfloat16
F32 = jnp.float32


def dot(x, y):
    return jnp.dot(x, y, preferred_element_type=F32)


def dot_t(x, y):
    return lax.dot_general(x, y, (((1,), (1,)), ((), ())), preferred_element_type=F32)


def iota(shape, dim):
    return lax.broadcasted_iota(jnp.int32, shape, dim)


def sine(r):
    x = r * (2 * math.pi)
    y = x * x
    total = -1 / math.factorial(11)
    for n in (9, 7, 5, 3, 1):
        total = total * y + (-1) ** (n // 2) / math.factorial(n)
    return x * total


def circle(index, period):
    r = (index & (period - 1)).astype(F32) * (1 / period) - 0.5
    near = jnp.maximum(jnp.minimum(-r, 0.5 + r), r - 0.5)
    return sine(jnp.abs(r) - 0.25), sine(near)


def high_low(x, low):
    high = x.astype(BF).astype(F32)
    return jnp.where(low, x - high, high).astype(BF)


def column(values, width):
    groups = []
    row = iota((8, width), 0)
    for group in range(len(values) // 8):
        value = jnp.zeros((8, width), jnp.int32)
        for r in range(8):
            value = jnp.where(row == r, values[group * 8 + r], value)
        groups.append(value)
    return jnp.concatenate(groups, axis=0)


def start_of(mine, sub_ref, off_ref, j, length):
    return (sub_ref[j] + off_ref[mine]) & (length - 1)


def table_kernel(length, turn_ref, fwd_ref):
    cos, sin = circle(iota((LANES, LANES), 0) * iota((LANES, LANES), 1), length)
    turn_ref[:LANES, :] = cos
    turn_ref[LANES:, :] = sin

    chunks = length // LANES
    shape = (2 * chunks, 4 * chunks)
    row, lane = iota(shape, 0), iota(shape, 1)
    cos, sin = circle((row & (chunks - 1)) * (lane & (chunks - 1)), chunks)
    row_im, lane_im = row // chunks, lane // chunks % 2
    table = jnp.where(row_im == lane_im, cos, jnp.where(row_im == 0, sin, -sin))
    fwd_ref[...] = high_low(table, lane >= 2 * chunks)


def join_kernel(*refs):
    out_ref = refs[-1]
    row = 0
    for ref in refs[:-1]:
        out_ref[row : row + ref.shape[0], :] = ref[...]
        row += ref.shape[0]


def pack_kernel(windows_ref, *refs):
    out_ref = refs[-1]
    out_ref[: windows_ref.shape[0], :] = windows_ref[...]
    held = jnp.concatenate([ref[...] for ref in refs[:-1]], axis=0)
    row = windows_ref.shape[0]
    for c in range(0, held.shape[1], LANES):
        out_ref[row : row + held.shape[0], :] = held[:, c : c + LANES].astype(BF)
        row += held.shape[0]


def scalars(pairs, sems):
    copies = [pltpu.make_async_copy(a, b, sems.at[n]) for n, (a, b) in enumerate(pairs)]
    for copy in copies:
        copy.start()
    return copies


def forward_kernel(
    sub_hbm, off_hbm, strips_ref, turn_ref, fwd_ref, out_ref, in_scr, mid_scr, out_scr, sub_ref, off_ref, sems
):
    copies = scalars([(sub_hbm, sub_ref), (off_hbm, off_ref)], sems)
    mine = lax.axis_index("facet")
    rows = strips_ref.shape[1]
    length = strips_ref.shape[2] // 2
    chunks = length // LANES
    count = sub_ref.shape[0]

    for c in range(2 * chunks):
        piece = strips_ref[0, :, c * LANES : (c + 1) * LANES].astype(F32)
        in_scr[pl.ds(c, rows, stride=2 * chunks), :] = piece
    points = jnp.concatenate(
        [in_scr[r * 2 * chunks : (r + 1) * 2 * chunks, :].astype(BF) for r in range(rows)], axis=1
    )
    inner = dot(fwd_ref[...], jnp.concatenate([points, points], axis=0))
    for r in range(rows):
        re = inner[:chunks, r * LANES : (r + 1) * LANES]
        im = inner[chunks:, r * LANES : (r + 1) * LANES]
        for q in range(LANES // chunks):
            cos = turn_ref[q * chunks : (q + 1) * chunks, :]
            sin = turn_ref[LANES + q * chunks : LANES + (q + 1) * chunks, :]
            at = r * LANES + q * chunks
            mid_scr[at : at + chunks, :LANES] = (re * cos + im * sin).astype(BF)
            mid_scr[at : at + chunks, LANES:] = (im * cos - re * sin).astype(BF)

    for copy in copies:
        copy.wait()
    starts = [start_of(mine, sub_ref, off_ref, j, length) for j in range(count)]
    block = column([s // M for s in starts], LANES)
    cos, sin = circle(block * iota((count, LANES), 1), length // M)
    scale = 1 / math.sqrt(length)
    cos, sin = cos * scale, sin * scale
    coarse = jnp.concatenate(
        [jnp.concatenate([cos, sin], axis=1), jnp.concatenate([-sin, cos], axis=1)], axis=0
    )
    coarse = jnp.concatenate([high_low(coarse, False), high_low(coarse, True)], axis=0)
    window = dot_t(coarse, mid_scr[...])
    window = window[: 2 * count] + window[2 * count :]
    for r in range(rows):
        out_scr[pl.ds(r, 2 * count, stride=rows), :] = window[:, r * LANES : (r + 1) * LANES]
    lane = iota((rows, LANES), 1)

    def emit(j):
        shift = starts[j] & (M - 1)
        re = out_scr[j * rows : (j + 1) * rows, :]
        im = out_scr[(count + j) * rows : (count + j + 1) * rows, :]
        re = pltpu.roll(re, (LANES - shift) & (LANES - 1), 1)
        im = pltpu.roll(im, M - shift, 1)
        return jnp.where(lane < M, re, im)

    for j in range(0, count, 2):
        out_ref[j * rows : (j + 2) * rows, :] = jnp.concatenate([emit(j), emit(j + 1)], axis=0).astype(BF)


def prepare_kernel(
    facets,
    subs,
    length,
    sub_hbm,
    off_hbm,
    owner_hbm,
    kind_hbm,
    after_ref,
    screens_ref,
    place_ref,
    cos_ref,
    sin_ref,
    both_ref,
    rank_ref,
    coarse_ref,
    inv_ref,
    seen,
    cos_scr,
    sin_scr,
    sub_ref,
    off_ref,
    owner_ref,
    kind_ref,
    sems,
):
    copies = scalars(
        [(sub_hbm, sub_ref), (off_hbm, off_ref), (owner_hbm, owner_ref), (kind_hbm, kind_ref)], sems
    )
    count = sub_ref.shape[0]
    rows = cos_ref.shape[0] // count
    span = screens_ref.shape[2] // 2
    pieces = span // LANES
    chunks = length // LANES
    mine = lax.axis_index("facet")
    my_sub = lax.axis_index("sub")

    shape = (chunks, LANES)
    cos, sin = circle(iota(shape, 0) * iota(shape, 1), chunks)
    table = jnp.concatenate(
        [jnp.concatenate([cos, -sin], axis=1), jnp.concatenate([sin, cos], axis=1)], axis=0
    )
    inv_ref[: 2 * chunks, :] = high_low(table, False)
    inv_ref[2 * chunks :, :] = high_low(table, True)

    for copy in copies:
        copy.wait()
    my_off = off_ref[mine]

    shape = (LANES, 2 * LANES)
    row = iota(shape, 0)
    lane = iota(shape, 1)
    lane_part = jnp.where((lane // M == 1) | (lane // M == 2), 1, 0)
    apart = (lane_part - row // M) * 8192 + (lane % M - row % M)
    for s in range(facets):
        delta = off_ref[mine ^ s] - my_off
        place_ref[s * LANES : (s + 1) * LANES, :] = jnp.where(apart == delta, 1.0, 0.0).astype(BF)

    shape = (span, LANES)
    row = iota(shape, 0)
    lane = iota(shape, 1)
    hit = row == my_off + lane % M
    both = jnp.where(hit, 1.0, 0.0).astype(BF)
    signed = jnp.where(hit, jnp.where(lane < M, -1.0, 1.0), 0.0).astype(BF)
    kinds = screens_ref.shape[0]
    tall = cos_scr.shape[0] // kinds
    first = my_sub * rows // tall * tall
    block = pl.ds(pl.multiple_of(first, tall), tall)
    cosines = screens_ref[:, block, :span].reshape(kinds * tall, span)
    sines = screens_ref[:, block, span:].reshape(kinds * tall, span)
    cos_scr[...] = dot(cosines, both)
    sin_scr[...] = dot(sines, signed)
    for j in range(count):
        kind = pl.multiple_of(kind_ref[j] * tall + my_sub * rows - first, rows)
        cos_ref[j * rows : (j + 1) * rows, :] = cos_scr[pl.ds(kind, rows), :]
        sin_ref[j * rows : (j + 1) * rows, :] = sin_scr[pl.ds(kind, rows), :]
    both_ref[...] = both

    for o in range(facets * subs):
        seen[o] = 0
    held = subs * CAP
    places = []
    for j in range(count):
        who = owner_ref[j]
        slot = seen[who]
        seen[who] = slot + 1
        facet_step = (who // subs) ^ mine
        sub_step = (who % subs) ^ my_sub
        places.append(facet_step * held * pieces + sub_step * CAP + slot)
    width = rank_ref.shape[1]
    place = column(places, width)
    lane = iota((count, width), 1)
    for c in range(pieces):
        hit = jnp.where(lane == place + c * held, 1.0, 0.0)
        rank_ref[c * count : (c + 1) * count, :] = hit.astype(BF)

    lane = iota((8, 4 * count), 1)
    block = jnp.zeros((8, 4 * count), jnp.int32)
    for j in range(count):
        start = start_of(mine, sub_ref, off_ref, j, length) // M
        block = jnp.where(lane % count == j, start, block)
    block = jnp.concatenate([block] * (M // 8), axis=0)
    shape = (M, 4 * count)
    lane = iota(shape, 1)
    cos, sin = circle(block * iota(shape, 0), length // M)
    scale = 1 / math.sqrt(length)
    cos, sin = cos * scale, sin * scale
    lane_im = lane // count % 2 == 1
    low = lane >= 2 * count
    coarse_ref[:M, :] = high_low(jnp.where(lane_im, -sin, cos), low)
    coarse_ref[M:, :] = high_low(jnp.where(lane_im, cos, sin), low)


def backward_kernel(facets, sub_hbm, off_hbm, *refs):
    arrived = refs[:facets]
    place_ref, cos_ref, sin_ref, both_ref, rank_ref, coarse_ref = refs[facets : facets + 6]
    inv_ref, turn_ref, out_hbm, re_scr, im_scr, out_scr, flat_scr, sub_ref, off_ref, sems, out_sems = refs[facets + 6 :]
    copies = scalars([(sub_hbm, sub_ref), (off_hbm, off_ref)], sems)
    mine = lax.axis_index("facet")
    rows = out_hbm.shape[1]
    length = out_hbm.shape[2] // 2
    chunks = length // LANES
    count = sub_ref.shape[0]
    windows = count * rows

    total = dot(arrived[0][:windows, :], place_ref[:LANES, :])
    for s in range(1, facets):
        total = total + dot(arrived[s][:windows, :], place_ref[s * LANES : (s + 1) * LANES, :])

    held = jnp.concatenate([block[windows:, :] for block in arrived], axis=0)
    ranked = dot(rank_ref[...], held).astype(BF)
    ranked = jnp.concatenate([ranked[c : c + count] for c in range(0, ranked.shape[0], count)], axis=1)
    weights = dot(ranked, both_ref[...])

    for copy in copies:
        copy.wait()
    lane = iota((rows, LANES), 1)
    for j in range(count):
        weight = weights[j : j + 1, :]
        cos = cos_ref[j * rows : (j + 1) * rows, :] * weight
        sin = sin_ref[j * rows : (j + 1) * rows, :] * weight
        here = total[j * rows : (j + 1) * rows, :LANES]
        swapped = total[j * rows : (j + 1) * rows, LANES:]
        value = (here * cos + swapped * sin).astype(BF).astype(F32)
        shift = start_of(mine, sub_ref, off_ref, j, length) & (M - 1)
        mask = (lane >= shift) & (lane < shift + M)
        re_scr[pl.ds(j, rows, stride=count), :] = jnp.where(mask, pltpu.roll(value, shift, 1), 0.0)
        im_scr[pl.ds(j, rows, stride=count), :] = jnp.where(mask, pltpu.roll(value, shift + M, 1), 0.0)

    halves = []
    for scr in (re_scr, im_scr):
        halves.append(
            jnp.concatenate([scr[r * count : (r + 1) * count, :].astype(BF) for r in range(rows)], axis=1)
        )
    spread = jnp.concatenate(halves + halves, axis=0)
    inner = dot(coarse_ref[...], spread)
    twisted = []
    for r in range(rows):
        re = inner[:M, r * LANES : (r + 1) * LANES]
        im = inner[M:, r * LANES : (r + 1) * LANES]
        for q in range(LANES // M):
            cos = turn_ref[q * M : (q + 1) * M, :]
            sin = turn_ref[LANES + q * M : LANES + (q + 1) * M, :]
            both = jnp.concatenate([re * cos - im * sin, re * sin + im * cos], axis=1)
            twisted.append(both.astype(BF))
    twisted = jnp.concatenate(twisted, axis=0)
    points = dot_t(inv_ref[...], twisted)
    points = points[: 2 * chunks] + points[2 * chunks :]
    for r in range(rows):
        out_scr[pl.ds(r, 2 * chunks, stride=rows), :] = points[:, r * LANES : (r + 1) * LANES]
    parts = out_sems.shape[0]
    width = 2 * length // parts
    copies = []
    for p in range(parts):
        for c in range(p * width // LANES, (p + 1) * width // LANES):
            flat_scr[:, c * LANES : (c + 1) * LANES] = out_scr[c * rows : (c + 1) * rows, :]
        part = pl.ds(p * width, width)
        copies.append(pltpu.make_async_copy(flat_scr.at[:, part], out_hbm.at[0, :, part], out_sems.at[p]))
        copies[-1].start()
    for copy in copies:
        copy.wait()


def local(strips, facet_offset, subgrid_offset, owner, screen_index, screens, grid_weight):
    facets = lax.axis_size("facet")
    subs = lax.axis_size("sub")
    rows = strips.shape[1]
    length = strips.shape[2] // 2
    chunks = length // LANES
    count = subgrid_offset.shape[0]
    span = grid_weight.shape[1]
    kinds = screens.shape[0]
    hbm = pl.BlockSpec(memory_space=pl.ANY)
    vmem = pl.BlockSpec(memory_space=pltpu.VMEM)
    limit = pltpu.CompilerParams(vmem_limit_bytes=32 * 1024 * 1024)
    shaped = jax.ShapeDtypeStruct

    subgrid_offset, facet_offset, owner, screen_index = [
        pltpu.with_memory_space_constraint(x, pltpu.HBM) for x in (subgrid_offset, facet_offset, owner, screen_index)
    ]

    def swap(x, step):
        return lax.ppermute(x, "facet", [(i, i ^ step) for i in range(facets)])

    def cost(flops):
        return pl.CostEstimate(flops=flops, bytes_accessed=1 << 20, transcendentals=0)

    turn, fwd = pl.pallas_call(
        functools.partial(table_kernel, length),
        out_shape=[shaped((2 * LANES, LANES), F32), shaped((2 * chunks, 4 * chunks), BF)],
        out_specs=[vmem] * 2,
        compiler_params=limit,
        cost_estimate=cost(10**11),
    )()
    held = grid_weight
    step = 1
    others = []
    while step < subs:
        beside = lax.ppermute(held, "sub", [(k, k ^ step) for k in range(subs)])
        if step == 1:
            windows = pl.pallas_call(
                forward_kernel,
                out_shape=shaped((count * rows, LANES), BF),
                in_specs=[hbm] * 2 + [vmem] * 3,
                out_specs=vmem,
                scratch_shapes=[
                    pltpu.VMEM((rows * 2 * chunks, LANES), F32),
                    pltpu.VMEM((rows * LANES, 2 * LANES), BF),
                    pltpu.VMEM((2 * count * rows, LANES), F32),
                    pltpu.SMEM((count,), jnp.int32),
                    pltpu.SMEM((facets,), jnp.int32),
                    pltpu.SemaphoreType.DMA((2,)),
                ],
                compiler_params=limit,
            )(subgrid_offset, facet_offset, strips, turn, fwd)
        step *= 2
        if step < subs:
            held = pl.pallas_call(
                join_kernel,
                out_shape=shaped((2 * held.shape[0], span), F32),
                in_specs=[vmem] * 2,
                out_specs=vmem,
                compiler_params=limit,
            )(held, beside)
            held, _ = lax.optimization_barrier((held, windows))
    held = [held, beside]

    tall = max(rows, 16)
    prepared = pl.pallas_call(
        functools.partial(prepare_kernel, facets, subs, length),
        out_shape=[
            shaped((facets * LANES, 2 * LANES), BF),
            shaped((count * rows, LANES), F32),
            shaped((count * rows, LANES), F32),
            shaped((span, LANES), BF),
            shaped((span // LANES * count, facets * subs * grid_weight.size // LANES), BF),
            shaped((2 * M, 4 * count), BF),
            shaped((4 * chunks, 2 * LANES), BF),
        ],
        in_specs=[hbm] * 5 + [vmem],
        out_specs=[vmem] * 7,
        scratch_shapes=[
            pltpu.SMEM((facets * subs,), jnp.int32),
            pltpu.VMEM((kinds * tall, LANES), F32),
            pltpu.VMEM((kinds * tall, LANES), F32),
            pltpu.SMEM((count,), jnp.int32),
            pltpu.SMEM((facets,), jnp.int32),
            pltpu.SMEM((count,), jnp.int32),
            pltpu.SMEM((count,), jnp.int32),
            pltpu.SemaphoreType.DMA((4,)),
        ],
        compiler_params=limit,
        cost_estimate=cost(2*10**10),
    )(subgrid_offset, facet_offset, owner, screen_index, held[0], screens)

    windows, _ = lax.optimization_barrier((windows, prepared[3]))
    payload = pl.pallas_call(
        pack_kernel,
        out_shape=shaped((count * rows + subs * grid_weight.size // LANES, LANES), BF),
        in_specs=[vmem] * (1 + len(held)),
        out_specs=vmem,
        compiler_params=limit,
    )(windows, *held)

    arrived = [payload] + [None] * (facets - 1)
    for s in reversed(range(2, facets, 2)):
        arrived[s] = swap(payload, s)

    for s in range(0, facets, 2):
        arrived[s + 1] = swap(arrived[s], 1)

    return pl.pallas_call(
        functools.partial(backward_kernel, facets),
        out_shape=shaped((1, rows, 2 * length), F32),
        in_specs=[hbm] * 2 + [vmem] * (facets + 8),
        out_specs=hbm,
        scratch_shapes=[
            pltpu.VMEM((rows * count, LANES), F32),
            pltpu.VMEM((rows * count, LANES), F32),
            pltpu.VMEM((2 * chunks * rows, LANES), F32),
            pltpu.VMEM((rows, 2 * length), F32),
            pltpu.SMEM((count,), jnp.int32),
            pltpu.SMEM((facets,), jnp.int32),
            pltpu.SemaphoreType.DMA((2,)),
            pltpu.SemaphoreType.DMA((4,)),
        ],
        compiler_params=limit,
    )(subgrid_offset, facet_offset, *arrived, *prepared, turn)


def solution(mesh):
    in_specs = (P("facet", "sub", None), P(), P(), P(), P(), P(), P(("facet", "sub"), None))
    out_specs = P("facet", "sub", None)
    return jax.shard_map(local, mesh=mesh, in_specs=in_specs, out_specs=out_specs, check_vma=False)
```

```python
import functools
import math

import jax
import jax.numpy as jnp
from jax import lax
from jax.experimental import pallas as pl
from jax.experimental.pallas import tpu as pltpu
from jax.sharding import PartitionSpec as P

M = 64
CAP = 4
LANES = 128

BF = jnp.bfloat16
F32 = jnp.float32


def dot(x, y):
    return jnp.dot(x, y, preferred_element_type=F32)


def dot_t(x, y):
    return lax.dot_general(x, y, (((1,), (1,)), ((), ())), preferred_element_type=F32)


def iota(shape, dim):
    return lax.broadcasted_iota(jnp.int32, shape, dim)


def sine(r):
    x = r * (2 * math.pi)
    y = x * x
    total = -1 / math.factorial(11)
    for n in (9, 7, 5, 3, 1):
        total = total * y + (-1) ** (n // 2) / math.factorial(n)
    return x * total


def circle(index, period):
    r = (index & (period - 1)).astype(F32) * (1 / period) - 0.5
    near = jnp.maximum(jnp.minimum(-r, 0.5 + r), r - 0.5)
    return sine(jnp.abs(r) - 0.25), sine(near)


def high_low(x, low):
    high = x.astype(BF).astype(F32)
    return jnp.where(low, x - high, high).astype(BF)


def column(values, width):
    groups = []
    row = iota((8, width), 0)
    for group in range(len(values) // 8):
        value = jnp.zeros((8, width), jnp.int32)
        for r in range(8):
            value = jnp.where(row == r, values[group * 8 + r], value)
        groups.append(value)
    return jnp.concatenate(groups, axis=0)


def start_of(mine, sub_ref, off_ref, j, length):
    return (sub_ref[j] + off_ref[mine]) & (length - 1)


def table_kernel(length, turn_ref, fwd_ref):
    cos, sin = circle(iota((LANES, LANES), 0) * iota((LANES, LANES), 1), length)
    turn_ref[:LANES, :] = cos
    turn_ref[LANES:, :] = sin

    chunks = length // LANES
    shape = (2 * chunks, 4 * chunks)
    row, lane = iota(shape, 0), iota(shape, 1)
    cos, sin = circle((row & (chunks - 1)) * (lane & (chunks - 1)), chunks)
    row_im, lane_im = row // chunks, lane // chunks % 2
    table = jnp.where(row_im == lane_im, cos, jnp.where(row_im == 0, sin, -sin))
    fwd_ref[...] = high_low(table, lane >= 2 * chunks)


def join_kernel(first_ref, second_ref, out_ref):
    out_ref[: first_ref.shape[0], :] = first_ref[...]
    out_ref[first_ref.shape[0] :, :] = second_ref[...]


def merge_kernel(windows_ref, passed_ref, shift_ref, own_ref, *out_refs):
    both = jnp.concatenate([windows_ref[...], passed_ref[...]], axis=1)
    merged = dot(both, shift_ref[...])
    own_ref[...] = merged[:, :LANES]
    for n, out_ref in enumerate(out_refs):
        out_ref[...] = merged[:, (n + 1) * LANES : (n + 2) * LANES].astype(BF)


def pack_kernel(others, *refs):
    merged_refs, held_refs, out_refs = refs[:others], refs[others : others + 2], refs[others + 2 :]
    held = jnp.concatenate([ref[...] for ref in held_refs], axis=0)
    laid = jnp.concatenate([held[:, c : c + LANES] for c in range(0, held.shape[1], LANES)], axis=0).astype(BF)
    out_refs[0][...] = laid
    for ref, out_ref in zip(merged_refs, out_refs[1:]):
        out_ref[: ref.shape[0], :] = ref[...]
        out_ref[ref.shape[0] :, :] = laid


def scalars(pairs, sems):
    copies = [pltpu.make_async_copy(a, b, sems.at[n]) for n, (a, b) in enumerate(pairs)]
    for copy in copies:
        copy.start()
    return copies


def forward_kernel(
    sub_hbm,
    off_hbm,
    strips_ref,
    turn_ref,
    fwd_ref,
    out_ref,
    shift_ref,
    in_scr,
    mid_scr,
    out_scr,
    sub_ref,
    off_ref,
    sems,
):
    copies = scalars([(sub_hbm, sub_ref), (off_hbm, off_ref)], sems)
    mine = lax.axis_index("facet")
    rows = strips_ref.shape[1]
    length = strips_ref.shape[2] // 2
    chunks = length // LANES
    count = sub_ref.shape[0]

    for c in range(2 * chunks):
        piece = strips_ref[0, :, c * LANES : (c + 1) * LANES].astype(F32)
        in_scr[pl.ds(c, rows, stride=2 * chunks), :] = piece
    points = jnp.concatenate(
        [in_scr[r * 2 * chunks : (r + 1) * 2 * chunks, :].astype(BF) for r in range(rows)], axis=1
    )
    inner = dot(fwd_ref[...], jnp.concatenate([points, points], axis=0))
    for r in range(rows):
        re = inner[:chunks, r * LANES : (r + 1) * LANES]
        im = inner[chunks:, r * LANES : (r + 1) * LANES]
        for q in range(LANES // chunks):
            cos = turn_ref[q * chunks : (q + 1) * chunks, :]
            sin = turn_ref[LANES + q * chunks : LANES + (q + 1) * chunks, :]
            at = r * LANES + q * chunks
            mid_scr[at : at + chunks, :LANES] = (re * cos + im * sin).astype(BF)
            mid_scr[at : at + chunks, LANES:] = (im * cos - re * sin).astype(BF)

    for copy in copies:
        copy.wait()
    shape = (LANES, LANES)
    row = iota(shape, 0)
    lane = iota(shape, 1)
    apart = (lane // M - row // M) * 8192 + (lane % M - row % M)
    for n in range(shift_ref.shape[1] // LANES):
        for core in range(2):
            delta = off_ref[mine ^ core] - off_ref[mine ^ (2 * n)]
            rows_here = slice(core * LANES, (core + 1) * LANES)
            shift_ref[rows_here, n * LANES : (n + 1) * LANES] = jnp.where(apart == delta, 1.0, 0.0).astype(BF)

    starts = [start_of(mine, sub_ref, off_ref, j, length) for j in range(count)]
    block = column([s // M for s in starts], LANES)
    cos, sin = circle(block * iota((count, LANES), 1), length // M)
    scale = 1 / math.sqrt(length)
    cos, sin = cos * scale, sin * scale
    coarse = jnp.concatenate(
        [jnp.concatenate([cos, sin], axis=1), jnp.concatenate([-sin, cos], axis=1)], axis=0
    )
    coarse = jnp.concatenate([high_low(coarse, False), high_low(coarse, True)], axis=0)
    window = dot_t(coarse, mid_scr[...])
    window = window[: 2 * count] + window[2 * count :]
    for r in range(rows):
        out_scr[pl.ds(r, 2 * count, stride=rows), :] = window[:, r * LANES : (r + 1) * LANES]
    lane = iota((rows, LANES), 1)

    def emit(j):
        shift = starts[j] & (M - 1)
        re = out_scr[j * rows : (j + 1) * rows, :]
        im = out_scr[(count + j) * rows : (count + j + 1) * rows, :]
        re = pltpu.roll(re, (LANES - shift) & (LANES - 1), 1)
        im = pltpu.roll(im, M - shift, 1)
        return jnp.where(lane < M, re, im)

    for j in range(0, count, 2):
        out_ref[j * rows : (j + 2) * rows, :] = jnp.concatenate([emit(j), emit(j + 1)], axis=0).astype(BF)


def prepare_kernel(
    facets,
    subs,
    length,
    sub_hbm,
    off_hbm,
    owner_hbm,
    kind_hbm,
    after_ref,
    screens_ref,
    cos_ref,
    sin_ref,
    gather_ref,
    both_ref,
    rank_ref,
    coarse_ref,
    inv_ref,
    seen,
    cos_scr,
    sin_scr,
    sub_ref,
    off_ref,
    owner_ref,
    kind_ref,
    sems,
):
    copies = scalars(
        [(sub_hbm, sub_ref), (off_hbm, off_ref), (owner_hbm, owner_ref), (kind_hbm, kind_ref)], sems
    )
    count = sub_ref.shape[0]
    rows = cos_ref.shape[0] // count
    span = screens_ref.shape[2] // 2
    chunks = length // LANES
    mine = lax.axis_index("facet")
    my_sub = lax.axis_index("sub")

    shape = (chunks, LANES)
    cos, sin = circle(iota(shape, 0) * iota(shape, 1), chunks)
    table = jnp.concatenate(
        [jnp.concatenate([cos, -sin], axis=1), jnp.concatenate([sin, cos], axis=1)], axis=0
    )
    inv_ref[: 2 * chunks, :] = high_low(table, False)
    inv_ref[2 * chunks :, :] = high_low(table, True)

    for copy in copies:
        copy.wait()
    my_off = off_ref[mine]

    shape = (span, LANES)
    row = iota(shape, 0)
    lane = iota(shape, 1)
    hit = row == my_off + lane % M
    both = jnp.where(hit, 1.0, 0.0).astype(BF)
    signed = jnp.where(hit, jnp.where(lane < M, -1.0, 1.0), 0.0).astype(BF)
    kinds = screens_ref.shape[0]
    tall = cos_scr.shape[0] // kinds
    first = my_sub * rows // tall * tall
    block = pl.ds(pl.multiple_of(first, tall), tall)
    cosines = screens_ref[:, block, :span].reshape(kinds * tall, span)
    sines = screens_ref[:, block, span:].reshape(kinds * tall, span)
    both_ref[...] = both
    cos_scr[...] = dot(cosines, both)
    sin_scr[...] = dot(sines, signed)
    for j in range(count):
        kind = pl.multiple_of(kind_ref[j] * tall + my_sub * rows - first, rows)
        cos_ref[j * rows : (j + 1) * rows, :] = cos_scr[pl.ds(kind, rows), :]
        sin_ref[j * rows : (j + 1) * rows, :] = sin_scr[pl.ds(kind, rows), :]

    for o in range(facets * subs):
        seen[o] = 0
    held = subs * CAP
    pieces = span // LANES
    places = []
    for j in range(count):
        who = owner_ref[j]
        slot = seen[who]
        seen[who] = slot + 1
        facet_step = (who // subs) ^ mine
        sub_step = (who % subs) ^ my_sub
        block = facet_step % 2 * (facets // 2) + facet_step // 2
        places.append(block * held * pieces + sub_step * CAP + slot)
    width = rank_ref.shape[1]
    place = column(places, width)
    lane = iota((count, width), 1)
    for c in range(pieces):
        hit = jnp.where(lane == place + c * held, 1.0, 0.0)
        rank_ref[c * count : (c + 1) * count, :] = hit.astype(BF)

    lane = iota((rows, LANES), 1)
    for j in range(count):
        shift = start_of(mine, sub_ref, off_ref, j, length) & (M - 1)
        gather_ref[j * rows : (j + 1) * rows, :] = (lane - shift) & (LANES - 1)

    lane = iota((8, 4 * count), 1)
    block = jnp.zeros((8, 4 * count), jnp.int32)
    for j in range(count):
        start = start_of(mine, sub_ref, off_ref, j, length) // M
        block = jnp.where(lane % count == j, start, block)
    block = jnp.concatenate([block] * (M // 8), axis=0)
    shape = (M, 4 * count)
    lane = iota(shape, 1)
    cos, sin = circle(block * iota(shape, 0), length // M)
    scale = 1 / math.sqrt(length)
    cos, sin = cos * scale, sin * scale
    lane_im = lane // count % 2 == 1
    low = lane >= 2 * count
    coarse_ref[:M, :] = high_low(jnp.where(lane_im, -sin, cos), low)
    coarse_ref[M:, :] = high_low(jnp.where(lane_im, cos, sin), low)


def tail_kernel(block_ref, out_ref):
    out_ref[...] = block_ref[block_ref.shape[0] - out_ref.shape[0] :, :]


def screen_kernel(own_ref, *refs):
    arrived, (cos_ref, sin_ref, out_ref) = refs[:-3], refs[-3:]
    windows = own_ref.shape[0]
    for at in range(0, windows, 16):
        pair = slice(at, at + 16)
        total = own_ref[pair, :]
        for ref in arrived:
            total = total + ref[pair, :].astype(F32)
        out_ref[pair, :] = total * cos_ref[pair, :] + pltpu.roll(total, M, 1) * sin_ref[pair, :]


def backward_kernel(others, size, product_ref, own_rows_ref, *refs):
    arrived, across, refs = refs[:others][::-1], refs[others : 2 * others + 1][::-1], refs[2 * others + 1 :]
    gather_ref, both_ref, rank_ref, coarse_ref, inv_ref, turn_ref, out_hbm = refs[:7]
    re_scr, im_scr, out_scr, flat_scr, out_sems = refs[7:]
    rows = out_hbm.shape[1]
    length = out_hbm.shape[2] // 2
    chunks = length // LANES
    windows = product_ref.shape[0]
    count = windows // rows

    held = [own_rows_ref[...]] + [ref[windows:, :] for ref in arrived] + [ref[...] for ref in across]
    ranked = dot(rank_ref[...], jnp.concatenate(held, axis=0)).astype(BF)
    ranked = jnp.concatenate([ranked[c : c + count] for c in range(0, ranked.shape[0], count)], axis=1)
    weights = dot(ranked, both_ref[...])

    for j in range(count):
        value = product_ref[j * rows : (j + 1) * rows, :] * weights[j : j + 1, :]
        value = value.astype(BF).astype(F32)
        place = gather_ref[j * rows : (j + 1) * rows, :]
        re = jnp.take_along_axis(value, place, axis=1)
        im = jnp.take_along_axis(value, place ^ M, axis=1)
        re_scr[pl.ds(j, rows, stride=count), :] = jnp.where(place < M, re, 0.0)
        im_scr[pl.ds(j, rows, stride=count), :] = jnp.where(place < M, im, 0.0)

    halves = []
    for scr in (re_scr, im_scr):
        halves.append(
            jnp.concatenate([scr[r * count : (r + 1) * count, :].astype(BF) for r in range(rows)], axis=1)
        )
    spread = jnp.concatenate(halves + halves, axis=0)
    inner = dot(coarse_ref[...], spread)
    twisted = []
    for r in range(rows):
        re = inner[:M, r * LANES : (r + 1) * LANES]
        im = inner[M:, r * LANES : (r + 1) * LANES]
        for q in range(LANES // M):
            cos = turn_ref[q * M : (q + 1) * M, :]
            sin = turn_ref[LANES + q * M : LANES + (q + 1) * M, :]
            both = jnp.concatenate([re * cos - im * sin, re * sin + im * cos], axis=1)
            twisted.append(both.astype(BF))
    twisted = jnp.concatenate(twisted, axis=0)
    points = dot_t(inv_ref[...], twisted)
    points = points[: 2 * chunks] + points[2 * chunks :]
    for r in range(rows):
        out_scr[pl.ds(r, 2 * chunks, stride=rows), :] = points[:, r * LANES : (r + 1) * LANES]
    parts = out_sems.shape[0]
    width = 2 * length // parts
    copies = []
    for p in range(parts):
        for c in range(p * width // LANES, (p + 1) * width // LANES):
            flat_scr[:, c * LANES : (c + 1) * LANES] = out_scr[c * rows : (c + 1) * rows, :]
        part = pl.ds(p * width, width)
        copies.append(pltpu.make_async_copy(flat_scr.at[:, part], out_hbm.at[0, :, part], out_sems.at[p]))
        copies[-1].start()
    for copy in copies:
        copy.wait()


def local(strips, facet_offset, subgrid_offset, owner, screen_index, screens, grid_weight):
    facets = lax.axis_size("facet")
    subs = lax.axis_size("sub")
    rows = strips.shape[1]
    length = strips.shape[2] // 2
    chunks = length // LANES
    count = subgrid_offset.shape[0]
    span = grid_weight.shape[1]
    kinds = screens.shape[0]
    hbm = pl.BlockSpec(memory_space=pl.ANY)
    vmem = pl.BlockSpec(memory_space=pltpu.VMEM)
    limit = pltpu.CompilerParams(vmem_limit_bytes=32 * 1024 * 1024)
    shaped = jax.ShapeDtypeStruct

    subgrid_offset, facet_offset, owner, screen_index = [
        pltpu.with_memory_space_constraint(x, pltpu.HBM) for x in (subgrid_offset, facet_offset, owner, screen_index)
    ]

    def swap(x, step):
        return lax.ppermute(x, "facet", [(i, i ^ step) for i in range(facets)])

    def cost(flops):
        return pl.CostEstimate(flops=flops, bytes_accessed=1 << 20, transcendentals=0)

    turn, fwd = pl.pallas_call(
        functools.partial(table_kernel, length),
        out_shape=[shaped((2 * LANES, LANES), F32), shaped((2 * chunks, 4 * chunks), BF)],
        out_specs=[vmem] * 2,
        compiler_params=limit,
        cost_estimate=cost(10**11),
    )()
    held = grid_weight
    step = 1
    while step < subs:
        last, beside = held, lax.ppermute(held, "sub", [(k, k ^ step) for k in range(subs)])
        if step == 1:
            windows, shift = pl.pallas_call(
                forward_kernel,
                out_shape=[shaped((count * rows, LANES), BF), shaped((2 * LANES, facets // 2 * LANES), BF)],
                in_specs=[hbm] * 2 + [vmem] * 3,
                out_specs=[vmem] * 2,
                scratch_shapes=[
                    pltpu.VMEM((rows * 2 * chunks, LANES), F32),
                    pltpu.VMEM((rows * LANES, 2 * LANES), BF),
                    pltpu.VMEM((2 * count * rows, LANES), F32),
                    pltpu.SMEM((count,), jnp.int32),
                    pltpu.SMEM((facets,), jnp.int32),
                    pltpu.SemaphoreType.DMA((2,)),
                ],
                compiler_params=limit,
            )(subgrid_offset, facet_offset, strips, turn, fwd)
            passed = swap(windows, 1)
        if step < subs // 2:
            beside = pl.pallas_call(
                join_kernel,
                out_shape=shaped((2 * held.shape[0], span), F32),
                in_specs=[vmem] * 2,
                out_specs=vmem,
                compiler_params=limit,
            )(held, beside)
        step *= 2
        held, _ = lax.optimization_barrier((beside, windows))

    tall = max(rows, 16)
    prepared = pl.pallas_call(
        functools.partial(prepare_kernel, facets, subs, length),
        out_shape=[
            shaped((count * rows, LANES), F32),
            shaped((count * rows, LANES), F32),
            shaped((count * rows, LANES), jnp.int32),
            shaped((span, LANES), BF),
            shaped((span // LANES * count, facets * subs * grid_weight.size // LANES), BF),
            shaped((2 * M, 4 * count), BF),
            shaped((4 * chunks, 2 * LANES), BF),
        ],
        in_specs=[hbm] * 5 + [vmem],
        out_specs=[vmem] * 7,
        scratch_shapes=[
            pltpu.SMEM((facets * subs,), jnp.int32),
            pltpu.VMEM((kinds * tall, LANES), F32),
            pltpu.VMEM((kinds * tall, LANES), F32),
            pltpu.SMEM((count,), jnp.int32),
            pltpu.SMEM((facets,), jnp.int32),
            pltpu.SMEM((count,), jnp.int32),
            pltpu.SMEM((count,), jnp.int32),
            pltpu.SemaphoreType.DMA((4,)),
        ],
        compiler_params=limit,
        cost_estimate=cost(2*10**10),
    )(subgrid_offset, facet_offset, owner, screen_index, last, screens)

    others = facets // 2 - 1
    shift, _ = lax.optimization_barrier((shift, prepared[0]))
    own, *merged = pl.pallas_call(
        merge_kernel,
        out_shape=[shaped(windows.shape, F32)] + [shaped(windows.shape, BF)] * others,
        in_specs=[vmem] * 3,
        out_specs=[vmem] * (1 + others),
        compiler_params=limit,
    )(windows, passed, shift)
    size = subs * grid_weight.size // LANES
    own_rows, *payloads = pl.pallas_call(
        functools.partial(pack_kernel, others),
        out_shape=[shaped((size, LANES), BF)] + [shaped((count * rows + size, LANES), BF)] * others,
        in_specs=[vmem] * (others + 2),
        out_specs=[vmem] * (1 + others),
        compiler_params=limit,
    )(*merged, last, beside)

    arrived = [swap(payload, 2 * n + 2) for n, payload in enumerate(payloads)]
    across = [swap(own_rows, 1), swap(own_rows, 3)]
    for block in arrived[1:]:
        tail = pl.pallas_call(
            tail_kernel,
            out_shape=shaped((size, LANES), BF),
            in_specs=[vmem],
            out_specs=vmem,
            compiler_params=limit,
        )(block)
        across.append(swap(tail, 1))

    cos, sin, *prepared = prepared
    product = pl.pallas_call(
        screen_kernel,
        out_shape=shaped(windows.shape, F32),
        in_specs=[vmem] * (others + 3),
        out_specs=vmem,
        compiler_params=limit,
    )(own, *arrived, cos, sin)

    return pl.pallas_call(
        functools.partial(backward_kernel, others, size),
        out_shape=shaped((1, rows, 2 * length), F32),
        in_specs=[vmem] * (2 * others + 9),
        out_specs=hbm,
        scratch_shapes=[
            pltpu.VMEM((rows * count, LANES), F32),
            pltpu.VMEM((rows * count, LANES), F32),
            pltpu.VMEM((2 * chunks * rows, LANES), F32),
            pltpu.VMEM((rows, 2 * length), F32),
            pltpu.SemaphoreType.DMA((4,)),
        ],
        compiler_params=limit,
    )(product, own_rows, *arrived[::-1], *across[::-1], *prepared, turn)


def solution(mesh):
    in_specs = (P("facet", "sub", None), P(), P(), P(), P(), P(), P(("facet", "sub"), None))
    out_specs = P("facet", "sub", None)
    return jax.shard_map(local, mesh=mesh, in_specs=in_specs, out_specs=out_specs, check_vma=False)
```

```python
import functools
import math

import jax
import jax.numpy as jnp
from jax import lax
from jax.experimental import pallas as pl
from jax.experimental.pallas import tpu as pltpu
from jax.sharding import PartitionSpec as P

M = 64
CAP = 4
LANES = 128

BF = jnp.bfloat16
F32 = jnp.float32


def dot(x, y):
    return jnp.dot(x, y, preferred_element_type=F32)


def dot_t(x, y):
    return lax.dot_general(x, y, (((1,), (1,)), ((), ())), preferred_element_type=F32)


def iota(shape, dim):
    return lax.broadcasted_iota(jnp.int32, shape, dim)


def sine(r):
    x = r * (2 * math.pi)
    y = x * x
    total = -1 / math.factorial(11)
    for n in (9, 7, 5, 3, 1):
        total = total * y + (-1) ** (n // 2) / math.factorial(n)
    return x * total


def circle(index, period):
    r = (index & (period - 1)).astype(F32) * (1 / period) - 0.5
    near = jnp.maximum(jnp.minimum(-r, 0.5 + r), r - 0.5)
    return sine(jnp.abs(r) - 0.25), sine(near)


def high_low(x, low):
    high = x.astype(BF).astype(F32)
    return jnp.where(low, x - high, high).astype(BF)


def column(values, width):
    groups = []
    row = iota((8, width), 0)
    for group in range(len(values) // 8):
        value = jnp.zeros((8, width), jnp.int32)
        for r in range(8):
            value = jnp.where(row == r, values[group * 8 + r], value)
        groups.append(value)
    return jnp.concatenate(groups, axis=0)


def start_of(mine, sub_ref, off_ref, j, length):
    return (sub_ref[j] + off_ref[mine]) & (length - 1)


def table_kernel(length, turn_ref, fwd_ref):
    cos, sin = circle(iota((LANES, LANES), 0) * iota((LANES, LANES), 1), length)
    turn_ref[:LANES, :] = cos
    turn_ref[LANES:, :] = sin

    chunks = length // LANES
    shape = (2 * chunks, 4 * chunks)
    row, lane = iota(shape, 0), iota(shape, 1)
    cos, sin = circle((row & (chunks - 1)) * (lane & (chunks - 1)), chunks)
    row_im, lane_im = row // chunks, lane // chunks % 2
    table = jnp.where(row_im == lane_im, cos, jnp.where(row_im == 0, sin, -sin))
    fwd_ref[...] = high_low(table, lane >= 2 * chunks)


def join_kernel(first_ref, second_ref, out_ref):
    out_ref[: first_ref.shape[0], :] = first_ref[...]
    out_ref[first_ref.shape[0] :, :] = second_ref[...]


def merge_kernel(windows_ref, passed_ref, shift_ref, own_ref, *out_refs):
    both = jnp.concatenate([windows_ref[...], passed_ref[...]], axis=1)
    merged = dot(both, shift_ref[...])
    own_ref[...] = merged[:, :LANES]
    for n, out_ref in enumerate(out_refs):
        out_ref[...] = merged[:, (n + 1) * LANES : (n + 2) * LANES].astype(BF)


def pack_kernel(others, *refs):
    merged_refs, held_refs, out_refs = refs[:others], refs[others : others + 2], refs[others + 2 :]
    held = jnp.concatenate([ref[...] for ref in held_refs], axis=0)
    laid = jnp.concatenate([held[:, c : c + LANES] for c in range(0, held.shape[1], LANES)], axis=0).astype(BF)
    out_refs[0][...] = laid
    for ref, out_ref in zip(merged_refs, out_refs[1:]):
        out_ref[: ref.shape[0], :] = ref[...]
        out_ref[ref.shape[0] :, :] = laid


def scalars(pairs, sems):
    copies = [pltpu.make_async_copy(a, b, sems.at[n]) for n, (a, b) in enumerate(pairs)]
    for copy in copies:
        copy.start()
    return copies


def forward_kernel(
    sub_hbm,
    off_hbm,
    strips_ref,
    turn_ref,
    fwd_ref,
    out_ref,
    shift_ref,
    in_scr,
    mid_scr,
    low_scr,
    sub_ref,
    off_ref,
    sems,
):
    copies = scalars([(sub_hbm, sub_ref), (off_hbm, off_ref)], sems)
    mine = lax.axis_index("facet")
    rows = strips_ref.shape[1]
    length = strips_ref.shape[2] // 2
    chunks = length // LANES
    count = sub_ref.shape[0]

    for c in range(2 * chunks):
        piece = strips_ref[0, :, c * LANES : (c + 1) * LANES].astype(F32)
        in_scr[pl.ds(c, rows, stride=2 * chunks), :] = piece
    points = jnp.concatenate(
        [in_scr[r * 2 * chunks : (r + 1) * 2 * chunks, :].astype(BF) for r in range(rows)], axis=1
    )
    inner = dot(fwd_ref[...], jnp.concatenate([points, points], axis=0))
    for r in range(rows):
        re = inner[:chunks, r * LANES : (r + 1) * LANES]
        im = inner[chunks:, r * LANES : (r + 1) * LANES]
        for q in range(LANES // chunks):
            cos = turn_ref[q * chunks : (q + 1) * chunks, :]
            sin = turn_ref[LANES + q * chunks : LANES + (q + 1) * chunks, :]
            at = r * LANES + q * chunks
            for lanes, value in ((slice(0, LANES), re * cos + im * sin), (slice(LANES, 2 * LANES), im * cos - re * sin)):
                high = value.astype(BF)
                mid_scr[at : at + chunks, lanes] = high
                low_scr[at : at + chunks, lanes] = (value - high.astype(F32)).astype(BF)

    for copy in copies:
        copy.wait()
    shape = (LANES, LANES)
    row = iota(shape, 0)
    lane = iota(shape, 1)
    apart = (lane // M - row // M) * 8192 + (lane % M - row % M)
    for n in range(shift_ref.shape[1] // LANES):
        for core in range(2):
            delta = off_ref[mine ^ core] - off_ref[mine ^ (2 * n)]
            rows_here = slice(core * LANES, (core + 1) * LANES)
            shift_ref[rows_here, n * LANES : (n + 1) * LANES] = jnp.where(apart == delta, 1.0, 0.0).astype(BF)

    starts = column([start_of(mine, sub_ref, off_ref, j, length) for j in range(count)], LANES)
    block = starts >> (M.bit_length() - 1)
    cos, sin = circle(block * iota((count, LANES), 1), length // M)
    scale = 1 / math.sqrt(length)
    cos, sin = cos * scale, sin * scale
    coarse = jnp.concatenate(
        [jnp.concatenate([cos, sin], axis=1), jnp.concatenate([-sin, cos], axis=1)], axis=0
    )
    coarse = jnp.concatenate([high_low(coarse, False), high_low(coarse, True)], axis=0)
    window = dot_t(coarse, mid_scr[...])
    window = window[: 2 * count] + window[2 * count :] + dot_t(coarse[: 2 * count], low_scr[...])
    lane = iota((count, LANES), 1)
    taken = (lane + (starts & (M - 1))) & (LANES - 1)
    for r in range(rows):
        re = window[:count, r * LANES : (r + 1) * LANES]
        im = window[count:, r * LANES : (r + 1) * LANES]
        re = jnp.take_along_axis(re, taken, axis=1)
        im = jnp.take_along_axis(im, taken ^ M, axis=1)
        out_ref[r * count : (r + 1) * count, :] = jnp.where(lane < M, re, im).astype(BF)


def prepare_kernel(
    subs,
    length,
    sub_hbm,
    off_hbm,
    kind_hbm,
    owner_hbm,
    after_ref,
    screens_ref,
    cos_ref,
    sin_ref,
    both_ref,
    other_ref,
    rank_ref,
    gather_ref,
    coarse_ref,
    inv_ref,
    cos_scr,
    sin_scr,
    sub_ref,
    off_ref,
    kind_ref,
    owner_ref,
    sems,
):
    pairs = [(sub_hbm, sub_ref), (off_hbm, off_ref), (kind_hbm, kind_ref), (owner_hbm, owner_ref)]
    copies = scalars(pairs, sems)
    chunks = length // LANES
    mine = lax.axis_index("facet")
    count = kind_ref.shape[0]
    rows = cos_ref.shape[0] // count
    span = screens_ref.shape[2] // 2
    my_sub = lax.axis_index("sub")
    shape = (span, LANES)
    lane = iota(shape, 1)
    apart = iota(shape, 0) - lane % M
    sign = jnp.where(lane < M, -1.0, 1.0)

    shape = (chunks, LANES)
    cos, sin = circle(iota(shape, 0) * iota(shape, 1), chunks)
    table = jnp.concatenate(
        [jnp.concatenate([cos, -sin], axis=1), jnp.concatenate([sin, cos], axis=1)], axis=0
    )
    inv_ref[: 2 * chunks, :] = high_low(table, False)
    inv_ref[2 * chunks :, :] = high_low(table, True)

    for copy in copies:
        copy.wait()
    hit = apart == off_ref[mine]
    both = jnp.where(hit, 1.0, 0.0).astype(BF)
    signed = jnp.where(hit, sign, 0.0).astype(BF)
    kinds = screens_ref.shape[0]
    tall = cos_scr.shape[0] // kinds
    first = my_sub * rows // tall * tall
    block = pl.ds(pl.multiple_of(first, tall), tall)
    cosines = screens_ref[:, block, :span].reshape(kinds * tall, span)
    sines = screens_ref[:, block, span:].reshape(kinds * tall, span)
    both_ref[...] = both
    other_ref[...] = jnp.where(apart == off_ref[mine ^ 1], 1.0, 0.0).astype(BF)
    cos_scr[...] = dot(cosines, both)
    sin_scr[...] = dot(sines, signed)
    for j in range(count):
        kind = pl.multiple_of(kind_ref[j] * tall + my_sub * rows - first, rows)
        cos_ref[pl.ds(j, rows, stride=count), :] = cos_scr[pl.ds(kind, rows), :]
        sin_ref[pl.ds(j, rows, stride=count), :] = sin_scr[pl.ds(kind, rows), :]

    owners = [owner_ref[j] for j in range(count)]
    lane = iota((8, LANES), 1)
    wide = []
    for first in range(0, count, LANES):
        value = jnp.full((8, LANES), -1, jnp.int32)
        for j in range(first, min(first + LANES, count)):
            value = jnp.where(lane == j - first, owners[j], value)
        wide.append(value)
    tall_owner = column(owners, LANES)
    slot = jnp.zeros((count, 1), F32)
    for n, value in enumerate(wide):
        same = jnp.concatenate([value] * (count // 8), axis=0) == tall_owner
        earlier = iota((count, LANES), 1) + n * LANES < iota((count, LANES), 0)
        slot = slot + jnp.sum(jnp.where(same & earlier, 1.0, 0.0), axis=1, keepdims=True)
    bits = subs.bit_length() - 1
    facet_step = (tall_owner >> bits) ^ mine
    sub_step = (tall_owner & (subs - 1)) ^ my_sub
    facets = off_ref.shape[0]
    block = (facet_step & 1) * (facets // 2) + (facet_step >> 1)
    place = (block * subs + sub_step) * CAP + slot.astype(jnp.int32)
    for at in range(0, rank_ref.shape[1], LANES):
        hit = iota((count, LANES), 1) + at == place
        rank_ref[:, at : at + LANES] = jnp.where(hit, 1.0, 0.0).astype(BF)

    starts = [start_of(mine, sub_ref, off_ref, j, length) for j in range(count)]
    gather_ref[...] = (iota((count, LANES), 1) - (column(starts, LANES) & (M - 1))) & (LANES - 1)

    lane = iota((8, 4 * count), 1)
    block = jnp.zeros((8, 4 * count), jnp.int32)
    for j in range(count):
        block = jnp.where(lane % count == j, starts[j] // M, block)
    block = jnp.concatenate([block] * (M // 8), axis=0)
    shape = (M, 4 * count)
    lane = iota(shape, 1)
    cos, sin = circle(block * iota(shape, 0), length // M)
    scale = 1 / math.sqrt(length)
    cos, sin = cos * scale, sin * scale
    lane_im = lane // count % 2 == 1
    low = lane >= 2 * count
    coarse_ref[:M, :] = high_low(jnp.where(lane_im, -sin, cos), low)
    coarse_ref[M:, :] = high_low(jnp.where(lane_im, cos, sin), low)


def cut(blocks, chunks, hits):
    rows = []
    for block in blocks:
        size = block.shape[0] // chunks
        rows.append(jnp.concatenate([block[c * size : (c + 1) * size] for c in range(chunks)], axis=1))
    return dot(jnp.concatenate(rows, axis=0), hits).astype(BF)


def tail_kernel(size, block_ref, hits_ref, out_ref):
    chunks = hits_ref.shape[0] // LANES
    out_ref[...] = cut([block_ref[block_ref.shape[0] - size :, :]], chunks, hits_ref[...])


def screen_kernel(size, own_ref, *refs):
    cos_ref, sin_ref, hits_ref, out_ref, cut_ref = refs[-5:]
    arrived, others = refs[:-8], refs[-8:-5]
    windows = own_ref.shape[0]
    for at in range(0, windows, 16):
        pair = slice(at, at + 16)
        total = own_ref[pair, :]
        for ref in arrived:
            total = total + ref[pair, :].astype(F32)
        out_ref[pair, :] = total * cos_ref[pair, :] + pltpu.roll(total, M, 1) * sin_ref[pair, :]
    held = [others[0][...]] + [ref[windows:, :] for ref in arrived] + [ref[...] for ref in others[1:]]
    cut_ref[...] = cut(held, hits_ref.shape[0] // LANES, hits_ref[...])


def backward_kernel(product_ref, *refs):
    cuts, refs = refs[:-9][::-1], refs[-9:]
    rank_ref, gather_ref, coarse_ref, inv_ref, turn_ref, out_hbm, out_scr, flat_scr, out_sems = refs
    rows = out_hbm.shape[1]
    length = out_hbm.shape[2] // 2
    chunks = length // LANES
    windows = product_ref.shape[0]
    count = windows // rows

    weights = dot(rank_ref[...], jnp.concatenate([ref[...] for ref in cuts], axis=0))

    place = gather_ref[...]
    inside = place < M
    blocks = []
    for r in range(rows):
        value = product_ref[r * count : (r + 1) * count, :] * weights
        value = value.astype(BF).astype(F32)
        re = jnp.where(inside, jnp.take_along_axis(value, place, axis=1), 0.0)
        im = jnp.where(inside, jnp.take_along_axis(value, place ^ M, axis=1), 0.0)
        blocks.append(jnp.concatenate([re, im], axis=0).astype(BF))
    spread = jnp.concatenate(blocks, axis=1)
    inner = dot(coarse_ref[...], jnp.concatenate([spread, spread], axis=0))
    twisted = []
    for r in range(rows):
        re = inner[:M, r * LANES : (r + 1) * LANES]
        im = inner[M:, r * LANES : (r + 1) * LANES]
        for q in range(LANES // M):
            cos = turn_ref[q * M : (q + 1) * M, :]
            sin = turn_ref[LANES + q * M : LANES + (q + 1) * M, :]
            both = jnp.concatenate([re * cos - im * sin, re * sin + im * cos], axis=1)
            twisted.append(both.astype(BF))
    twisted = jnp.concatenate(twisted, axis=0)
    points = dot_t(inv_ref[...], twisted)
    points = points[: 2 * chunks] + points[2 * chunks :]
    for r in range(rows):
        out_scr[pl.ds(r, 2 * chunks, stride=rows), :] = points[:, r * LANES : (r + 1) * LANES]
    parts = out_sems.shape[0]
    width = 2 * length // parts
    copies = []
    for p in range(parts):
        for c in range(p * width // LANES, (p + 1) * width // LANES):
            flat_scr[:, c * LANES : (c + 1) * LANES] = out_scr[c * rows : (c + 1) * rows, :]
        part = pl.ds(p * width, width)
        copies.append(pltpu.make_async_copy(flat_scr.at[:, part], out_hbm.at[0, :, part], out_sems.at[p]))
        copies[-1].start()
    for copy in copies:
        copy.wait()


def local(strips, facet_offset, subgrid_offset, owner, screen_index, screens, grid_weight):
    facets = lax.axis_size("facet")
    subs = lax.axis_size("sub")
    rows = strips.shape[1]
    length = strips.shape[2] // 2
    chunks = length // LANES
    count = subgrid_offset.shape[0]
    span = grid_weight.shape[1]
    kinds = screens.shape[0]
    hbm = pl.BlockSpec(memory_space=pl.ANY)
    vmem = pl.BlockSpec(memory_space=pltpu.VMEM)
    limit = pltpu.CompilerParams(vmem_limit_bytes=32 * 1024 * 1024)
    shaped = jax.ShapeDtypeStruct

    subgrid_offset, facet_offset, owner, screen_index = [
        pltpu.with_memory_space_constraint(x, pltpu.HBM) for x in (subgrid_offset, facet_offset, owner, screen_index)
    ]

    def swap(x, step):
        return lax.ppermute(x, "facet", [(i, i ^ step) for i in range(facets)])

    def cost(flops):
        return pl.CostEstimate(flops=flops, bytes_accessed=1 << 20, transcendentals=0)

    turn, fwd = pl.pallas_call(
        functools.partial(table_kernel, length),
        out_shape=[shaped((2 * LANES, LANES), F32), shaped((2 * chunks, 4 * chunks), BF)],
        out_specs=[vmem] * 2,
        compiler_params=limit,
        cost_estimate=cost(10**11),
    )()
    held = grid_weight
    steps = [1 << n for n in range(subs.bit_length() - 1)]
    for step in steps:
        last, beside = held, lax.ppermute(held, "sub", [(k, k ^ step) for k in range(subs)])
        if step == steps[0]:
            windows, shift = pl.pallas_call(
                forward_kernel,
                out_shape=[shaped((count * rows, LANES), BF), shaped((2 * LANES, facets // 2 * LANES), BF)],
                in_specs=[hbm] * 2 + [vmem] * 3,
                out_specs=[vmem] * 2,
                scratch_shapes=[
                    pltpu.VMEM((rows * 2 * chunks, LANES), F32),
                    pltpu.VMEM((rows * LANES, 2 * LANES), BF),
                    pltpu.VMEM((rows * LANES, 2 * LANES), BF),
                    pltpu.SMEM((count,), jnp.int32),
                    pltpu.SMEM((facets,), jnp.int32),
                    pltpu.SemaphoreType.DMA((2,)),
                ],
                compiler_params=limit,
            )(subgrid_offset, facet_offset, strips, turn, fwd)
            passed = swap(windows, 1)
        if step != steps[-1]:
            beside = pl.pallas_call(
                join_kernel,
                out_shape=shaped((2 * held.shape[0], span), F32),
                in_specs=[vmem] * 2,
                out_specs=vmem,
                compiler_params=limit,
            )(held, beside)
        held, _ = lax.optimization_barrier((beside, windows))

    tall = max(rows, 16)
    cos, sin, both, other, *ready = pl.pallas_call(
        functools.partial(prepare_kernel, subs, length),
        out_shape=[
            shaped((count * rows, LANES), F32),
            shaped((count * rows, LANES), F32),
            shaped((span, LANES), BF),
            shaped((span, LANES), BF),
            shaped((count, facets * subs * CAP), BF),
            shaped((count, LANES), jnp.int32),
            shaped((2 * M, 4 * count), BF),
            shaped((4 * chunks, 2 * LANES), BF),
        ],
        in_specs=[hbm] * 5 + [vmem],
        out_specs=[vmem] * 8,
        scratch_shapes=[
            pltpu.VMEM((kinds * tall, LANES), F32),
            pltpu.VMEM((kinds * tall, LANES), F32),
            pltpu.SMEM((count,), jnp.int32),
            pltpu.SMEM((facets,), jnp.int32),
            pltpu.SMEM((count,), jnp.int32),
            pltpu.SMEM((count,), jnp.int32),
            pltpu.SemaphoreType.DMA((4,)),
        ],
        compiler_params=limit,
        cost_estimate=cost(2 * 10**10),
    )(subgrid_offset, facet_offset, screen_index, owner, last, screens)

    others = facets // 2 - 1
    shift, _ = lax.optimization_barrier((shift, both))
    own, *merged = pl.pallas_call(
        merge_kernel,
        out_shape=[shaped(windows.shape, F32)] + [shaped(windows.shape, BF)] * others,
        in_specs=[vmem] * 3,
        out_specs=[vmem] * (1 + others),
        compiler_params=limit,
    )(windows, passed, shift)
    size = subs * grid_weight.size // LANES
    own_rows, *payloads = pl.pallas_call(
        functools.partial(pack_kernel, others),
        out_shape=[shaped((size, LANES), BF)] + [shaped((count * rows + size, LANES), BF)] * others,
        in_specs=[vmem] * (others + 2),
        out_specs=[vmem] * (1 + others),
        compiler_params=limit,
    )(*merged, last, beside)

    arrived = [swap(payload, 2 * n + 2) for n, payload in enumerate(payloads)]
    across = [swap(own_rows, 1), swap(own_rows, 3)]
    late = []
    for block in arrived[1:]:
        tail = pl.pallas_call(
            functools.partial(tail_kernel, size),
            out_shape=shaped((subs * CAP, LANES), BF),
            in_specs=[vmem] * 2,
            out_specs=vmem,
            compiler_params=limit,
        )(block, other)
        late.append(swap(tail, 1))

    product, early = pl.pallas_call(
        functools.partial(screen_kernel, size),
        out_shape=[shaped(windows.shape, F32), shaped(((others + 3) * subs * CAP, LANES), BF)],
        in_specs=[vmem] * (others + 7),
        out_specs=[vmem] * 2,
        compiler_params=limit,
    )(own, *arrived, own_rows, *across, cos, sin, both)

    return pl.pallas_call(
        backward_kernel,
        out_shape=shaped((1, rows, 2 * length), F32),
        in_specs=[vmem] * (len(late) + 7),
        out_specs=hbm,
        scratch_shapes=[
            pltpu.VMEM((2 * chunks * rows, LANES), F32),
            pltpu.VMEM((rows, 2 * length), F32),
            pltpu.SemaphoreType.DMA((4,)),
        ],
        compiler_params=limit,
    )(product, *late[::-1], early, *ready, turn)


def solution(mesh):
    in_specs = (P("facet", "sub", None), P(), P(), P(), P(), P(), P(("facet", "sub"), None))
    out_specs = P("facet", "sub", None)
    return jax.shard_map(local, mesh=mesh, in_specs=in_specs, out_specs=out_specs, check_vma=False)
```

```python
import functools
import math

import jax
import jax.numpy as jnp
from jax import lax
from jax.experimental import pallas as pl
from jax.experimental.pallas import tpu as pltpu
from jax.sharding import PartitionSpec as P

M = 64
CAP = 4
LANES = 128

BF = jnp.bfloat16
F32 = jnp.float32


def dot(x, y):
    return jnp.dot(x, y, preferred_element_type=F32)


def dot_t(x, y):
    return lax.dot_general(x, y, (((1,), (1,)), ((), ())), preferred_element_type=F32)


def iota(shape, dim):
    return lax.broadcasted_iota(jnp.int32, shape, dim)


def sine(r):
    x = r * (2 * math.pi)
    y = x * x
    total = -1 / math.factorial(11)
    for n in (9, 7, 5, 3, 1):
        total = total * y + (-1) ** (n // 2) / math.factorial(n)
    return x * total


def circle(index, period):
    r = (index & (period - 1)).astype(F32) * (1 / period) - 0.5
    near = jnp.maximum(jnp.minimum(-r, 0.5 + r), r - 0.5)
    return sine(jnp.abs(r) - 0.25), sine(near)


def high_low(x, low):
    high = x.astype(BF).astype(F32)
    return jnp.where(low, x - high, high).astype(BF)


def column(values, width):
    groups = []
    row = iota((8, width), 0)
    for group in range(len(values) // 8):
        value = jnp.zeros((8, width), jnp.int32)
        for r in range(8):
            value = jnp.where(row == r, values[group * 8 + r], value)
        groups.append(value)
    return jnp.concatenate(groups, axis=0)


def start_of(mine, sub_ref, off_ref, j, length):
    return (sub_ref[j] + off_ref[mine]) & (length - 1)


def table_kernel(length, turn_ref, fwd_ref):
    cos, sin = circle(iota((LANES, LANES), 0) * iota((LANES, LANES), 1), length)
    turn_ref[:LANES, :] = cos
    turn_ref[LANES:, :] = sin

    chunks = length // LANES
    shape = (2 * chunks, 4 * chunks)
    row, lane = iota(shape, 0), iota(shape, 1)
    cos, sin = circle((row & (chunks - 1)) * (lane & (chunks - 1)), chunks)
    row_im, lane_im = row // chunks, lane // chunks % 2
    table = jnp.where(row_im == lane_im, cos, jnp.where(row_im == 0, sin, -sin))
    fwd_ref[...] = high_low(table, lane >= 2 * chunks)


def join_kernel(first_ref, second_ref, out_ref):
    out_ref[: first_ref.shape[0], :] = first_ref[...]
    out_ref[first_ref.shape[0] :, :] = second_ref[...]


def merge_kernel(windows_ref, passed_ref, shift_ref, own_ref, *out_refs):
    both = jnp.concatenate([windows_ref[...], passed_ref[...]], axis=1)
    merged = dot(both, shift_ref[...])
    own_ref[...] = merged[:, :LANES]
    for n, out_ref in enumerate(out_refs):
        out_ref[...] = merged[:, (n + 1) * LANES : (n + 2) * LANES].astype(BF)


def pack_kernel(merged_ref, first_ref, second_ref, laid_ref, out_ref):
    held = jnp.concatenate([first_ref[...], second_ref[...]], axis=0)
    laid = jnp.concatenate([held[:, c : c + LANES] for c in range(0, held.shape[1], LANES)], axis=0).astype(BF)
    laid_ref[...] = laid
    out_ref[: merged_ref.shape[0], :] = merged_ref[...]
    out_ref[merged_ref.shape[0] :, :] = laid


def cut(blocks, hits):
    chunks = hits.shape[0] // LANES
    rows = []
    for block in blocks:
        size = block.shape[0] // chunks
        rows.append(jnp.concatenate([block[c * size : (c + 1) * size] for c in range(chunks)], axis=1))
    return dot(jnp.concatenate(rows, axis=0), hits).astype(BF)


def attach_kernel(parts, *refs):
    merged_refs, (laid_ref, passed_ref, shown_ref), out_refs = refs[:parts], refs[parts : parts + 3], refs[parts + 3 :]
    for n in range(parts):
        hits = shown_ref[:, n * LANES : (n + 1) * LANES]
        windows = merged_refs[n].shape[0]
        out_refs[n][:windows, :] = merged_refs[n][...]
        out_refs[n][windows:, :] = cut([laid_ref[...], passed_ref[...]], hits)


def scalars(pairs, sems):
    copies = [pltpu.make_async_copy(a, b, sems.at[n]) for n, (a, b) in enumerate(pairs)]
    for copy in copies:
        copy.start()
    return copies


def forward_kernel(
    sub_hbm,
    off_hbm,
    strips_ref,
    turn_ref,
    fwd_ref,
    out_ref,
    shift_ref,
    in_scr,
    mid_scr,
    low_scr,
    sub_ref,
    off_ref,
    sems,
):
    copies = scalars([(sub_hbm, sub_ref), (off_hbm, off_ref)], sems)
    mine = lax.axis_index("facet")
    rows = strips_ref.shape[1]
    length = strips_ref.shape[2] // 2
    chunks = length // LANES
    count = sub_ref.shape[0]

    for c in range(2 * chunks):
        piece = strips_ref[0, :, c * LANES : (c + 1) * LANES].astype(F32)
        in_scr[pl.ds(c, rows, stride=2 * chunks), :] = piece
    points = jnp.concatenate(
        [in_scr[r * 2 * chunks : (r + 1) * 2 * chunks, :].astype(BF) for r in range(rows)], axis=1
    )
    inner = dot(fwd_ref[...], jnp.concatenate([points, points], axis=0))
    for r in range(rows):
        re = inner[:chunks, r * LANES : (r + 1) * LANES]
        im = inner[chunks:, r * LANES : (r + 1) * LANES]
        for q in range(LANES // chunks):
            cos = turn_ref[q * chunks : (q + 1) * chunks, :]
            sin = turn_ref[LANES + q * chunks : LANES + (q + 1) * chunks, :]
            at = r * LANES + q * chunks
            for lanes, value in ((slice(0, LANES), re * cos + im * sin), (slice(LANES, 2 * LANES), im * cos - re * sin)):
                high = value.astype(BF)
                mid_scr[at : at + chunks, lanes] = high
                low_scr[at : at + chunks, lanes] = (value - high.astype(F32)).astype(BF)

    for copy in copies:
        copy.wait()
    shape = (LANES, LANES)
    row = iota(shape, 0)
    lane = iota(shape, 1)
    apart = (lane // M - row // M) * 8192 + (lane % M - row % M)
    for n in range(shift_ref.shape[1] // LANES):
        for core in range(2):
            delta = off_ref[mine ^ core] - off_ref[mine ^ (2 * n)]
            rows_here = slice(core * LANES, (core + 1) * LANES)
            shift_ref[rows_here, n * LANES : (n + 1) * LANES] = jnp.where(apart == delta, 1.0, 0.0).astype(BF)

    starts = column([start_of(mine, sub_ref, off_ref, j, length) for j in range(count)], LANES)
    block = starts >> (M.bit_length() - 1)
    cos, sin = circle(block * iota((count, LANES), 1), length // M)
    scale = 1 / math.sqrt(length)
    cos, sin = cos * scale, sin * scale
    coarse = jnp.concatenate(
        [jnp.concatenate([cos, sin], axis=1), jnp.concatenate([-sin, cos], axis=1)], axis=0
    )
    coarse = jnp.concatenate([high_low(coarse, False), high_low(coarse, True)], axis=0)
    window = dot_t(coarse, mid_scr[...])
    window = window[: 2 * count] + window[2 * count :] + dot_t(coarse[: 2 * count], low_scr[...])
    lane = iota((count, LANES), 1)
    taken = (lane + (starts & (M - 1))) & (LANES - 1)
    for r in range(rows):
        re = window[:count, r * LANES : (r + 1) * LANES]
        im = window[count:, r * LANES : (r + 1) * LANES]
        re = jnp.take_along_axis(re, taken, axis=1)
        im = jnp.take_along_axis(im, taken ^ M, axis=1)
        out_ref[r * count : (r + 1) * count, :] = jnp.where(lane < M, re, im).astype(BF)


def prepare_kernel(
    subs,
    length,
    sub_hbm,
    off_hbm,
    kind_hbm,
    owner_hbm,
    after_ref,
    screens_ref,
    cos_ref,
    sin_ref,
    both_ref,
    other_ref,
    shown_ref,
    rank_ref,
    gather_ref,
    coarse_ref,
    inv_ref,
    cos_scr,
    sin_scr,
    sub_ref,
    off_ref,
    kind_ref,
    owner_ref,
    sems,
):
    pairs = [(sub_hbm, sub_ref), (off_hbm, off_ref), (kind_hbm, kind_ref), (owner_hbm, owner_ref)]
    copies = scalars(pairs, sems)
    chunks = length // LANES
    mine = lax.axis_index("facet")
    count = kind_ref.shape[0]
    rows = cos_ref.shape[0] // count
    span = screens_ref.shape[2] // 2
    my_sub = lax.axis_index("sub")
    shape = (span, LANES)
    lane = iota(shape, 1)
    apart = iota(shape, 0) - lane % M
    sign = jnp.where(lane < M, -1.0, 1.0)

    shape = (chunks, LANES)
    cos, sin = circle(iota(shape, 0) * iota(shape, 1), chunks)
    table = jnp.concatenate(
        [jnp.concatenate([cos, -sin], axis=1), jnp.concatenate([sin, cos], axis=1)], axis=0
    )
    inv_ref[: 2 * chunks, :] = high_low(table, False)
    inv_ref[2 * chunks :, :] = high_low(table, True)

    for copy in copies:
        copy.wait()
    hit = apart == off_ref[mine]
    both = jnp.where(hit, 1.0, 0.0).astype(BF)
    signed = jnp.where(hit, sign, 0.0).astype(BF)
    kinds = screens_ref.shape[0]
    tall = cos_scr.shape[0] // kinds
    first = my_sub * rows // tall * tall
    block = pl.ds(pl.multiple_of(first, tall), tall)
    cosines = screens_ref[:, block, :span].reshape(kinds * tall, span)
    sines = screens_ref[:, block, span:].reshape(kinds * tall, span)
    both_ref[...] = both
    other_ref[...] = jnp.where(apart == off_ref[mine ^ 1], 1.0, 0.0).astype(BF)
    for n in range(shown_ref.shape[1] // LANES):
        hit = apart == off_ref[mine ^ (2 * n + 2)]
        shown_ref[:, n * LANES : (n + 1) * LANES] = jnp.where(hit, 1.0, 0.0).astype(BF)
    cos_scr[...] = dot(cosines, both)
    sin_scr[...] = dot(sines, signed)
    for j in range(count):
        kind = pl.multiple_of(kind_ref[j] * tall + my_sub * rows - first, rows)
        cos_ref[pl.ds(j, rows, stride=count), :] = cos_scr[pl.ds(kind, rows), :]
        sin_ref[pl.ds(j, rows, stride=count), :] = sin_scr[pl.ds(kind, rows), :]

    owners = [owner_ref[j] for j in range(count)]
    lane = iota((8, LANES), 1)
    wide = []
    for first in range(0, count, LANES):
        value = jnp.full((8, LANES), -1, jnp.int32)
        for j in range(first, min(first + LANES, count)):
            value = jnp.where(lane == j - first, owners[j], value)
        wide.append(value)
    tall_owner = column(owners, LANES)
    slot = jnp.zeros((count, 1), F32)
    for n, value in enumerate(wide):
        same = jnp.concatenate([value] * (count // 8), axis=0) == tall_owner
        earlier = iota((count, LANES), 1) + n * LANES < iota((count, LANES), 0)
        slot = slot + jnp.sum(jnp.where(same & earlier, 1.0, 0.0), axis=1, keepdims=True)
    bits = subs.bit_length() - 1
    facet_step = (tall_owner >> bits) ^ mine
    sub_step = (tall_owner & (subs - 1)) ^ my_sub
    facets = off_ref.shape[0]
    block = jnp.where(facet_step < 2, facet_step, facet_step + 1)
    block = jnp.where(facet_step == facets - 2, 2, block)
    block = jnp.where(facet_step == facets - 1, facets - 1, block)
    place = (block * subs + sub_step) * CAP + slot.astype(jnp.int32)
    for at in range(0, rank_ref.shape[1], LANES):
        hit = iota((count, LANES), 1) + at == place
        rank_ref[:, at : at + LANES] = jnp.where(hit, 1.0, 0.0).astype(BF)

    starts = [start_of(mine, sub_ref, off_ref, j, length) for j in range(count)]
    gather_ref[...] = (iota((count, LANES), 1) - (column(starts, LANES) & (M - 1))) & (LANES - 1)

    lane = iota((8, 4 * count), 1)
    block = jnp.zeros((8, 4 * count), jnp.int32)
    for j in range(count):
        block = jnp.where(lane % count == j, starts[j] // M, block)
    block = jnp.concatenate([block] * (M // 8), axis=0)
    shape = (M, 4 * count)
    lane = iota(shape, 1)
    cos, sin = circle(block * iota(shape, 0), length // M)
    scale = 1 / math.sqrt(length)
    cos, sin = cos * scale, sin * scale
    lane_im = lane // count % 2 == 1
    low = lane >= 2 * count
    coarse_ref[:M, :] = high_low(jnp.where(lane_im, -sin, cos), low)
    coarse_ref[M:, :] = high_low(jnp.where(lane_im, cos, sin), low)


def tail_kernel(size, block_ref, hits_ref, out_ref):
    out_ref[...] = cut([block_ref[block_ref.shape[0] - size :, :]], hits_ref[...])


def screen_kernel(own_ref, *refs):
    laid_ref, passed_ref, cos_ref, sin_ref, hits_ref, out_ref, cut_ref = refs[-7:]
    arrived = refs[:-7]
    windows = own_ref.shape[0]
    for at in range(0, windows, 16):
        pair = slice(at, at + 16)
        total = own_ref[pair, :]
        for ref in arrived:
            total = total + ref[pair, :].astype(F32)
        out_ref[pair, :] = total * cos_ref[pair, :] + pltpu.roll(total, M, 1) * sin_ref[pair, :]
    here = cut([laid_ref[...], passed_ref[...], arrived[-1][windows:, :]], hits_ref[...])
    cut_ref[: here.shape[0], :] = here
    at = here.shape[0]
    for ref in arrived[:-1]:
        rows = ref.shape[0] - windows
        cut_ref[at : at + rows, :] = ref[windows:, :]
        at += rows


def backward_kernel(product_ref, *refs):
    cuts, refs = refs[:-9], refs[-9:]
    rank_ref, gather_ref, coarse_ref, inv_ref, turn_ref, out_hbm, out_scr, flat_scr, out_sems = refs
    rows = out_hbm.shape[1]
    length = out_hbm.shape[2] // 2
    chunks = length // LANES
    windows = product_ref.shape[0]
    count = windows // rows

    weights = dot(rank_ref[...], jnp.concatenate([ref[...] for ref in cuts], axis=0))

    place = gather_ref[...]
    inside = place < M
    blocks = []
    for r in range(rows):
        value = product_ref[r * count : (r + 1) * count, :] * weights
        value = value.astype(BF).astype(F32)
        re = jnp.where(inside, jnp.take_along_axis(value, place, axis=1), 0.0)
        im = jnp.where(inside, jnp.take_along_axis(value, place ^ M, axis=1), 0.0)
        blocks.append(jnp.concatenate([re, im], axis=0).astype(BF))
    spread = jnp.concatenate(blocks, axis=1)
    inner = dot(coarse_ref[...], jnp.concatenate([spread, spread], axis=0))
    twisted = []
    for r in range(rows):
        re = inner[:M, r * LANES : (r + 1) * LANES]
        im = inner[M:, r * LANES : (r + 1) * LANES]
        for q in range(LANES // M):
            cos = turn_ref[q * M : (q + 1) * M, :]
            sin = turn_ref[LANES + q * M : LANES + (q + 1) * M, :]
            both = jnp.concatenate([re * cos - im * sin, re * sin + im * cos], axis=1)
            twisted.append(both.astype(BF))
    twisted = jnp.concatenate(twisted, axis=0)
    points = dot_t(inv_ref[...], twisted)
    points = points[: 2 * chunks] + points[2 * chunks :]
    for r in range(rows):
        out_scr[pl.ds(r, 2 * chunks, stride=rows), :] = points[:, r * LANES : (r + 1) * LANES]
    parts = out_sems.shape[0]
    width = 2 * length // parts
    copies = []
    for p in range(parts):
        for c in range(p * width // LANES, (p + 1) * width // LANES):
            flat_scr[:, c * LANES : (c + 1) * LANES] = out_scr[c * rows : (c + 1) * rows, :]
        part = pl.ds(p * width, width)
        copies.append(pltpu.make_async_copy(flat_scr.at[:, part], out_hbm.at[0, :, part], out_sems.at[p]))
        copies[-1].start()
    for copy in copies:
        copy.wait()


def local(strips, facet_offset, subgrid_offset, owner, screen_index, screens, grid_weight):
    facets = lax.axis_size("facet")
    subs = lax.axis_size("sub")
    rows = strips.shape[1]
    length = strips.shape[2] // 2
    chunks = length // LANES
    count = subgrid_offset.shape[0]
    span = grid_weight.shape[1]
    kinds = screens.shape[0]
    hbm = pl.BlockSpec(memory_space=pl.ANY)
    vmem = pl.BlockSpec(memory_space=pltpu.VMEM)
    limit = pltpu.CompilerParams(vmem_limit_bytes=32 * 1024 * 1024)
    shaped = jax.ShapeDtypeStruct

    subgrid_offset, facet_offset, owner, screen_index = [
        pltpu.with_memory_space_constraint(x, pltpu.HBM) for x in (subgrid_offset, facet_offset, owner, screen_index)
    ]

    def swap(x, step):
        return lax.ppermute(x, "facet", [(i, i ^ step) for i in range(facets)])

    def cost(flops):
        return pl.CostEstimate(flops=flops, bytes_accessed=1 << 20, transcendentals=0)

    turn, fwd = pl.pallas_call(
        functools.partial(table_kernel, length),
        out_shape=[shaped((2 * LANES, LANES), F32), shaped((2 * chunks, 4 * chunks), BF)],
        out_specs=[vmem] * 2,
        compiler_params=limit,
        cost_estimate=cost(10**11),
    )()
    held = grid_weight
    steps = [1 << n for n in range(subs.bit_length() - 1)]
    for step in steps:
        last, beside = held, lax.ppermute(held, "sub", [(k, k ^ step) for k in range(subs)])
        if step == steps[0]:
            windows, shift = pl.pallas_call(
                forward_kernel,
                out_shape=[shaped((count * rows, LANES), BF), shaped((2 * LANES, facets // 2 * LANES), BF)],
                in_specs=[hbm] * 2 + [vmem] * 3,
                out_specs=[vmem] * 2,
                scratch_shapes=[
                    pltpu.VMEM((rows * 2 * chunks, LANES), F32),
                    pltpu.VMEM((rows * LANES, 2 * LANES), BF),
                    pltpu.VMEM((rows * LANES, 2 * LANES), BF),
                    pltpu.SMEM((count,), jnp.int32),
                    pltpu.SMEM((facets,), jnp.int32),
                    pltpu.SemaphoreType.DMA((2,)),
                ],
                compiler_params=limit,
            )(subgrid_offset, facet_offset, strips, turn, fwd)
            passed = swap(windows, 1)
        if step != steps[-1]:
            beside = pl.pallas_call(
                join_kernel,
                out_shape=shaped((2 * held.shape[0], span), F32),
                in_specs=[vmem] * 2,
                out_specs=vmem,
                compiler_params=limit,
            )(held, beside)
        held, _ = lax.optimization_barrier((beside, windows))

    tall = max(rows, 16)
    cos, sin, both, other, shown, *ready = pl.pallas_call(
        functools.partial(prepare_kernel, subs, length),
        out_shape=[
            shaped((count * rows, LANES), F32),
            shaped((count * rows, LANES), F32),
            shaped((span, LANES), BF),
            shaped((span, LANES), BF),
            shaped((span, (facets // 2 - 2) * LANES), BF),
            shaped((count, facets * subs * CAP), BF),
            shaped((count, LANES), jnp.int32),
            shaped((2 * M, 4 * count), BF),
            shaped((4 * chunks, 2 * LANES), BF),
        ],
        in_specs=[hbm] * 5 + [vmem],
        out_specs=[vmem] * 9,
        scratch_shapes=[
            pltpu.VMEM((kinds * tall, LANES), F32),
            pltpu.VMEM((kinds * tall, LANES), F32),
            pltpu.SMEM((count,), jnp.int32),
            pltpu.SMEM((facets,), jnp.int32),
            pltpu.SMEM((count,), jnp.int32),
            pltpu.SMEM((count,), jnp.int32),
            pltpu.SemaphoreType.DMA((4,)),
        ],
        compiler_params=limit,
        cost_estimate=cost(2 * 10**10),
    )(subgrid_offset, facet_offset, screen_index, owner, last, screens)

    others = facets // 2 - 1
    shift, _ = lax.optimization_barrier((shift, both))
    own, *merged = pl.pallas_call(
        merge_kernel,
        out_shape=[shaped(windows.shape, F32)] + [shaped(windows.shape, BF)] * others,
        in_specs=[vmem] * 3,
        out_specs=[vmem] * (1 + others),
        compiler_params=limit,
    )(windows, passed, shift)
    size = subs * grid_weight.size // LANES
    laid, payload = pl.pallas_call(
        pack_kernel,
        out_shape=[shaped((size, LANES), BF), shaped((count * rows + size, LANES), BF)],
        in_specs=[vmem] * 3,
        out_specs=[vmem] * 2,
        compiler_params=limit,
    )(merged[-1], last, beside)

    far = swap(payload, facets - 2)
    laid_other = swap(laid, 1)
    parts = others - 1
    payloads = pl.pallas_call(
        functools.partial(attach_kernel, parts),
        out_shape=[shaped((count * rows + 2 * subs * CAP, LANES), BF)] * parts,
        in_specs=[vmem] * (parts + 3),
        out_specs=[vmem] * parts,
        compiler_params=limit,
    )(*merged[:-1], laid, laid_other, shown)
    arrived = [swap(block, 2 * n + 2) for n, block in enumerate(payloads)] + [far]
    tail = pl.pallas_call(
        functools.partial(tail_kernel, size),
        out_shape=shaped((subs * CAP, LANES), BF),
        in_specs=[vmem] * 2,
        out_specs=vmem,
        compiler_params=limit,
    )(far, other)
    late = swap(tail, 1)

    product, early = pl.pallas_call(
        screen_kernel,
        out_shape=[shaped(windows.shape, F32), shaped(((facets - 1) * subs * CAP, LANES), BF)],
        in_specs=[vmem] * (others + 6),
        out_specs=[vmem] * 2,
        compiler_params=limit,
    )(own, *arrived, laid, laid_other, cos, sin, both)

    return pl.pallas_call(
        backward_kernel,
        out_shape=shaped((1, rows, 2 * length), F32),
        in_specs=[vmem] * 8,
        out_specs=hbm,
        scratch_shapes=[
            pltpu.VMEM((2 * chunks * rows, LANES), F32),
            pltpu.VMEM((rows, 2 * length), F32),
            pltpu.SemaphoreType.DMA((4,)),
        ],
        compiler_params=limit,
    )(product, early, late, *ready, turn)


def solution(mesh):
    in_specs = (P("facet", "sub", None), P(), P(), P(), P(), P(), P(("facet", "sub"), None))
    out_specs = P("facet", "sub", None)
    return jax.shard_map(local, mesh=mesh, in_specs=in_specs, out_specs=out_specs, check_vma=False)
```

```python
import functools
import math

import jax
import jax.numpy as jnp
from jax import lax
from jax.experimental import pallas as pl
from jax.experimental.pallas import tpu as pltpu
from jax.sharding import PartitionSpec as P

M = 64
CAP = 4
LANES = 128

BF = jnp.bfloat16
F32 = jnp.float32


def dot(x, y):
    return jnp.dot(x, y, preferred_element_type=F32)


def dot_t(x, y):
    return lax.dot_general(x, y, (((1,), (1,)), ((), ())), preferred_element_type=F32)


def iota(shape, dim):
    return lax.broadcasted_iota(jnp.int32, shape, dim)


def sine(r):
    x = r * (2 * math.pi)
    y = x * x
    total = -1 / math.factorial(11)
    for n in (9, 7, 5, 3, 1):
        total = total * y + (-1) ** (n // 2) / math.factorial(n)
    return x * total


def circle(index, period):
    r = (index & (period - 1)).astype(F32) * (1 / period) - 0.5
    near = jnp.maximum(jnp.minimum(-r, 0.5 + r), r - 0.5)
    return sine(jnp.abs(r) - 0.25), sine(near)


def high_low(x, low):
    high = x.astype(BF).astype(F32)
    return jnp.where(low, x - high, high).astype(BF)


def column(values, width):
    groups = []
    row = iota((8, width), 0)
    for group in range(len(values) // 8):
        value = jnp.zeros((8, width), jnp.int32)
        for r in range(8):
            value = jnp.where(row == r, values[group * 8 + r], value)
        groups.append(value)
    return jnp.concatenate(groups, axis=0)


def start_of(mine, sub_ref, off_ref, j, length):
    return (sub_ref[j] + off_ref[mine]) & (length - 1)


def table_kernel(length, turn_ref, fwd_ref):
    cos, sin = circle(iota((LANES, LANES), 0) * iota((LANES, LANES), 1), length)
    turn_ref[:LANES, :] = cos
    turn_ref[LANES:, :] = sin

    chunks = length // LANES
    shape = (2 * chunks, 4 * chunks)
    row, lane = iota(shape, 0), iota(shape, 1)
    cos, sin = circle((row & (chunks - 1)) * (lane & (chunks - 1)), chunks)
    row_im, lane_im = row // chunks, lane // chunks % 2
    table = jnp.where(row_im == lane_im, cos, jnp.where(row_im == 0, sin, -sin))
    fwd_ref[...] = high_low(table, lane >= 2 * chunks)


def join_kernel(first_ref, second_ref, out_ref):
    out_ref[: first_ref.shape[0], :] = first_ref[...]
    out_ref[first_ref.shape[0] :, :] = second_ref[...]


def merge_kernel(windows_ref, passed_ref, shift_ref, own_ref, *out_refs):
    both = jnp.concatenate([windows_ref[...], passed_ref[...]], axis=1)
    merged = dot(both, shift_ref[...])
    own_ref[...] = merged[:, :LANES]
    for n, out_ref in enumerate(out_refs):
        out_ref[...] = merged[:, (n + 1) * LANES : (n + 2) * LANES].astype(BF)


def pack_kernel(merged_ref, first_ref, second_ref, laid_ref, out_ref):
    held = jnp.concatenate([first_ref[...], second_ref[...]], axis=0)
    laid = jnp.concatenate([held[:, c : c + LANES] for c in range(0, held.shape[1], LANES)], axis=0).astype(BF)
    laid_ref[...] = laid
    out_ref[: merged_ref.shape[0], :] = merged_ref[...]
    out_ref[merged_ref.shape[0] :, :] = laid


def cut(blocks, hits):
    chunks = hits.shape[0] // LANES
    rows = []
    for block in blocks:
        size = block.shape[0] // chunks
        rows.append(jnp.concatenate([block[c * size : (c + 1) * size] for c in range(chunks)], axis=1))
    return dot(jnp.concatenate(rows, axis=0), hits).astype(BF)


def attach_kernel(parts, *refs):
    merged_refs, (laid_ref, passed_ref, shown_ref), out_refs = refs[:parts], refs[parts : parts + 3], refs[parts + 3 :]
    for n in range(parts):
        hits = shown_ref[:, n * LANES : (n + 1) * LANES]
        windows = merged_refs[n].shape[0]
        out_refs[n][:windows, :] = merged_refs[n][...]
        out_refs[n][windows:, :] = cut([laid_ref[...], passed_ref[...]], hits)


def scalars(pairs, sems):
    copies = [pltpu.make_async_copy(a, b, sems.at[n]) for n, (a, b) in enumerate(pairs)]
    for copy in copies:
        copy.start()
    return copies


def forward_kernel(
    sub_hbm,
    off_hbm,
    strips_ref,
    turn_ref,
    fwd_ref,
    out_ref,
    shift_ref,
    in_scr,
    mid_scr,
    low_scr,
    sub_ref,
    off_ref,
    sems,
):
    copies = scalars([(sub_hbm, sub_ref), (off_hbm, off_ref)], sems)
    mine = lax.axis_index("facet")
    rows = strips_ref.shape[1]
    length = strips_ref.shape[2] // 2
    chunks = length // LANES
    count = sub_ref.shape[0]

    for c in range(2 * chunks):
        piece = strips_ref[0, :, c * LANES : (c + 1) * LANES].astype(F32)
        in_scr[pl.ds(c, rows, stride=2 * chunks), :] = piece
    points = jnp.concatenate(
        [in_scr[r * 2 * chunks : (r + 1) * 2 * chunks, :].astype(BF) for r in range(rows)], axis=1
    )
    inner = dot(fwd_ref[...], jnp.concatenate([points, points], axis=0))
    for r in range(rows):
        re = inner[:chunks, r * LANES : (r + 1) * LANES]
        im = inner[chunks:, r * LANES : (r + 1) * LANES]
        for q in range(LANES // chunks):
            cos = turn_ref[q * chunks : (q + 1) * chunks, :]
            sin = turn_ref[LANES + q * chunks : LANES + (q + 1) * chunks, :]
            at = r * LANES + q * chunks
            for lanes, value in ((slice(0, LANES), re * cos + im * sin), (slice(LANES, 2 * LANES), im * cos - re * sin)):
                high = value.astype(BF)
                mid_scr[at : at + chunks, lanes] = high
                low_scr[at : at + chunks, lanes] = (value - high.astype(F32)).astype(BF)

    for copy in copies:
        copy.wait()
    shape = (LANES, LANES)
    row = iota(shape, 0)
    lane = iota(shape, 1)
    apart = (lane // M - row // M) * 8192 + (lane % M - row % M)
    for n in range(shift_ref.shape[1] // LANES):
        for core in range(2):
            delta = off_ref[mine ^ core] - off_ref[mine ^ (2 * n)]
            rows_here = slice(core * LANES, (core + 1) * LANES)
            shift_ref[rows_here, n * LANES : (n + 1) * LANES] = jnp.where(apart == delta, 1.0, 0.0).astype(BF)

    starts = column([start_of(mine, sub_ref, off_ref, j, length) for j in range(count)], LANES)
    block = starts >> (M.bit_length() - 1)
    cos, sin = circle(block * iota((count, LANES), 1), length // M)
    scale = 1 / math.sqrt(length)
    cos, sin = cos * scale, sin * scale
    coarse = jnp.concatenate(
        [jnp.concatenate([cos, sin], axis=1), jnp.concatenate([-sin, cos], axis=1)], axis=0
    )
    coarse = jnp.concatenate([high_low(coarse, False), high_low(coarse, True)], axis=0)
    window = dot_t(coarse, mid_scr[...])
    window = window[: 2 * count] + window[2 * count :] + dot_t(coarse[: 2 * count], low_scr[...])
    lane = iota((count, LANES), 1)
    taken = (lane + (starts & (M - 1))) & (LANES - 1)
    for r in range(rows):
        re = window[:count, r * LANES : (r + 1) * LANES]
        im = window[count:, r * LANES : (r + 1) * LANES]
        re = jnp.take_along_axis(re, taken, axis=1)
        im = jnp.take_along_axis(im, taken ^ M, axis=1)
        out_ref[r * count : (r + 1) * count, :] = jnp.where(lane < M, re, im).astype(BF)


def prepare_kernel(
    subs,
    length,
    sub_hbm,
    off_hbm,
    kind_hbm,
    owner_hbm,
    after_ref,
    screens_ref,
    cos_ref,
    sin_ref,
    both_ref,
    other_ref,
    shown_ref,
    rank_ref,
    gather_ref,
    coarse_ref,
    inv_ref,
    cos_scr,
    sin_scr,
    sub_ref,
    off_ref,
    kind_ref,
    owner_ref,
    sems,
):
    pairs = [(sub_hbm, sub_ref), (off_hbm, off_ref), (kind_hbm, kind_ref), (owner_hbm, owner_ref)]
    copies = scalars(pairs, sems)
    chunks = length // LANES
    mine = lax.axis_index("facet")
    count = kind_ref.shape[0]
    rows = cos_ref.shape[0] // count
    span = screens_ref.shape[2] // 2
    my_sub = lax.axis_index("sub")
    shape = (span, LANES)
    lane = iota(shape, 1)
    apart = iota(shape, 0) - lane % M
    sign = jnp.where(lane < M, -1.0, 1.0)

    shape = (chunks, LANES)
    cos, sin = circle(iota(shape, 0) * iota(shape, 1), chunks)
    table = jnp.concatenate(
        [jnp.concatenate([cos, -sin], axis=1), jnp.concatenate([sin, cos], axis=1)], axis=0
    )
    inv_ref[: 2 * chunks, :] = high_low(table, False)
    inv_ref[2 * chunks :, :] = high_low(table, True)

    for copy in copies:
        copy.wait()
    hit = apart == off_ref[mine]
    both = jnp.where(hit, 1.0, 0.0).astype(BF)
    signed = jnp.where(hit, sign, 0.0).astype(BF)
    kinds = screens_ref.shape[0]
    tall = cos_scr.shape[0] // kinds
    first = my_sub * rows // tall * tall
    block = pl.ds(pl.multiple_of(first, tall), tall)
    cosines = screens_ref[:, block, :span].reshape(kinds * tall, span)
    sines = screens_ref[:, block, span:].reshape(kinds * tall, span)
    both_ref[...] = both
    other_ref[...] = jnp.where(apart == off_ref[mine ^ 1], 1.0, 0.0).astype(BF)
    for n in range(shown_ref.shape[1] // LANES):
        hit = apart == off_ref[mine ^ (2 * n + 2)]
        shown_ref[:, n * LANES : (n + 1) * LANES] = jnp.where(hit, 1.0, 0.0).astype(BF)
    cos_scr[...] = dot(cosines, both)
    sin_scr[...] = dot(sines, signed)
    for j in range(count):
        kind = pl.multiple_of(kind_ref[j] * tall + my_sub * rows - first, rows)
        cos_ref[pl.ds(j, rows, stride=count), :] = cos_scr[pl.ds(kind, rows), :]
        sin_ref[pl.ds(j, rows, stride=count), :] = sin_scr[pl.ds(kind, rows), :]

    owners = [owner_ref[j] for j in range(count)]
    lane = iota((8, LANES), 1)
    wide = []
    for first in range(0, count, LANES):
        value = jnp.full((8, LANES), -1, jnp.int32)
        for j in range(first, min(first + LANES, count)):
            value = jnp.where(lane == j - first, owners[j], value)
        wide.append(value)
    tall_owner = column(owners, LANES)
    slot = jnp.zeros((count, 1), F32)
    for n, value in enumerate(wide):
        same = jnp.concatenate([value] * (count // 8), axis=0) == tall_owner
        earlier = iota((count, LANES), 1) + n * LANES < iota((count, LANES), 0)
        slot = slot + jnp.sum(jnp.where(same & earlier, 1.0, 0.0), axis=1, keepdims=True)
    bits = subs.bit_length() - 1
    facet_step = (tall_owner >> bits) ^ mine
    sub_step = (tall_owner & (subs - 1)) ^ my_sub
    facets = off_ref.shape[0]
    block = jnp.where(facet_step < 2, facet_step, facet_step + 1)
    block = jnp.where(facet_step == facets - 2, 2, block)
    block = jnp.where(facet_step == facets - 1, facets - 1, block)
    place = (block * subs + sub_step) * CAP + slot.astype(jnp.int32)
    for at in range(0, rank_ref.shape[1], LANES):
        hit = iota((count, LANES), 1) + at == place
        rank_ref[:, at : at + LANES] = jnp.where(hit, 1.0, 0.0).astype(BF)

    starts = [start_of(mine, sub_ref, off_ref, j, length) for j in range(count)]
    gather_ref[...] = (iota((count, LANES), 1) - (column(starts, LANES) & (M - 1))) & (LANES - 1)

    lane = iota((8, 4 * count), 1)
    block = jnp.zeros((8, 4 * count), jnp.int32)
    for j in range(count):
        block = jnp.where(lane % count == j, starts[j] // M, block)
    block = jnp.concatenate([block] * (M // 8), axis=0)
    shape = (M, 4 * count)
    lane = iota(shape, 1)
    cos, sin = circle(block * iota(shape, 0), length // M)
    scale = 1 / math.sqrt(length)
    cos, sin = cos * scale, sin * scale
    lane_im = lane // count % 2 == 1
    low = lane >= 2 * count
    coarse_ref[:M, :] = high_low(jnp.where(lane_im, -sin, cos), low)
    coarse_ref[M:, :] = high_low(jnp.where(lane_im, cos, sin), low)


def first_kernel(own_ref, block_ref, laid_ref, passed_ref, hits_ref, other_ref, tail_ref, cut_ref, total_ref):
    windows = own_ref.shape[0]
    rows = block_ref[windows:, :]
    tail_ref[...] = cut([rows], other_ref[...])
    cut_ref[...] = cut([laid_ref[...], passed_ref[...], rows], hits_ref[...])
    total_ref[...] = own_ref[...] + block_ref[:windows, :].astype(F32)


def backward_kernel(total_ref, *refs):
    arrived, refs = refs[:-13], refs[-13:]
    cut_ref, late_ref, cos_ref, sin_ref = refs[:4]
    rank_ref, gather_ref, coarse_ref, inv_ref, turn_ref, out_hbm, out_scr, flat_scr, out_sems = refs[4:]
    rows = out_hbm.shape[1]
    length = out_hbm.shape[2] // 2
    chunks = length // LANES
    windows = total_ref.shape[0]
    count = windows // rows

    cuts = [cut_ref[...]] + [ref[windows:, :] for ref in arrived] + [late_ref[...]]
    weights = dot(rank_ref[...], jnp.concatenate(cuts, axis=0))

    place = gather_ref[...]
    inside = place < M
    blocks = []
    for r in range(rows):
        here = slice(r * count, (r + 1) * count)
        total = total_ref[here, :]
        for ref in arrived:
            total = total + ref[here, :].astype(F32)
        value = (total * cos_ref[here, :] + pltpu.roll(total, M, 1) * sin_ref[here, :]) * weights
        value = value.astype(BF).astype(F32)
        re = jnp.where(inside, jnp.take_along_axis(value, place, axis=1), 0.0)
        im = jnp.where(inside, jnp.take_along_axis(value, place ^ M, axis=1), 0.0)
        blocks.append(jnp.concatenate([re, im], axis=0).astype(BF))
    spread = jnp.concatenate(blocks, axis=1)
    inner = dot(coarse_ref[...], jnp.concatenate([spread, spread], axis=0))
    twisted = []
    for r in range(rows):
        re = inner[:M, r * LANES : (r + 1) * LANES]
        im = inner[M:, r * LANES : (r + 1) * LANES]
        for q in range(LANES // M):
            cos = turn_ref[q * M : (q + 1) * M, :]
            sin = turn_ref[LANES + q * M : LANES + (q + 1) * M, :]
            both = jnp.concatenate([re * cos - im * sin, re * sin + im * cos], axis=1)
            twisted.append(both.astype(BF))
    twisted = jnp.concatenate(twisted, axis=0)
    points = dot_t(inv_ref[...], twisted)
    points = points[: 2 * chunks] + points[2 * chunks :]
    for r in range(rows):
        out_scr[pl.ds(r, 2 * chunks, stride=rows), :] = points[:, r * LANES : (r + 1) * LANES]
    parts = out_sems.shape[0]
    width = 2 * length // parts
    copies = []
    for p in range(parts):
        for c in range(p * width // LANES, (p + 1) * width // LANES):
            flat_scr[:, c * LANES : (c + 1) * LANES] = out_scr[c * rows : (c + 1) * rows, :]
        part = pl.ds(p * width, width)
        copies.append(pltpu.make_async_copy(flat_scr.at[:, part], out_hbm.at[0, :, part], out_sems.at[p]))
        copies[-1].start()
    for copy in copies:
        copy.wait()


def local(strips, facet_offset, subgrid_offset, owner, screen_index, screens, grid_weight):
    facets = lax.axis_size("facet")
    subs = lax.axis_size("sub")
    rows = strips.shape[1]
    length = strips.shape[2] // 2
    chunks = length // LANES
    count = subgrid_offset.shape[0]
    span = grid_weight.shape[1]
    kinds = screens.shape[0]
    hbm = pl.BlockSpec(memory_space=pl.ANY)
    vmem = pl.BlockSpec(memory_space=pltpu.VMEM)
    limit = pltpu.CompilerParams(vmem_limit_bytes=32 * 1024 * 1024)
    shaped = jax.ShapeDtypeStruct

    subgrid_offset, facet_offset, owner, screen_index = [
        pltpu.with_memory_space_constraint(x, pltpu.HBM) for x in (subgrid_offset, facet_offset, owner, screen_index)
    ]

    def swap(x, step):
        return lax.ppermute(x, "facet", [(i, i ^ step) for i in range(facets)])

    def cost(flops):
        return pl.CostEstimate(flops=flops, bytes_accessed=1 << 20, transcendentals=0)

    turn, fwd = pl.pallas_call(
        functools.partial(table_kernel, length),
        out_shape=[shaped((2 * LANES, LANES), F32), shaped((2 * chunks, 4 * chunks), BF)],
        out_specs=[vmem] * 2,
        compiler_params=limit,
        cost_estimate=cost(10**11),
    )()
    held = grid_weight
    steps = [1 << n for n in range(subs.bit_length() - 1)]
    for step in steps:
        last, beside = held, lax.ppermute(held, "sub", [(k, k ^ step) for k in range(subs)])
        if step == steps[0]:
            windows, shift = pl.pallas_call(
                forward_kernel,
                out_shape=[shaped((count * rows, LANES), BF), shaped((2 * LANES, facets // 2 * LANES), BF)],
                in_specs=[hbm] * 2 + [vmem] * 3,
                out_specs=[vmem] * 2,
                scratch_shapes=[
                    pltpu.VMEM((rows * 2 * chunks, LANES), F32),
                    pltpu.VMEM((rows * LANES, 2 * LANES), BF),
                    pltpu.VMEM((rows * LANES, 2 * LANES), BF),
                    pltpu.SMEM((count,), jnp.int32),
                    pltpu.SMEM((facets,), jnp.int32),
                    pltpu.SemaphoreType.DMA((2,)),
                ],
                compiler_params=limit,
            )(subgrid_offset, facet_offset, strips, turn, fwd)
            passed = swap(windows, 1)
        if step != steps[-1]:
            beside = pl.pallas_call(
                join_kernel,
                out_shape=shaped((2 * held.shape[0], span), F32),
                in_specs=[vmem] * 2,
                out_specs=vmem,
                compiler_params=limit,
            )(held, beside)
        held, _ = lax.optimization_barrier((beside, windows))

    tall = max(rows, 16)
    cos, sin, both, other, shown, *ready = pl.pallas_call(
        functools.partial(prepare_kernel, subs, length),
        out_shape=[
            shaped((count * rows, LANES), F32),
            shaped((count * rows, LANES), F32),
            shaped((span, LANES), BF),
            shaped((span, LANES), BF),
            shaped((span, (facets // 2 - 2) * LANES), BF),
            shaped((count, facets * subs * CAP), BF),
            shaped((count, LANES), jnp.int32),
            shaped((2 * M, 4 * count), BF),
            shaped((4 * chunks, 2 * LANES), BF),
        ],
        in_specs=[hbm] * 5 + [vmem],
        out_specs=[vmem] * 9,
        scratch_shapes=[
            pltpu.VMEM((kinds * tall, LANES), F32),
            pltpu.VMEM((kinds * tall, LANES), F32),
            pltpu.SMEM((count,), jnp.int32),
            pltpu.SMEM((facets,), jnp.int32),
            pltpu.SMEM((count,), jnp.int32),
            pltpu.SMEM((count,), jnp.int32),
            pltpu.SemaphoreType.DMA((4,)),
        ],
        compiler_params=limit,
        cost_estimate=cost(2 * 10**10),
    )(subgrid_offset, facet_offset, screen_index, owner, last, screens)

    others = facets // 2 - 1
    shift, _ = lax.optimization_barrier((shift, both))
    own, *merged = pl.pallas_call(
        merge_kernel,
        out_shape=[shaped(windows.shape, F32)] + [shaped(windows.shape, BF)] * others,
        in_specs=[vmem] * 3,
        out_specs=[vmem] * (1 + others),
        compiler_params=limit,
    )(windows, passed, shift)
    size = subs * grid_weight.size // LANES
    laid, payload = pl.pallas_call(
        pack_kernel,
        out_shape=[shaped((size, LANES), BF), shaped((count * rows + size, LANES), BF)],
        in_specs=[vmem] * 3,
        out_specs=[vmem] * 2,
        compiler_params=limit,
    )(merged[-1], last, beside)

    far = swap(payload, facets - 2)
    laid_other = swap(laid, 1)
    parts = others - 1
    payloads = pl.pallas_call(
        functools.partial(attach_kernel, parts),
        out_shape=[shaped((count * rows + 2 * subs * CAP, LANES), BF)] * parts,
        in_specs=[vmem] * (parts + 3),
        out_specs=[vmem] * parts,
        compiler_params=limit,
    )(*merged[:-1], laid, laid_other, shown)
    arrived = [swap(block, 2 * n + 2) for n, block in enumerate(payloads)]
    tail, here, total = pl.pallas_call(
        first_kernel,
        out_shape=[
            shaped((subs * CAP, LANES), BF),
            shaped((3 * subs * CAP, LANES), BF),
            shaped(windows.shape, F32),
        ],
        in_specs=[vmem] * 6,
        out_specs=[vmem] * 3,
        compiler_params=limit,
    )(own, far, laid, laid_other, both, other)
    late = swap(tail, 1)

    return pl.pallas_call(
        backward_kernel,
        out_shape=shaped((1, rows, 2 * length), F32),
        in_specs=[vmem] * (parts + 10),
        out_specs=hbm,
        scratch_shapes=[
            pltpu.VMEM((2 * chunks * rows, LANES), F32),
            pltpu.VMEM((rows, 2 * length), F32),
            pltpu.SemaphoreType.DMA((4,)),
        ],
        compiler_params=limit,
    )(total, *arrived, here, late, cos, sin, *ready, turn)


def solution(mesh):
    in_specs = (P("facet", "sub", None), P(), P(), P(), P(), P(), P(("facet", "sub"), None))
    out_specs = P("facet", "sub", None)
    return jax.shard_map(local, mesh=mesh, in_specs=in_specs, out_specs=out_specs, check_vma=False)
```

```python
import functools
import math

import jax
import jax.numpy as jnp
from jax import lax
from jax.experimental import pallas as pl
from jax.experimental.pallas import tpu as pltpu
from jax.sharding import PartitionSpec as P

M = 64
CAP = 4
LANES = 128

BF = jnp.bfloat16
F32 = jnp.float32


def dot(x, y):
    return jnp.dot(x, y, preferred_element_type=F32)


def dot_t(x, y):
    return lax.dot_general(x, y, (((1,), (1,)), ((), ())), preferred_element_type=F32)


def iota(shape, dim):
    return lax.broadcasted_iota(jnp.int32, shape, dim)


def sine(r):
    x = r * (2 * math.pi)
    y = x * x
    total = -1 / math.factorial(11)
    for n in (9, 7, 5, 3, 1):
        total = total * y + (-1) ** (n // 2) / math.factorial(n)
    return x * total


def circle(index, period):
    r = (index & (period - 1)).astype(F32) * (1 / period) - 0.5
    near = jnp.maximum(jnp.minimum(-r, 0.5 + r), r - 0.5)
    return sine(jnp.abs(r) - 0.25), sine(near)


def high_low(x, low):
    high = x.astype(BF).astype(F32)
    return jnp.where(low, x - high, high).astype(BF)


def column(values, width):
    groups = []
    row = iota((8, width), 0)
    for group in range(len(values) // 8):
        value = jnp.zeros((8, width), jnp.int32)
        for r in range(8):
            value = jnp.where(row == r, values[group * 8 + r], value)
        groups.append(value)
    return jnp.concatenate(groups, axis=0)


def start_of(mine, sub_ref, off_ref, j, length):
    return (sub_ref[j] + off_ref[mine]) & (length - 1)


def table_kernel(length, turn_ref, fwd_ref):
    cos, sin = circle(iota((LANES, LANES), 0) * iota((LANES, LANES), 1), length)
    turn_ref[:LANES, :] = cos
    turn_ref[LANES:, :] = sin

    chunks = length // LANES
    shape = (2 * chunks, 4 * chunks)
    row, lane = iota(shape, 0), iota(shape, 1)
    cos, sin = circle((row & (chunks - 1)) * (lane & (chunks - 1)), chunks)
    row_im, lane_im = row // chunks, lane // chunks % 2
    table = jnp.where(row_im == lane_im, cos, jnp.where(row_im == 0, sin, -sin))
    fwd_ref[...] = high_low(table, lane >= 2 * chunks)


def join_kernel(first_ref, second_ref, out_ref):
    out_ref[: first_ref.shape[0], :] = first_ref[...]
    out_ref[first_ref.shape[0] :, :] = second_ref[...]


def merge_kernel(windows_ref, passed_ref, shift_ref, own_ref, *out_refs):
    both = jnp.concatenate([windows_ref[...], passed_ref[...]], axis=1)
    merged = dot(both, shift_ref[...])
    own_ref[...] = merged[:, :LANES]
    for n, out_ref in enumerate(out_refs):
        out_ref[...] = merged[:, (n + 1) * LANES : (n + 2) * LANES].astype(BF)


def pack_kernel(merged_ref, first_ref, second_ref, laid_ref, out_ref):
    held = jnp.concatenate([first_ref[...], second_ref[...]], axis=0)
    laid = jnp.concatenate([held[:, c : c + LANES] for c in range(0, held.shape[1], LANES)], axis=0).astype(BF)
    laid_ref[...] = laid
    out_ref[: merged_ref.shape[0], :] = merged_ref[...]
    out_ref[merged_ref.shape[0] :, :] = laid


def cut(blocks, hits):
    chunks = hits.shape[0] // LANES
    rows = []
    for block in blocks:
        size = block.shape[0] // chunks
        rows.append(jnp.concatenate([block[c * size : (c + 1) * size] for c in range(chunks)], axis=1))
    return dot(jnp.concatenate(rows, axis=0), hits).astype(BF)


def attach_kernel(parts, *refs):
    merged_refs, (laid_ref, passed_ref, shown_ref), out_refs = refs[:parts], refs[parts : parts + 3], refs[parts + 3 :]
    rows = cut([laid_ref[...], passed_ref[...]], shown_ref[...])
    for n in range(parts):
        windows = merged_refs[n].shape[0]
        out_refs[n][:windows, :] = merged_refs[n][...]
        out_refs[n][windows:, :] = rows[:, n * LANES : (n + 1) * LANES]


def scalars(pairs, sems):
    copies = [pltpu.make_async_copy(a, b, sems.at[n]) for n, (a, b) in enumerate(pairs)]
    for copy in copies:
        copy.start()
    return copies


def forward_kernel(
    sub_hbm,
    off_hbm,
    strips_ref,
    turn_ref,
    fwd_ref,
    out_ref,
    shift_ref,
    in_scr,
    mid_scr,
    low_scr,
    sub_ref,
    off_ref,
    sems,
):
    copies = scalars([(sub_hbm, sub_ref), (off_hbm, off_ref)], sems)
    mine = lax.axis_index("facet")
    rows = strips_ref.shape[1]
    length = strips_ref.shape[2] // 2
    chunks = length // LANES
    count = sub_ref.shape[0]

    for c in range(2 * chunks):
        piece = strips_ref[0, :, c * LANES : (c + 1) * LANES].astype(F32)
        in_scr[pl.ds(c, rows, stride=2 * chunks), :] = piece
    points = jnp.concatenate(
        [in_scr[r * 2 * chunks : (r + 1) * 2 * chunks, :].astype(BF) for r in range(rows)], axis=1
    )
    inner = dot(fwd_ref[...], jnp.concatenate([points, points], axis=0))
    for r in range(rows):
        re = inner[:chunks, r * LANES : (r + 1) * LANES]
        im = inner[chunks:, r * LANES : (r + 1) * LANES]
        for q in range(LANES // chunks):
            cos = turn_ref[q * chunks : (q + 1) * chunks, :]
            sin = turn_ref[LANES + q * chunks : LANES + (q + 1) * chunks, :]
            at = r * LANES + q * chunks
            for lanes, value in ((slice(0, LANES), re * cos + im * sin), (slice(LANES, 2 * LANES), im * cos - re * sin)):
                high = value.astype(BF)
                mid_scr[at : at + chunks, lanes] = high
                low_scr[at : at + chunks, lanes] = (value - high.astype(F32)).astype(BF)

    for copy in copies:
        copy.wait()
    shape = (LANES, LANES)
    row = iota(shape, 0)
    lane = iota(shape, 1)
    apart = (lane // M - row // M) * 8192 + (lane % M - row % M)
    for n in range(shift_ref.shape[1] // LANES):
        for core in range(2):
            delta = off_ref[mine ^ core] - off_ref[mine ^ (2 * n)]
            rows_here = slice(core * LANES, (core + 1) * LANES)
            shift_ref[rows_here, n * LANES : (n + 1) * LANES] = jnp.where(apart == delta, 1.0, 0.0).astype(BF)

    starts = column([start_of(mine, sub_ref, off_ref, j, length) for j in range(count)], LANES)
    block = starts >> (M.bit_length() - 1)
    cos, sin = circle(block * iota((count, LANES), 1), length // M)
    scale = 1 / math.sqrt(length)
    cos, sin = cos * scale, sin * scale
    coarse = jnp.concatenate(
        [jnp.concatenate([cos, sin], axis=1), jnp.concatenate([-sin, cos], axis=1)], axis=0
    )
    coarse = jnp.concatenate([high_low(coarse, False), high_low(coarse, True)], axis=0)
    window = dot_t(coarse, mid_scr[...])
    window = window[: 2 * count] + window[2 * count :] + dot_t(coarse[: 2 * count], low_scr[...])
    lane = iota((count, LANES), 1)
    taken = (lane + (starts & (M - 1))) & (LANES - 1)
    for r in range(rows):
        re = window[:count, r * LANES : (r + 1) * LANES]
        im = window[count:, r * LANES : (r + 1) * LANES]
        re = jnp.take_along_axis(re, taken, axis=1)
        im = jnp.take_along_axis(im, taken ^ M, axis=1)
        out_ref[r * count : (r + 1) * count, :] = jnp.where(lane < M, re, im).astype(BF)


def prepare_kernel(
    subs,
    length,
    sub_hbm,
    off_hbm,
    kind_hbm,
    owner_hbm,
    after_ref,
    screens_ref,
    cos_ref,
    sin_ref,
    both_ref,
    other_ref,
    shown_ref,
    rank_ref,
    gather_ref,
    coarse_ref,
    inv_ref,
    cos_scr,
    sin_scr,
    sub_ref,
    off_ref,
    kind_ref,
    owner_ref,
    sems,
):
    pairs = [(sub_hbm, sub_ref), (off_hbm, off_ref), (kind_hbm, kind_ref), (owner_hbm, owner_ref)]
    copies = scalars(pairs, sems)
    chunks = length // LANES
    mine = lax.axis_index("facet")
    count = kind_ref.shape[0]
    rows = cos_ref.shape[0] // count
    span = screens_ref.shape[2] // 2
    my_sub = lax.axis_index("sub")
    shape = (span, LANES)
    lane = iota(shape, 1)
    apart = iota(shape, 0) - lane % M
    sign = jnp.where(lane < M, -1.0, 1.0)

    shape = (chunks, LANES)
    cos, sin = circle(iota(shape, 0) * iota(shape, 1), chunks)
    table = jnp.concatenate(
        [jnp.concatenate([cos, -sin], axis=1), jnp.concatenate([sin, cos], axis=1)], axis=0
    )
    inv_ref[: 2 * chunks, :] = high_low(table, False)
    inv_ref[2 * chunks :, :] = high_low(table, True)

    for copy in copies:
        copy.wait()
    hit = apart == off_ref[mine]
    both = jnp.where(hit, 1.0, 0.0).astype(BF)
    signed = jnp.where(hit, sign, 0.0).astype(BF)
    kinds = screens_ref.shape[0]
    tall = cos_scr.shape[0] // kinds
    first = my_sub * rows // tall * tall
    block = pl.ds(pl.multiple_of(first, tall), tall)
    cosines = screens_ref[:, block, :span].reshape(kinds * tall, span)
    sines = screens_ref[:, block, span:].reshape(kinds * tall, span)
    both_ref[...] = both
    other_ref[...] = jnp.where(apart == off_ref[mine ^ 1], 1.0, 0.0).astype(BF)
    for n in range(shown_ref.shape[1] // LANES):
        hit = apart == off_ref[mine ^ (2 * n + 2)]
        shown_ref[:, n * LANES : (n + 1) * LANES] = jnp.where(hit, 1.0, 0.0).astype(BF)
    cos_scr[...] = dot(cosines, both)
    sin_scr[...] = dot(sines, signed)
    for j in range(count):
        kind = pl.multiple_of(kind_ref[j] * tall + my_sub * rows - first, rows)
        cos_ref[pl.ds(j, rows, stride=count), :] = cos_scr[pl.ds(kind, rows), :]
        sin_ref[pl.ds(j, rows, stride=count), :] = sin_scr[pl.ds(kind, rows), :]

    owners = [owner_ref[j] for j in range(count)]
    lane = iota((8, LANES), 1)
    wide = []
    for first in range(0, count, LANES):
        value = jnp.full((8, LANES), -1, jnp.int32)
        for j in range(first, min(first + LANES, count)):
            value = jnp.where(lane == j - first, owners[j], value)
        wide.append(value)
    tall_owner = column(owners, LANES)
    slot = jnp.zeros((count, 1), F32)
    for n, value in enumerate(wide):
        same = jnp.concatenate([value] * (count // 8), axis=0) == tall_owner
        earlier = iota((count, LANES), 1) + n * LANES < iota((count, LANES), 0)
        slot = slot + jnp.sum(jnp.where(same & earlier, 1.0, 0.0), axis=1, keepdims=True)
    bits = subs.bit_length() - 1
    facet_step = (tall_owner >> bits) ^ mine
    sub_step = (tall_owner & (subs - 1)) ^ my_sub
    facets = off_ref.shape[0]
    block = jnp.where(facet_step < 2, facet_step, facet_step + 1)
    block = jnp.where(facet_step == facets - 2, 2, block)
    block = jnp.where(facet_step == facets - 1, facets - 1, block)
    place = (block * subs + sub_step) * CAP + slot.astype(jnp.int32)
    for at in range(0, rank_ref.shape[1], LANES):
        hit = iota((count, LANES), 1) + at == place
        rank_ref[:, at : at + LANES] = jnp.where(hit, 1.0, 0.0).astype(BF)

    starts = [start_of(mine, sub_ref, off_ref, j, length) for j in range(count)]
    gather_ref[...] = (iota((count, LANES), 1) - (column(starts, LANES) & (M - 1))) & (LANES - 1)

    lane = iota((8, 4 * count), 1)
    block = jnp.zeros((8, 4 * count), jnp.int32)
    for j in range(count):
        block = jnp.where(lane % count == j, starts[j] // M, block)
    block = jnp.concatenate([block] * (M // 8), axis=0)
    shape = (M, 4 * count)
    lane = iota(shape, 1)
    cos, sin = circle(block * iota(shape, 0), length // M)
    scale = 1 / math.sqrt(length)
    cos, sin = cos * scale, sin * scale
    lane_im = lane // count % 2 == 1
    low = lane >= 2 * count
    coarse_ref[:M, :] = high_low(jnp.where(lane_im, -sin, cos), low)
    coarse_ref[M:, :] = high_low(jnp.where(lane_im, cos, sin), low)


def first_kernel(own_ref, block_ref, laid_ref, passed_ref, hits_ref, other_ref, tail_ref, cut_ref, total_ref):
    windows = own_ref.shape[0]
    rows = block_ref[windows:, :]
    tail_ref[...] = cut([rows], other_ref[...])
    cut_ref[...] = cut([laid_ref[...], passed_ref[...], rows], hits_ref[...])
    total_ref[...] = own_ref[...] + block_ref[:windows, :].astype(F32)


def backward_kernel(total_ref, *refs):
    arrived, refs = refs[:-13][::-1], refs[-13:]
    cut_ref, late_ref, cos_ref, sin_ref = refs[:4]
    rank_ref, gather_ref, coarse_ref, inv_ref, turn_ref, out_hbm, out_scr, flat_scr, out_sems = refs[4:]
    rows = out_hbm.shape[1]
    length = out_hbm.shape[2] // 2
    chunks = length // LANES
    windows = total_ref.shape[0]
    count = windows // rows

    cuts = [cut_ref[...]] + [ref[windows:, :] for ref in arrived] + [late_ref[...]]
    weights = dot(rank_ref[...], jnp.concatenate(cuts, axis=0))

    place = gather_ref[...]
    inside = place < M
    blocks = []
    for r in range(rows):
        here = slice(r * count, (r + 1) * count)
        total = total_ref[here, :]
        for ref in arrived:
            total = total + ref[here, :].astype(F32)
        value = (total * cos_ref[here, :] + pltpu.roll(total, M, 1) * sin_ref[here, :]) * weights
        value = value.astype(BF).astype(F32)
        re = jnp.where(inside, jnp.take_along_axis(value, place, axis=1), 0.0)
        im = jnp.where(inside, jnp.take_along_axis(value, place ^ M, axis=1), 0.0)
        blocks.append(jnp.concatenate([re, im], axis=0).astype(BF))
    spread = jnp.concatenate(blocks, axis=1)
    inner = dot(coarse_ref[...], jnp.concatenate([spread, spread], axis=0))
    twisted = []
    for r in range(rows):
        re = inner[:M, r * LANES : (r + 1) * LANES]
        im = inner[M:, r * LANES : (r + 1) * LANES]
        for q in range(LANES // M):
            cos = turn_ref[q * M : (q + 1) * M, :]
            sin = turn_ref[LANES + q * M : LANES + (q + 1) * M, :]
            both = jnp.concatenate([re * cos - im * sin, re * sin + im * cos], axis=1)
            twisted.append(both.astype(BF))
    twisted = jnp.concatenate(twisted, axis=0)
    points = dot_t(inv_ref[...], twisted)
    points = points[: 2 * chunks] + points[2 * chunks :]
    for r in range(rows):
        out_scr[pl.ds(r, 2 * chunks, stride=rows), :] = points[:, r * LANES : (r + 1) * LANES]
    parts = out_sems.shape[0]
    width = 2 * length // parts
    copies = []
    for p in range(parts):
        for c in range(p * width // LANES, (p + 1) * width // LANES):
            flat_scr[:, c * LANES : (c + 1) * LANES] = out_scr[c * rows : (c + 1) * rows, :]
        part = pl.ds(p * width, width)
        copies.append(pltpu.make_async_copy(flat_scr.at[:, part], out_hbm.at[0, :, part], out_sems.at[p]))
        copies[-1].start()
    for copy in copies:
        copy.wait()


def local(strips, facet_offset, subgrid_offset, owner, screen_index, screens, grid_weight):
    facets = lax.axis_size("facet")
    subs = lax.axis_size("sub")
    rows = strips.shape[1]
    length = strips.shape[2] // 2
    chunks = length // LANES
    count = subgrid_offset.shape[0]
    span = grid_weight.shape[1]
    kinds = screens.shape[0]
    hbm = pl.BlockSpec(memory_space=pl.ANY)
    vmem = pl.BlockSpec(memory_space=pltpu.VMEM)
    limit = pltpu.CompilerParams(vmem_limit_bytes=32 * 1024 * 1024)
    shaped = jax.ShapeDtypeStruct

    subgrid_offset, facet_offset, owner, screen_index = [
        pltpu.with_memory_space_constraint(x, pltpu.HBM) for x in (subgrid_offset, facet_offset, owner, screen_index)
    ]

    def swap(x, step):
        return lax.ppermute(x, "facet", [(i, i ^ step) for i in range(facets)])

    def cost(flops):
        return pl.CostEstimate(flops=flops, bytes_accessed=1 << 20, transcendentals=0)

    turn, fwd = pl.pallas_call(
        functools.partial(table_kernel, length),
        out_shape=[shaped((2 * LANES, LANES), F32), shaped((2 * chunks, 4 * chunks), BF)],
        out_specs=[vmem] * 2,
        compiler_params=limit,
        cost_estimate=cost(10**11),
    )()
    held = grid_weight
    steps = [1 << n for n in range(subs.bit_length() - 1)]
    for step in steps:
        last, beside = held, lax.ppermute(held, "sub", [(k, k ^ step) for k in range(subs)])
        if step == steps[0]:
            windows, shift = pl.pallas_call(
                forward_kernel,
                out_shape=[shaped((count * rows, LANES), BF), shaped((2 * LANES, facets // 2 * LANES), BF)],
                in_specs=[hbm] * 2 + [vmem] * 3,
                out_specs=[vmem] * 2,
                scratch_shapes=[
                    pltpu.VMEM((rows * 2 * chunks, LANES), F32),
                    pltpu.VMEM((rows * LANES, 2 * LANES), BF),
                    pltpu.VMEM((rows * LANES, 2 * LANES), BF),
                    pltpu.SMEM((count,), jnp.int32),
                    pltpu.SMEM((facets,), jnp.int32),
                    pltpu.SemaphoreType.DMA((2,)),
                ],
                compiler_params=limit,
            )(subgrid_offset, facet_offset, strips, turn, fwd)
            passed = swap(windows, 1)
        if step != steps[-1]:
            beside = pl.pallas_call(
                join_kernel,
                out_shape=shaped((2 * held.shape[0], span), F32),
                in_specs=[vmem] * 2,
                out_specs=vmem,
                compiler_params=limit,
            )(held, beside)
        held, _ = lax.optimization_barrier((beside, windows))

    tall = max(rows, 16)
    cos, sin, both, other, shown, *ready = pl.pallas_call(
        functools.partial(prepare_kernel, subs, length),
        out_shape=[
            shaped((count * rows, LANES), F32),
            shaped((count * rows, LANES), F32),
            shaped((span, LANES), BF),
            shaped((span, LANES), BF),
            shaped((span, (facets // 2 - 2) * LANES), BF),
            shaped((count, facets * subs * CAP), BF),
            shaped((count, LANES), jnp.int32),
            shaped((2 * M, 4 * count), BF),
            shaped((4 * chunks, 2 * LANES), BF),
        ],
        in_specs=[hbm] * 5 + [vmem],
        out_specs=[vmem] * 9,
        scratch_shapes=[
            pltpu.VMEM((kinds * tall, LANES), F32),
            pltpu.VMEM((kinds * tall, LANES), F32),
            pltpu.SMEM((count,), jnp.int32),
            pltpu.SMEM((facets,), jnp.int32),
            pltpu.SMEM((count,), jnp.int32),
            pltpu.SMEM((count,), jnp.int32),
            pltpu.SemaphoreType.DMA((4,)),
        ],
        compiler_params=limit,
        cost_estimate=cost(2 * 10**10),
    )(subgrid_offset, facet_offset, screen_index, owner, last, screens)

    others = facets // 2 - 1
    shift, _ = lax.optimization_barrier((shift, both))
    own, *merged = pl.pallas_call(
        merge_kernel,
        out_shape=[shaped(windows.shape, F32)] + [shaped(windows.shape, BF)] * others,
        in_specs=[vmem] * 3,
        out_specs=[vmem] * (1 + others),
        compiler_params=limit,
    )(windows, passed, shift)
    size = subs * grid_weight.size // LANES
    laid, payload = pl.pallas_call(
        pack_kernel,
        out_shape=[shaped((size, LANES), BF), shaped((count * rows + size, LANES), BF)],
        in_specs=[vmem] * 3,
        out_specs=[vmem] * 2,
        compiler_params=limit,
    )(merged[-1], last, beside)

    far = swap(payload, facets - 2)
    laid_other = swap(laid, 1)
    parts = others - 1
    payloads = pl.pallas_call(
        functools.partial(attach_kernel, parts),
        out_shape=[shaped((count * rows + 2 * subs * CAP, LANES), BF)] * parts,
        in_specs=[vmem] * (parts + 3),
        out_specs=[vmem] * parts,
        compiler_params=limit,
    )(*merged[:-1], laid, laid_other, shown)
    arrived = [swap(block, 2 * n + 2) for n, block in enumerate(payloads)]
    tail, here, total = pl.pallas_call(
        first_kernel,
        out_shape=[
            shaped((subs * CAP, LANES), BF),
            shaped((3 * subs * CAP, LANES), BF),
            shaped(windows.shape, F32),
        ],
        in_specs=[vmem] * 6,
        out_specs=[vmem] * 3,
        compiler_params=limit,
    )(own, far, laid, laid_other, both, other)
    late = swap(tail, 1)

    return pl.pallas_call(
        backward_kernel,
        out_shape=shaped((1, rows, 2 * length), F32),
        in_specs=[vmem] * (parts + 10),
        out_specs=hbm,
        scratch_shapes=[
            pltpu.VMEM((2 * chunks * rows, LANES), F32),
            pltpu.VMEM((rows, 2 * length), F32),
            pltpu.SemaphoreType.DMA((4,)),
        ],
        compiler_params=limit,
    )(total, *arrived[::-1], here, late, cos, sin, *ready, turn)


def solution(mesh):
    in_specs = (P("facet", "sub", None), P(), P(), P(), P(), P(), P(("facet", "sub"), None))
    out_specs = P("facet", "sub", None)
    return jax.shard_map(local, mesh=mesh, in_specs=in_specs, out_specs=out_specs, check_vma=False)
```

```python
import functools
import math

import jax
import jax.numpy as jnp
from jax import lax
from jax.experimental import pallas as pl
from jax.experimental.pallas import tpu as pltpu
from jax.sharding import PartitionSpec as P

M = 64
CAP = 4
LANES = 128

BF = jnp.bfloat16
F32 = jnp.float32


def dot(x, y):
    return jnp.dot(x, y, preferred_element_type=F32)


def dot_t(x, y):
    return lax.dot_general(x, y, (((1,), (1,)), ((), ())), preferred_element_type=F32)


def iota(shape, dim):
    return lax.broadcasted_iota(jnp.int32, shape, dim)


def sine(r):
    x = r * (2 * math.pi)
    y = x * x
    total = -1 / math.factorial(11)
    for n in (9, 7, 5, 3, 1):
        total = total * y + (-1) ** (n // 2) / math.factorial(n)
    return x * total


def circle(index, period):
    r = (index & (period - 1)).astype(F32) * (1 / period) - 0.5
    near = jnp.maximum(jnp.minimum(-r, 0.5 + r), r - 0.5)
    return sine(jnp.abs(r) - 0.25), sine(near)


def high_low(x, low):
    high = x.astype(BF).astype(F32)
    return jnp.where(low, x - high, high).astype(BF)


def column(values, width):
    groups = []
    row = iota((8, width), 0)
    for group in range(len(values) // 8):
        value = jnp.zeros((8, width), jnp.int32)
        for r in range(8):
            value = jnp.where(row == r, values[group * 8 + r], value)
        groups.append(value)
    return jnp.concatenate(groups, axis=0)


def start_of(mine, sub_ref, off_ref, j, length):
    return (sub_ref[j] + off_ref[mine]) & (length - 1)


def table_kernel(length, turn_ref, fwd_ref):
    cos, sin = circle(iota((LANES, LANES), 0) * iota((LANES, LANES), 1), length)
    turn_ref[:LANES, :] = cos
    turn_ref[LANES:, :] = sin

    chunks = length // LANES
    shape = (2 * chunks, 4 * chunks)
    row, lane = iota(shape, 0), iota(shape, 1)
    cos, sin = circle((row & (chunks - 1)) * (lane & (chunks - 1)), chunks)
    row_im, lane_im = row // chunks, lane // chunks % 2
    table = jnp.where(row_im == lane_im, cos, jnp.where(row_im == 0, sin, -sin))
    fwd_ref[...] = high_low(table, lane >= 2 * chunks)


def join_kernel(first_ref, second_ref, out_ref):
    out_ref[: first_ref.shape[0], :] = first_ref[...]
    out_ref[first_ref.shape[0] :, :] = second_ref[...]


def merge_kernel(windows_ref, passed_ref, shift_ref, own_ref, *out_refs):
    both = jnp.concatenate([windows_ref[...], passed_ref[...]], axis=1)
    merged = dot(both, shift_ref[...])
    own_ref[...] = merged[:, :LANES]
    for n, out_ref in enumerate(out_refs):
        out_ref[...] = merged[:, (n + 1) * LANES : (n + 2) * LANES].astype(BF)


def pack_kernel(merged_ref, first_ref, second_ref, laid_ref, out_ref):
    held = jnp.concatenate([first_ref[...], second_ref[...]], axis=0)
    laid = jnp.concatenate([held[:, c : c + LANES] for c in range(0, held.shape[1], LANES)], axis=0).astype(BF)
    laid_ref[...] = laid
    out_ref[: merged_ref.shape[0], :] = merged_ref[...]
    out_ref[merged_ref.shape[0] :, :] = laid


def cut(blocks, hits):
    chunks = hits.shape[0] // LANES
    rows = []
    for block in blocks:
        size = block.shape[0] // chunks
        rows.append(jnp.concatenate([block[c * size : (c + 1) * size] for c in range(chunks)], axis=1))
    return dot(jnp.concatenate(rows, axis=0), hits).astype(BF)


def attach_kernel(parts, *refs):
    merged_refs, (laid_ref, passed_ref, shown_ref), out_refs = refs[:parts], refs[parts : parts + 3], refs[parts + 3 :]
    rows = cut([laid_ref[...], passed_ref[...]], shown_ref[...])
    for n in range(parts):
        windows = merged_refs[n].shape[0]
        out_refs[n][:windows, :] = merged_refs[n][...]
        out_refs[n][windows:, :] = rows[:, n * LANES : (n + 1) * LANES]


def scalars(pairs, sems):
    copies = [pltpu.make_async_copy(a, b, sems.at[n]) for n, (a, b) in enumerate(pairs)]
    for copy in copies:
        copy.start()
    return copies


def forward_kernel(
    sub_hbm,
    off_hbm,
    strips_ref,
    turn_ref,
    fwd_ref,
    out_ref,
    shift_ref,
    in_scr,
    mid_scr,
    low_scr,
    sub_ref,
    off_ref,
    sems,
):
    copies = scalars([(sub_hbm, sub_ref), (off_hbm, off_ref)], sems)
    mine = lax.axis_index("facet")
    rows = strips_ref.shape[1]
    length = strips_ref.shape[2] // 2
    chunks = length // LANES
    count = sub_ref.shape[0]

    for c in range(2 * chunks):
        piece = strips_ref[0, :, c * LANES : (c + 1) * LANES].astype(F32)
        in_scr[pl.ds(c, rows, stride=2 * chunks), :] = piece
    points = jnp.concatenate(
        [in_scr[r * 2 * chunks : (r + 1) * 2 * chunks, :].astype(BF) for r in range(rows)], axis=1
    )
    inner = dot(fwd_ref[...], jnp.concatenate([points, points], axis=0))
    for r in range(rows):
        re = inner[:chunks, r * LANES : (r + 1) * LANES]
        im = inner[chunks:, r * LANES : (r + 1) * LANES]
        for q in range(LANES // chunks):
            cos = turn_ref[q * chunks : (q + 1) * chunks, :]
            sin = turn_ref[LANES + q * chunks : LANES + (q + 1) * chunks, :]
            at = r * LANES + q * chunks
            for lanes, value in ((slice(0, LANES), re * cos + im * sin), (slice(LANES, 2 * LANES), im * cos - re * sin)):
                high = value.astype(BF)
                mid_scr[at : at + chunks, lanes] = high
                low_scr[at : at + chunks, lanes] = (value - high.astype(F32)).astype(BF)

    for copy in copies:
        copy.wait()
    shape = (LANES, LANES)
    row = iota(shape, 0)
    lane = iota(shape, 1)
    apart = (lane // M - row // M) * 8192 + (lane % M - row % M)
    for n in range(shift_ref.shape[1] // LANES):
        for core in range(2):
            delta = off_ref[mine ^ core] - off_ref[mine ^ (2 * n)]
            rows_here = slice(core * LANES, (core + 1) * LANES)
            shift_ref[rows_here, n * LANES : (n + 1) * LANES] = jnp.where(apart == delta, 1.0, 0.0).astype(BF)

    starts = column([start_of(mine, sub_ref, off_ref, j, length) for j in range(count)], LANES)
    block = starts >> (M.bit_length() - 1)
    cos, sin = circle(block * iota((count, LANES), 1), length // M)
    scale = 1 / math.sqrt(length)
    cos, sin = cos * scale, sin * scale
    coarse = jnp.concatenate(
        [jnp.concatenate([cos, sin], axis=1), jnp.concatenate([-sin, cos], axis=1)], axis=0
    )
    coarse = jnp.concatenate([high_low(coarse, False), high_low(coarse, True)], axis=0)
    window = dot_t(coarse, mid_scr[...])
    window = window[: 2 * count] + window[2 * count :] + dot_t(coarse[: 2 * count], low_scr[...])
    lane = iota((count, LANES), 1)
    taken = (lane + (starts & (M - 1))) & (LANES - 1)
    for r in range(rows):
        re = window[:count, r * LANES : (r + 1) * LANES]
        im = window[count:, r * LANES : (r + 1) * LANES]
        re = jnp.take_along_axis(re, taken, axis=1)
        im = jnp.take_along_axis(im, taken ^ M, axis=1)
        out_ref[r * count : (r + 1) * count, :] = jnp.where(lane < M, re, im).astype(BF)


def prepare_kernel(
    subs,
    length,
    sub_hbm,
    off_hbm,
    kind_hbm,
    owner_hbm,
    after_ref,
    screens_ref,
    cos_ref,
    sin_ref,
    both_ref,
    other_ref,
    shown_ref,
    rank_ref,
    gather_ref,
    coarse_ref,
    inv_ref,
    cos_scr,
    sin_scr,
    sub_ref,
    off_ref,
    kind_ref,
    owner_ref,
    sems,
):
    pairs = [(sub_hbm, sub_ref), (off_hbm, off_ref), (kind_hbm, kind_ref), (owner_hbm, owner_ref)]
    copies = scalars(pairs, sems)
    chunks = length // LANES
    mine = lax.axis_index("facet")
    count = kind_ref.shape[0]
    rows = cos_ref.shape[0] // count
    span = screens_ref.shape[2] // 2
    my_sub = lax.axis_index("sub")
    shape = (span, LANES)
    lane = iota(shape, 1)
    apart = iota(shape, 0) - lane % M
    sign = jnp.where(lane < M, -1.0, 1.0)

    shape = (chunks, LANES)
    cos, sin = circle(iota(shape, 0) * iota(shape, 1), chunks)
    table = jnp.concatenate(
        [jnp.concatenate([cos, -sin], axis=1), jnp.concatenate([sin, cos], axis=1)], axis=0
    )
    inv_ref[: 2 * chunks, :] = high_low(table, False)
    inv_ref[2 * chunks :, :] = high_low(table, True)

    for copy in copies:
        copy.wait()
    hit = apart == off_ref[mine]
    both = jnp.where(hit, 1.0, 0.0).astype(BF)
    signed = jnp.where(hit, sign, 0.0).astype(BF)
    kinds = screens_ref.shape[0]
    tall = cos_scr.shape[0] // kinds
    first = my_sub * rows // tall * tall
    block = pl.ds(pl.multiple_of(first, tall), tall)
    cosines = screens_ref[:, block, :span].reshape(kinds * tall, span)
    sines = screens_ref[:, block, span:].reshape(kinds * tall, span)
    both_ref[...] = both
    other_ref[...] = jnp.where(apart == off_ref[mine ^ 1], 1.0, 0.0).astype(BF)
    for n in range(shown_ref.shape[1] // LANES):
        hit = apart == off_ref[mine ^ (2 * n + 2)]
        shown_ref[:, n * LANES : (n + 1) * LANES] = jnp.where(hit, 1.0, 0.0).astype(BF)
    cos_scr[...] = dot(cosines, both)
    sin_scr[...] = dot(sines, signed)
    for j in range(count):
        kind = pl.multiple_of(kind_ref[j] * tall + my_sub * rows - first, rows)
        cos_ref[pl.ds(j, rows, stride=count), :] = cos_scr[pl.ds(kind, rows), :]
        sin_ref[pl.ds(j, rows, stride=count), :] = sin_scr[pl.ds(kind, rows), :]

    owners = [owner_ref[j] for j in range(count)]
    lane = iota((8, LANES), 1)
    wide = []
    for first in range(0, count, LANES):
        value = jnp.full((8, LANES), -1, jnp.int32)
        for j in range(first, min(first + LANES, count)):
            value = jnp.where(lane == j - first, owners[j], value)
        wide.append(value)
    tall_owner = column(owners, LANES)
    slot = jnp.zeros((count, 1), F32)
    for n, value in enumerate(wide):
        same = jnp.concatenate([value] * (count // 8), axis=0) == tall_owner
        earlier = iota((count, LANES), 1) + n * LANES < iota((count, LANES), 0)
        slot = slot + jnp.sum(jnp.where(same & earlier, 1.0, 0.0), axis=1, keepdims=True)
    bits = subs.bit_length() - 1
    facet_step = (tall_owner >> bits) ^ mine
    sub_step = (tall_owner & (subs - 1)) ^ my_sub
    facets = off_ref.shape[0]
    block = jnp.where(facet_step < 2, facet_step, facet_step + 1)
    block = jnp.where(facet_step == facets - 2, 2, block)
    block = jnp.where(facet_step == facets - 1, facets - 1, block)
    place = (block * subs + sub_step) * CAP + slot.astype(jnp.int32)
    for at in range(0, rank_ref.shape[1], LANES):
        hit = iota((count, LANES), 1) + at == place
        rank_ref[:, at : at + LANES] = jnp.where(hit, 1.0, 0.0).astype(BF)

    starts = [start_of(mine, sub_ref, off_ref, j, length) for j in range(count)]
    gather_ref[...] = (iota((count, LANES), 1) - (column(starts, LANES) & (M - 1))) & (LANES - 1)

    lane = iota((8, 4 * count), 1)
    block = jnp.zeros((8, 4 * count), jnp.int32)
    for j in range(count):
        block = jnp.where(lane % count == j, starts[j] // M, block)
    block = jnp.concatenate([block] * (M // 8), axis=0)
    shape = (M, 4 * count)
    lane = iota(shape, 1)
    cos, sin = circle(block * iota(shape, 0), length // M)
    scale = 1 / math.sqrt(length)
    cos, sin = cos * scale, sin * scale
    lane_im = lane // count % 2 == 1
    low = lane >= 2 * count
    coarse_ref[:M, :] = high_low(jnp.where(lane_im, -sin, cos), low)
    coarse_ref[M:, :] = high_low(jnp.where(lane_im, cos, sin), low)


def first_kernel(own_ref, block_ref, laid_ref, passed_ref, hits_ref, other_ref, tail_ref, cut_ref, total_ref):
    windows = own_ref.shape[0]
    rows = block_ref[windows:, :]
    tail_ref[...] = cut([rows], other_ref[...])
    cut_ref[...] = cut([laid_ref[...], passed_ref[...], rows], hits_ref[...])
    total_ref[...] = own_ref[...] + block_ref[:windows, :].astype(F32)


def backward_kernel(total_ref, *refs):
    arrived, refs = refs[:-13][::-1], refs[-13:]
    cut_ref, late_ref, cos_ref, sin_ref = refs[:4]
    rank_ref, gather_ref, coarse_ref, inv_ref, turn_ref, out_hbm, out_scr, flat_scr, out_sems = refs[4:]
    rows = out_hbm.shape[1]
    length = out_hbm.shape[2] // 2
    chunks = length // LANES
    windows = total_ref.shape[0]
    count = windows // rows

    cuts = [cut_ref[...]] + [ref[windows:, :] for ref in arrived] + [late_ref[...]]
    weights = dot(rank_ref[...], jnp.concatenate(cuts, axis=0))

    place = gather_ref[...]
    inside = place < M
    blocks = []
    for r in range(rows):
        here = slice(r * count, (r + 1) * count)
        total = total_ref[here, :]
        for ref in arrived:
            total = total + ref[here, :].astype(F32)
        value = (total * cos_ref[here, :] + pltpu.roll(total, M, 1) * sin_ref[here, :]) * weights
        value = value.astype(BF).astype(F32)
        re = jnp.where(inside, jnp.take_along_axis(value, place, axis=1), 0.0)
        im = jnp.where(inside, jnp.take_along_axis(value, place ^ M, axis=1), 0.0)
        blocks.append(jnp.concatenate([re, im], axis=0).astype(BF))
    spread = jnp.concatenate(blocks, axis=1)
    inner = dot(coarse_ref[...], jnp.concatenate([spread, spread], axis=0))
    twisted = []
    for r in range(rows):
        re = inner[:M, r * LANES : (r + 1) * LANES]
        im = inner[M:, r * LANES : (r + 1) * LANES]
        for q in range(LANES // M):
            cos = turn_ref[q * M : (q + 1) * M, :]
            sin = turn_ref[LANES + q * M : LANES + (q + 1) * M, :]
            both = jnp.concatenate([re * cos - im * sin, re * sin + im * cos], axis=1)
            twisted.append(both.astype(BF))
    twisted = jnp.concatenate(twisted, axis=0)
    points = dot_t(inv_ref[...], twisted)
    points = points[: 2 * chunks] + points[2 * chunks :]
    for r in range(rows):
        out_scr[pl.ds(r, 2 * chunks, stride=rows), :] = points[:, r * LANES : (r + 1) * LANES]
    parts = out_sems.shape[0]
    width = 2 * length // parts
    copies = []
    for p in range(parts):
        for c in range(p * width // LANES, (p + 1) * width // LANES):
            flat_scr[:, c * LANES : (c + 1) * LANES] = out_scr[c * rows : (c + 1) * rows, :]
        part = pl.ds(p * width, width)
        copies.append(pltpu.make_async_copy(flat_scr.at[:, part], out_hbm.at[0, :, part], out_sems.at[p]))
        copies[-1].start()
    for copy in copies:
        copy.wait()


def local(strips, facet_offset, subgrid_offset, owner, screen_index, screens, grid_weight):
    facets = lax.axis_size("facet")
    subs = lax.axis_size("sub")
    rows = strips.shape[1]
    length = strips.shape[2] // 2
    chunks = length // LANES
    count = subgrid_offset.shape[0]
    span = grid_weight.shape[1]
    kinds = screens.shape[0]
    hbm = pl.BlockSpec(memory_space=pl.ANY)
    vmem = pl.BlockSpec(memory_space=pltpu.VMEM)
    limit = pltpu.CompilerParams(vmem_limit_bytes=32 * 1024 * 1024)
    shaped = jax.ShapeDtypeStruct

    subgrid_offset, facet_offset, owner, screen_index = [
        pltpu.with_memory_space_constraint(x, pltpu.HBM) for x in (subgrid_offset, facet_offset, owner, screen_index)
    ]

    def swap(x, step):
        return lax.ppermute(x, "facet", [(i, i ^ step) for i in range(facets)])

    def cost(flops):
        return pl.CostEstimate(flops=flops, bytes_accessed=1 << 20, transcendentals=0)

    turn, fwd = pl.pallas_call(
        functools.partial(table_kernel, length),
        out_shape=[shaped((2 * LANES, LANES), F32), shaped((2 * chunks, 4 * chunks), BF)],
        out_specs=[vmem] * 2,
        compiler_params=limit,
        cost_estimate=cost(10**11),
    )()
    held = grid_weight
    steps = [1 << n for n in range(subs.bit_length() - 1)]
    for step in steps:
        last, beside = held, lax.ppermute(held, "sub", [(k, k ^ step) for k in range(subs)])
        if step == steps[0]:
            windows, shift = pl.pallas_call(
                forward_kernel,
                out_shape=[shaped((count * rows, LANES), BF), shaped((2 * LANES, facets // 2 * LANES), BF)],
                in_specs=[hbm] * 2 + [vmem] * 3,
                out_specs=[vmem] * 2,
                scratch_shapes=[
                    pltpu.VMEM((rows * 2 * chunks, LANES), F32),
                    pltpu.VMEM((rows * LANES, 2 * LANES), BF),
                    pltpu.VMEM((rows * LANES, 2 * LANES), BF),
                    pltpu.SMEM((count,), jnp.int32),
                    pltpu.SMEM((facets,), jnp.int32),
                    pltpu.SemaphoreType.DMA((2,)),
                ],
                compiler_params=limit,
            )(subgrid_offset, facet_offset, strips, turn, fwd)
            passed = swap(windows, 1)
        if step != steps[-1]:
            beside = pl.pallas_call(
                join_kernel,
                out_shape=shaped((2 * held.shape[0], span), F32),
                in_specs=[vmem] * 2,
                out_specs=vmem,
                compiler_params=limit,
            )(held, beside)
        held, _ = lax.optimization_barrier((beside, windows))

    tall = max(rows, 16)
    cos, sin, both, other, shown, *ready = pl.pallas_call(
        functools.partial(prepare_kernel, subs, length),
        out_shape=[
            shaped((count * rows, LANES), F32),
            shaped((count * rows, LANES), F32),
            shaped((span, LANES), BF),
            shaped((span, LANES), BF),
            shaped((span, (facets // 2 - 2) * LANES), BF),
            shaped((count, facets * subs * CAP), BF),
            shaped((count, LANES), jnp.int32),
            shaped((2 * M, 4 * count), BF),
            shaped((4 * chunks, 2 * LANES), BF),
        ],
        in_specs=[hbm] * 5 + [vmem],
        out_specs=[vmem] * 9,
        scratch_shapes=[
            pltpu.VMEM((kinds * tall, LANES), F32),
            pltpu.VMEM((kinds * tall, LANES), F32),
            pltpu.SMEM((count,), jnp.int32),
            pltpu.SMEM((facets,), jnp.int32),
            pltpu.SMEM((count,), jnp.int32),
            pltpu.SMEM((count,), jnp.int32),
            pltpu.SemaphoreType.DMA((4,)),
        ],
        compiler_params=limit,
        cost_estimate=cost(2 * 10**10),
    )(subgrid_offset, facet_offset, screen_index, owner, last, screens)

    others = facets // 2 - 1
    shift, _ = lax.optimization_barrier((shift, both))
    own, *merged = pl.pallas_call(
        merge_kernel,
        out_shape=[shaped(windows.shape, F32)] + [shaped(windows.shape, BF)] * others,
        in_specs=[vmem] * 3,
        out_specs=[vmem] * (1 + others),
        compiler_params=limit,
    )(windows, passed, shift)
    size = subs * grid_weight.size // LANES
    laid, payload = pl.pallas_call(
        pack_kernel,
        out_shape=[shaped((size, LANES), BF), shaped((count * rows + size, LANES), BF)],
        in_specs=[vmem] * 3,
        out_specs=[vmem] * 2,
        compiler_params=limit,
    )(merged[-1], last, beside)

    far = swap(payload, facets - 2)
    laid_other = swap(laid, 1)
    parts = others - 1
    payloads = pl.pallas_call(
        functools.partial(attach_kernel, parts),
        out_shape=[shaped((count * rows + 2 * subs * CAP, LANES), BF)] * parts,
        in_specs=[vmem] * (parts + 3),
        out_specs=[vmem] * parts,
        compiler_params=limit,
    )(*merged[:-1], laid, laid_other, shown)
    arrived = [swap(block, 2 * n + 2) for n, block in enumerate(payloads)]
    tail, here, total = pl.pallas_call(
        first_kernel,
        out_shape=[
            shaped((subs * CAP, LANES), BF),
            shaped((3 * subs * CAP, LANES), BF),
            shaped(windows.shape, F32),
        ],
        in_specs=[vmem] * 6,
        out_specs=[vmem] * 3,
        compiler_params=limit,
    )(own, far, laid, laid_other, both, other)
    late = swap(tail, 1)

    return pl.pallas_call(
        backward_kernel,
        out_shape=shaped((1, rows, 2 * length), F32),
        in_specs=[vmem] * (parts + 10),
        out_specs=hbm,
        scratch_shapes=[
            pltpu.VMEM((2 * chunks * rows, LANES), F32),
            pltpu.VMEM((rows, 2 * length), F32),
            pltpu.SemaphoreType.DMA((2,)),
        ],
        compiler_params=limit,
    )(total, *arrived[::-1], here, late, cos, sin, *ready, turn)


def solution(mesh):
    in_specs = (P("facet", "sub", None), P(), P(), P(), P(), P(), P(("facet", "sub"), None))
    out_specs = P("facet", "sub", None)
    return jax.shard_map(local, mesh=mesh, in_specs=in_specs, out_specs=out_specs, check_vma=False)
```

```python
import functools
import math

import jax
import jax.numpy as jnp
from jax import lax
from jax.experimental import pallas as pl
from jax.experimental.pallas import tpu as pltpu
from jax.sharding import PartitionSpec as P

M = 64
CAP = 4
LANES = 128

BF = jnp.bfloat16
F32 = jnp.float32


def dot(x, y):
    return jnp.dot(x, y, preferred_element_type=F32)


def dot_t(x, y):
    return lax.dot_general(x, y, (((1,), (1,)), ((), ())), preferred_element_type=F32)


def iota(shape, dim):
    return lax.broadcasted_iota(jnp.int32, shape, dim)


def sine(r):
    x = r * (2 * math.pi)
    y = x * x
    total = -1 / math.factorial(11)
    for n in (9, 7, 5, 3, 1):
        total = total * y + (-1) ** (n // 2) / math.factorial(n)
    return x * total


def circle(index, period):
    r = (index & (period - 1)).astype(F32) * (1 / period) - 0.5
    near = jnp.maximum(jnp.minimum(-r, 0.5 + r), r - 0.5)
    return sine(jnp.abs(r) - 0.25), sine(near)


def high_low(x, low):
    high = x.astype(BF).astype(F32)
    return jnp.where(low, x - high, high).astype(BF)


def column(values, width):
    groups = []
    row = iota((8, width), 0)
    for group in range(len(values) // 8):
        value = jnp.zeros((8, width), jnp.int32)
        for r in range(8):
            value = jnp.where(row == r, values[group * 8 + r], value)
        groups.append(value)
    return jnp.concatenate(groups, axis=0)


def start_of(mine, sub_ref, off_ref, j, length):
    return (sub_ref[j] + off_ref[mine]) & (length - 1)


def table_kernel(length, turn_ref, fwd_ref):
    cos, sin = circle(iota((LANES, LANES), 0) * iota((LANES, LANES), 1), length)
    turn_ref[:LANES, :] = cos
    turn_ref[LANES:, :] = sin

    chunks = length // LANES
    shape = (2 * chunks, 4 * chunks)
    row, lane = iota(shape, 0), iota(shape, 1)
    cos, sin = circle((row & (chunks - 1)) * (lane & (chunks - 1)), chunks)
    row_im, lane_im = row // chunks, lane // chunks % 2
    table = jnp.where(row_im == lane_im, cos, jnp.where(row_im == 0, sin, -sin))
    fwd_ref[...] = high_low(table, lane >= 2 * chunks)


def join_kernel(first_ref, second_ref, out_ref):
    out_ref[: first_ref.shape[0], :] = first_ref[...]
    out_ref[first_ref.shape[0] :, :] = second_ref[...]


def merge_kernel(windows_ref, passed_ref, shift_ref, own_ref, *out_refs):
    both = jnp.concatenate([windows_ref[...], passed_ref[...]], axis=1)
    merged = dot(both, shift_ref[...])
    own_ref[...] = merged[:, :LANES]
    for n, out_ref in enumerate(out_refs):
        out_ref[...] = merged[:, (n + 1) * LANES : (n + 2) * LANES].astype(BF)


def pack_kernel(merged_ref, first_ref, second_ref, laid_ref, out_ref):
    held = jnp.concatenate([first_ref[...], second_ref[...]], axis=0)
    laid = jnp.concatenate([held[:, c : c + LANES] for c in range(0, held.shape[1], LANES)], axis=0).astype(BF)
    laid_ref[...] = laid
    out_ref[: merged_ref.shape[0], :] = merged_ref[...]
    out_ref[merged_ref.shape[0] :, :] = laid


def cut(blocks, hits):
    chunks = hits.shape[0] // LANES
    rows = []
    for block in blocks:
        size = block.shape[0] // chunks
        rows.append(jnp.concatenate([block[c * size : (c + 1) * size] for c in range(chunks)], axis=1))
    return dot(jnp.concatenate(rows, axis=0), hits).astype(BF)


def attach_kernel(parts, *refs):
    merged_refs, (laid_ref, passed_ref, shown_ref), out_refs = refs[:parts], refs[parts : parts + 3], refs[parts + 3 :]
    rows = cut([laid_ref[...], passed_ref[...]], shown_ref[...])
    for n in range(parts):
        windows = merged_refs[n].shape[0]
        out_refs[n][:windows, :] = merged_refs[n][...]
        out_refs[n][windows:, :] = rows[:, n * LANES : (n + 1) * LANES]


def scalars(pairs, sems):
    copies = [pltpu.make_async_copy(a, b, sems.at[n]) for n, (a, b) in enumerate(pairs)]
    for copy in copies:
        copy.start()
    return copies


def forward_kernel(
    sub_hbm,
    off_hbm,
    strips_ref,
    turn_ref,
    fwd_ref,
    out_ref,
    shift_ref,
    in_scr,
    mid_scr,
    low_scr,
    sub_ref,
    off_ref,
    sems,
):
    copies = scalars([(sub_hbm, sub_ref), (off_hbm, off_ref)], sems)
    mine = lax.axis_index("facet")
    rows = strips_ref.shape[1]
    length = strips_ref.shape[2] // 2
    chunks = length // LANES
    count = sub_ref.shape[0]

    for c in range(2 * chunks):
        piece = strips_ref[0, :, c * LANES : (c + 1) * LANES].astype(F32)
        in_scr[pl.ds(c, rows, stride=2 * chunks), :] = piece
    points = jnp.concatenate(
        [in_scr[r * 2 * chunks : (r + 1) * 2 * chunks, :].astype(BF) for r in range(rows)], axis=1
    )
    inner = dot(fwd_ref[...], jnp.concatenate([points, points], axis=0))
    for r in range(rows):
        re = inner[:chunks, r * LANES : (r + 1) * LANES]
        im = inner[chunks:, r * LANES : (r + 1) * LANES]
        for q in range(LANES // chunks):
            cos = turn_ref[q * chunks : (q + 1) * chunks, :]
            sin = turn_ref[LANES + q * chunks : LANES + (q + 1) * chunks, :]
            at = r * LANES + q * chunks
            for lanes, value in ((slice(0, LANES), re * cos + im * sin), (slice(LANES, 2 * LANES), im * cos - re * sin)):
                high = value.astype(BF)
                mid_scr[at : at + chunks, lanes] = high
                low_scr[at : at + chunks, lanes] = (value - high.astype(F32)).astype(BF)

    for copy in copies:
        copy.wait()
    shape = (LANES, LANES)
    row = iota(shape, 0)
    lane = iota(shape, 1)
    apart = (lane // M - row // M) * 8192 + (lane % M - row % M)
    for n in range(shift_ref.shape[1] // LANES):
        for core in range(2):
            delta = off_ref[mine ^ core] - off_ref[mine ^ (2 * n)]
            rows_here = slice(core * LANES, (core + 1) * LANES)
            shift_ref[rows_here, n * LANES : (n + 1) * LANES] = jnp.where(apart == delta, 1.0, 0.0).astype(BF)

    starts = column([start_of(mine, sub_ref, off_ref, j, length) for j in range(count)], LANES)
    block = starts >> (M.bit_length() - 1)
    cos, sin = circle(block * iota((count, LANES), 1), length // M)
    scale = 1 / math.sqrt(length)
    cos, sin = cos * scale, sin * scale
    coarse = jnp.concatenate(
        [jnp.concatenate([cos, sin], axis=1), jnp.concatenate([-sin, cos], axis=1)], axis=0
    )
    coarse = jnp.concatenate([high_low(coarse, False), high_low(coarse, True)], axis=0)
    window = dot_t(coarse, mid_scr[...])
    window = window[: 2 * count] + window[2 * count :] + dot_t(coarse[: 2 * count], low_scr[...])
    lane = iota((count, LANES), 1)
    taken = (lane + (starts & (M - 1))) & (LANES - 1)
    for r in range(rows):
        re = window[:count, r * LANES : (r + 1) * LANES]
        im = window[count:, r * LANES : (r + 1) * LANES]
        re = jnp.take_along_axis(re, taken, axis=1)
        im = jnp.take_along_axis(im, taken ^ M, axis=1)
        out_ref[r * count : (r + 1) * count, :] = jnp.where(lane < M, re, im).astype(BF)


def prepare_kernel(
    subs,
    length,
    sub_hbm,
    off_hbm,
    kind_hbm,
    owner_hbm,
    after_ref,
    screens_ref,
    cos_ref,
    sin_ref,
    both_ref,
    other_ref,
    shown_ref,
    rank_ref,
    gather_ref,
    coarse_ref,
    inv_ref,
    cos_scr,
    sin_scr,
    sub_ref,
    off_ref,
    kind_ref,
    owner_ref,
    sems,
):
    pairs = [(sub_hbm, sub_ref), (off_hbm, off_ref), (kind_hbm, kind_ref), (owner_hbm, owner_ref)]
    copies = scalars(pairs, sems)
    chunks = length // LANES
    mine = lax.axis_index("facet")
    count = kind_ref.shape[0]
    rows = cos_ref.shape[0] // count
    span = screens_ref.shape[2] // 2
    my_sub = lax.axis_index("sub")
    shape = (span, LANES)
    lane = iota(shape, 1)
    apart = iota(shape, 0) - lane % M
    sign = jnp.where(lane < M, -1.0, 1.0)

    shape = (chunks, LANES)
    cos, sin = circle(iota(shape, 0) * iota(shape, 1), chunks)
    table = jnp.concatenate(
        [jnp.concatenate([cos, -sin], axis=1), jnp.concatenate([sin, cos], axis=1)], axis=0
    )
    inv_ref[: 2 * chunks, :] = high_low(table, False)
    inv_ref[2 * chunks :, :] = high_low(table, True)

    for copy in copies:
        copy.wait()
    hit = apart == off_ref[mine]
    both = jnp.where(hit, 1.0, 0.0).astype(BF)
    signed = jnp.where(hit, sign, 0.0).astype(BF)
    kinds = screens_ref.shape[0]
    tall = cos_scr.shape[0] // kinds
    first = my_sub * rows // tall * tall
    block = pl.ds(pl.multiple_of(first, tall), tall)
    cosines = screens_ref[:, block, :span].reshape(kinds * tall, span)
    sines = screens_ref[:, block, span:].reshape(kinds * tall, span)
    both_ref[...] = both
    other_ref[...] = jnp.where(apart == off_ref[mine ^ 1], 1.0, 0.0).astype(BF)
    for n in range(shown_ref.shape[1] // LANES):
        hit = apart == off_ref[mine ^ (2 * n + 2)]
        shown_ref[:, n * LANES : (n + 1) * LANES] = jnp.where(hit, 1.0, 0.0).astype(BF)
    cos_scr[...] = dot(cosines, both)
    sin_scr[...] = dot(sines, signed)
    for j in range(count):
        kind = pl.multiple_of(kind_ref[j] * tall + my_sub * rows - first, rows)
        cos_ref[pl.ds(j, rows, stride=count), :] = cos_scr[pl.ds(kind, rows), :]
        sin_ref[pl.ds(j, rows, stride=count), :] = sin_scr[pl.ds(kind, rows), :]

    owners = [owner_ref[j] for j in range(count)]
    lane = iota((8, LANES), 1)
    wide = []
    for first in range(0, count, LANES):
        value = jnp.full((8, LANES), -1, jnp.int32)
        for j in range(first, min(first + LANES, count)):
            value = jnp.where(lane == j - first, owners[j], value)
        wide.append(value)
    tall_owner = column(owners, LANES)
    slot = jnp.zeros((count, 1), F32)
    for n, value in enumerate(wide):
        same = jnp.concatenate([value] * (count // 8), axis=0) == tall_owner
        earlier = iota((count, LANES), 1) + n * LANES < iota((count, LANES), 0)
        slot = slot + jnp.sum(jnp.where(same & earlier, 1.0, 0.0), axis=1, keepdims=True)
    bits = subs.bit_length() - 1
    facet_step = (tall_owner >> bits) ^ mine
    sub_step = (tall_owner & (subs - 1)) ^ my_sub
    facets = off_ref.shape[0]
    block = jnp.where(facet_step < 2, facet_step, facet_step + 1)
    block = jnp.where(facet_step == facets - 2, 2, block)
    block = jnp.where(facet_step == facets - 1, facets - 1, block)
    order = jnp.zeros_like(sub_step)
    for n in range(bits):
        order = order * 2 + ((sub_step >> n) & 1)
    place = (block * subs + order) * CAP + slot.astype(jnp.int32)
    for at in range(0, rank_ref.shape[1], LANES):
        hit = iota((count, LANES), 1) + at == place
        rank_ref[:, at : at + LANES] = jnp.where(hit, 1.0, 0.0).astype(BF)

    starts = [start_of(mine, sub_ref, off_ref, j, length) for j in range(count)]
    gather_ref[...] = (iota((count, LANES), 1) - (column(starts, LANES) & (M - 1))) & (LANES - 1)

    lane = iota((8, 4 * count), 1)
    block = jnp.zeros((8, 4 * count), jnp.int32)
    for j in range(count):
        block = jnp.where(lane % count == j, starts[j] // M, block)
    block = jnp.concatenate([block] * (M // 8), axis=0)
    shape = (M, 4 * count)
    lane = iota(shape, 1)
    cos, sin = circle(block * iota(shape, 0), length // M)
    scale = 1 / math.sqrt(length)
    cos, sin = cos * scale, sin * scale
    lane_im = lane // count % 2 == 1
    low = lane >= 2 * count
    coarse_ref[:M, :] = high_low(jnp.where(lane_im, -sin, cos), low)
    coarse_ref[M:, :] = high_low(jnp.where(lane_im, cos, sin), low)


def first_kernel(own_ref, block_ref, laid_ref, passed_ref, hits_ref, other_ref, tail_ref, cut_ref, total_ref):
    windows = own_ref.shape[0]
    rows = block_ref[windows:, :]
    tail_ref[...] = cut([rows], other_ref[...])
    cut_ref[...] = cut([laid_ref[...], passed_ref[...], rows], hits_ref[...])
    total_ref[...] = own_ref[...] + block_ref[:windows, :].astype(F32)


def backward_kernel(total_ref, *refs):
    arrived, refs = refs[:-13][::-1], refs[-13:]
    cut_ref, late_ref, cos_ref, sin_ref = refs[:4]
    rank_ref, gather_ref, coarse_ref, inv_ref, turn_ref, out_hbm, out_scr, flat_scr, out_sems = refs[4:]
    rows = out_hbm.shape[1]
    length = out_hbm.shape[2] // 2
    chunks = length // LANES
    windows = total_ref.shape[0]
    count = windows // rows

    cuts = [cut_ref[...]] + [ref[windows:, :] for ref in arrived] + [late_ref[...]]
    weights = dot(rank_ref[...], jnp.concatenate(cuts, axis=0))

    place = gather_ref[...]
    inside = place < M
    blocks = []
    for r in range(rows):
        here = slice(r * count, (r + 1) * count)
        total = total_ref[here, :]
        for ref in arrived:
            total = total + ref[here, :].astype(F32)
        value = (total * cos_ref[here, :] + pltpu.roll(total, M, 1) * sin_ref[here, :]) * weights
        value = value.astype(BF).astype(F32)
        re = jnp.where(inside, jnp.take_along_axis(value, place, axis=1), 0.0)
        im = jnp.where(inside, jnp.take_along_axis(value, place ^ M, axis=1), 0.0)
        blocks.append(jnp.concatenate([re, im], axis=0).astype(BF))
    spread = jnp.concatenate(blocks, axis=1)
    inner = dot(coarse_ref[...], jnp.concatenate([spread, spread], axis=0))
    twisted = []
    for r in range(rows):
        re = inner[:M, r * LANES : (r + 1) * LANES]
        im = inner[M:, r * LANES : (r + 1) * LANES]
        for q in range(LANES // M):
            cos = turn_ref[q * M : (q + 1) * M, :]
            sin = turn_ref[LANES + q * M : LANES + (q + 1) * M, :]
            both = jnp.concatenate([re * cos - im * sin, re * sin + im * cos], axis=1)
            twisted.append(both.astype(BF))
    twisted = jnp.concatenate(twisted, axis=0)
    points = dot_t(inv_ref[...], twisted)
    points = points[: 2 * chunks] + points[2 * chunks :]
    for r in range(rows):
        out_scr[pl.ds(r, 2 * chunks, stride=rows), :] = points[:, r * LANES : (r + 1) * LANES]
    parts = out_sems.shape[0]
    width = 2 * length // parts
    copies = []
    for p in range(parts):
        for c in range(p * width // LANES, (p + 1) * width // LANES):
            flat_scr[:, c * LANES : (c + 1) * LANES] = out_scr[c * rows : (c + 1) * rows, :]
        part = pl.ds(p * width, width)
        copies.append(pltpu.make_async_copy(flat_scr.at[:, part], out_hbm.at[0, :, part], out_sems.at[p]))
        copies[-1].start()
    for copy in copies:
        copy.wait()


def local(strips, facet_offset, subgrid_offset, owner, screen_index, screens, grid_weight):
    facets = lax.axis_size("facet")
    subs = lax.axis_size("sub")
    rows = strips.shape[1]
    length = strips.shape[2] // 2
    chunks = length // LANES
    count = subgrid_offset.shape[0]
    span = grid_weight.shape[1]
    kinds = screens.shape[0]
    hbm = pl.BlockSpec(memory_space=pl.ANY)
    vmem = pl.BlockSpec(memory_space=pltpu.VMEM)
    limit = pltpu.CompilerParams(vmem_limit_bytes=32 * 1024 * 1024)
    shaped = jax.ShapeDtypeStruct

    subgrid_offset, facet_offset, owner, screen_index = [
        pltpu.with_memory_space_constraint(x, pltpu.HBM) for x in (subgrid_offset, facet_offset, owner, screen_index)
    ]

    def swap(x, step):
        return lax.ppermute(x, "facet", [(i, i ^ step) for i in range(facets)])

    def cost(flops):
        return pl.CostEstimate(flops=flops, bytes_accessed=1 << 20, transcendentals=0)

    turn, fwd = pl.pallas_call(
        functools.partial(table_kernel, length),
        out_shape=[shaped((2 * LANES, LANES), F32), shaped((2 * chunks, 4 * chunks), BF)],
        out_specs=[vmem] * 2,
        compiler_params=limit,
        cost_estimate=cost(10**11),
    )()
    held = grid_weight
    steps = [1 << n for n in reversed(range(subs.bit_length() - 1))]
    for step in steps:
        last, beside = held, lax.ppermute(held, "sub", [(k, k ^ step) for k in range(subs)])
        if step == steps[0]:
            windows, shift = pl.pallas_call(
                forward_kernel,
                out_shape=[shaped((count * rows, LANES), BF), shaped((2 * LANES, facets // 2 * LANES), BF)],
                in_specs=[hbm] * 2 + [vmem] * 3,
                out_specs=[vmem] * 2,
                scratch_shapes=[
                    pltpu.VMEM((rows * 2 * chunks, LANES), F32),
                    pltpu.VMEM((rows * LANES, 2 * LANES), BF),
                    pltpu.VMEM((rows * LANES, 2 * LANES), BF),
                    pltpu.SMEM((count,), jnp.int32),
                    pltpu.SMEM((facets,), jnp.int32),
                    pltpu.SemaphoreType.DMA((2,)),
                ],
                compiler_params=limit,
            )(subgrid_offset, facet_offset, strips, turn, fwd)
            passed = swap(windows, 1)
        if step != steps[-1]:
            beside = pl.pallas_call(
                join_kernel,
                out_shape=shaped((2 * held.shape[0], span), F32),
                in_specs=[vmem] * 2,
                out_specs=vmem,
                compiler_params=limit,
            )(held, beside)
        held, _ = lax.optimization_barrier((beside, windows))

    tall = max(rows, 16)
    cos, sin, both, other, shown, *ready = pl.pallas_call(
        functools.partial(prepare_kernel, subs, length),
        out_shape=[
            shaped((count * rows, LANES), F32),
            shaped((count * rows, LANES), F32),
            shaped((span, LANES), BF),
            shaped((span, LANES), BF),
            shaped((span, (facets // 2 - 2) * LANES), BF),
            shaped((count, facets * subs * CAP), BF),
            shaped((count, LANES), jnp.int32),
            shaped((2 * M, 4 * count), BF),
            shaped((4 * chunks, 2 * LANES), BF),
        ],
        in_specs=[hbm] * 5 + [vmem],
        out_specs=[vmem] * 9,
        scratch_shapes=[
            pltpu.VMEM((kinds * tall, LANES), F32),
            pltpu.VMEM((kinds * tall, LANES), F32),
            pltpu.SMEM((count,), jnp.int32),
            pltpu.SMEM((facets,), jnp.int32),
            pltpu.SMEM((count,), jnp.int32),
            pltpu.SMEM((count,), jnp.int32),
            pltpu.SemaphoreType.DMA((4,)),
        ],
        compiler_params=limit,
        cost_estimate=cost(2 * 10**10),
    )(subgrid_offset, facet_offset, screen_index, owner, last, screens)

    others = facets // 2 - 1
    shift, _ = lax.optimization_barrier((shift, both))
    own, *merged = pl.pallas_call(
        merge_kernel,
        out_shape=[shaped(windows.shape, F32)] + [shaped(windows.shape, BF)] * others,
        in_specs=[vmem] * 3,
        out_specs=[vmem] * (1 + others),
        compiler_params=limit,
    )(windows, passed, shift)
    size = subs * grid_weight.size // LANES
    laid, payload = pl.pallas_call(
        pack_kernel,
        out_shape=[shaped((size, LANES), BF), shaped((count * rows + size, LANES), BF)],
        in_specs=[vmem] * 3,
        out_specs=[vmem] * 2,
        compiler_params=limit,
    )(merged[-1], last, beside)

    far = swap(payload, facets - 2)
    laid_other = swap(laid, 1)
    parts = others - 1
    payloads = pl.pallas_call(
        functools.partial(attach_kernel, parts),
        out_shape=[shaped((count * rows + 2 * subs * CAP, LANES), BF)] * parts,
        in_specs=[vmem] * (parts + 3),
        out_specs=[vmem] * parts,
        compiler_params=limit,
    )(*merged[:-1], laid, laid_other, shown)
    arrived = [swap(block, 2 * n + 2) for n, block in enumerate(payloads)]
    tail, here, total = pl.pallas_call(
        first_kernel,
        out_shape=[
            shaped((subs * CAP, LANES), BF),
            shaped((3 * subs * CAP, LANES), BF),
            shaped(windows.shape, F32),
        ],
        in_specs=[vmem] * 6,
        out_specs=[vmem] * 3,
        compiler_params=limit,
    )(own, far, laid, laid_other, both, other)
    late = swap(tail, 1)

    return pl.pallas_call(
        backward_kernel,
        out_shape=shaped((1, rows, 2 * length), F32),
        in_specs=[vmem] * (parts + 10),
        out_specs=hbm,
        scratch_shapes=[
            pltpu.VMEM((2 * chunks * rows, LANES), F32),
            pltpu.VMEM((rows, 2 * length), F32),
            pltpu.SemaphoreType.DMA((4,)),
        ],
        compiler_params=limit,
    )(total, *arrived[::-1], here, late, cos, sin, *ready, turn)


def solution(mesh):
    in_specs = (P("facet", "sub", None), P(), P(), P(), P(), P(), P(("facet", "sub"), None))
    out_specs = P("facet", "sub", None)
    return jax.shard_map(local, mesh=mesh, in_specs=in_specs, out_specs=out_specs, check_vma=False)
```
